32 devices in a mesh: dp: 8 (over z, x), head: 4 (over y, core).
Axes of the slice: x: 2, y: 2, z: 4, core: 2. Of those that a mesh axis runs over, the one named last changes fastest.
Arguments:
- media_tokens: bfloat16 [128, 576, 1024], P(('dp', 'head')), may hold values from -6 to 6
- latents: bfloat16 [128, 64, 1024], P(('dp', 'head')), may hold values from -6 to 6
- cotangent: float32 [128, 64, 1024], P(('dp', 'head')), may hold values from -7.2 to 7.2
- counts: int32 [128], P('dp'), may hold values from 256 to 576, as said below
- attention_weights: float32 [4, 1024, 1024], P(None, 'dp', 'head')
- attention_first: float32 [4, 1024, 1024], P(None, 'dp', 'head'), may hold values from -2.2888184e-05 to 2.2888184e-05
- attention_second: float32 [4, 1024, 1024], P(None, 'dp', 'head'), may hold values from 1.9858518e-13 to 7.943407e-13
- expand_weight: float32 [1024, 4096], P('dp', 'head'), may hold values from -0.1875 to 0.1875
- expand_first: float32 [1024, 4096], P('dp', 'head'), may hold values from -2.2888184e-05 to 2.2888184e-05
- expand_second: float32 [1024, 4096], P('dp', 'head'), may hold values from 1.9858518e-13 to 7.943407e-13
- reduce_weight: float32 [4096, 1024], P('head', 'dp'), may hold values from -0.09375 to 0.09375
- reduce_first: float32 [4096, 1024], P('head', 'dp'), may hold values from -2.2888184e-05 to 2.2888184e-05
- reduce_second: float32 [4096, 1024], P('head', 'dp'), may hold values from 1.9858518e-13 to 7.943407e-13
- norm_params: float32 [6, 1024], replicated, may hold values from -1.2 to 2.52
- norm_first: float32 [6, 1024], replicated, may hold values from -9.1552734e-05 to 9.1552734e-05
- norm_second: float32 [6, 1024], replicated, may hold values from 3.1773629e-12 to 1.27094515e-11
Outputs:
- resampled: bfloat16 [128, 64, 1024], P(('dp', 'head'))
- media_grad: bfloat16 [128, 576, 1024], P(('dp', 'head'))
- latent_grad: bfloat16 [128, 64, 1024], P(('dp', 'head'))
- grad_norm: float32 [], replicated
- attention_new: float32 [4, 1024, 1024], P(None, 'dp', 'head')
- attention_first_new: float32 [4, 1024, 1024], P(None, 'dp', 'head')
- attention_second_new: float32 [4, 1024, 1024], P(None, 'dp', 'head')
- expand_new: float32 [1024, 4096], P('dp', 'head')
- expand_first_new: float32 [1024, 4096], P('dp', 'head')
- expand_second_new: float32 [1024, 4096], P('dp', 'head')
- reduce_new: float32 [4096, 1024], P('head', 'dp')
- reduce_first_new: float32 [4096, 1024], P('head', 'dp')
- reduce_second_new: float32 [4096, 1024], P('head', 'dp')
- norm_new: float32 [6, 1024], replicated
- norm_first_new: float32 [6, 1024], replicated
- norm_second_new: float32 [6, 1024], replicated
The draws below stay inside these ranges and needn't reach their ends.
Inputs may be any that keep to these rules, and one draw needn't show every extreme that they name: `counts`: each image has either 256 or 576 patch rows; rows of its slot past that count are padding.
All inputs are finite; a program needn't handle non-finite values.
Results may differ from the reference program's by a relative error of at most 0.015.
Values may be sent and summed in bfloat16 or wider, within the bound.
A program may use at most 192 MiB of HBM per device.

```python
import math
from functools import partial
import jax
import jax.numpy as jnp
from jax import lax

D = 1024
HEADS = 16
FF = 4096
LAT = 64
PATCH = 576
SHORT = 256
STEP = 10
IMAGES = 128


def ramp(lowest, highest, length):
    return lowest + (highest - lowest) * jnp.arange(length, dtype=jnp.float32) / (length - 1)


def draw_norm_params(key, part):
    key = jax.random.fold_in(key, 11)
    noise = jnp.clip(jax.random.normal(key, (6, D), jnp.float32), -4.0, 4.0)
    rising = ramp(0.6, 1.8, D)
    gains = rising[None, :] * (1.0 + 0.1 * noise)
    shifts = 0.3 * noise
    even_rows = (jnp.arange(6) % 2 == 0)[:, None]
    return jnp.where(even_rows, gains, shifts)


def draw_attention_weights(key, part):
    key = jax.random.fold_in(key, 12)
    noise = jnp.clip(jax.random.normal(key, (4, D, D), jnp.float32), -4.0, 4.0)
    scales = jnp.where(jnp.arange(4) == 3, 4.0, 1.0)[:, None, None] * D ** (-0.5)
    return noise * scales


def draw_cotangent(key, part):
    key = jax.random.fold_in(key, 13)
    noise = jnp.clip(jax.random.normal(key, (IMAGES, LAT, D), jnp.float32), -4.0, 4.0)
    rising = ramp(0.6, 1.8, D)
    return noise * rising[None, None, :]


def draw_counts(key, part):
    key = jax.random.fold_in(key, 14)
    key_pick, key_first, key_second = jax.random.split(key, 3)
    picks = jax.random.randint(key_pick, (IMAGES,), 0, 2)
    counts = jnp.where(picks == 1, PATCH, SHORT).astype(jnp.int32)
    first = jax.random.randint(key_first, (), 0, IMAGES)
    second = (first + 1 + jax.random.randint(key_second, (), 0, IMAGES - 1)) % IMAGES
    counts = counts.at[first].set(PATCH)
    counts = counts.at[second].set(SHORT)
    return counts


def block_scale(rng, shape, cuts, least, largest):
    gain, own = 1.0, jax.random.fold_in(rng, 6)
    for dim, parts in cuts:
        steps = jnp.exp(jax.random.uniform(jax.random.fold_in(own, dim), (parts,), jnp.float32, least / len(cuts), largest / len(cuts)))
        gain = gain * jnp.repeat(steps, shape[dim] // parts).reshape([-1 if axis == dim else 1 for axis in range(len(shape))])
    return gain


def scatter_about(own_key, dims, scale, most, shards=(), held_as=jnp.bfloat16):
    result = jax.random.normal(own_key, dims, jnp.float32) * scale
    if len(shards) > 0:
        result = block_scale(own_key, dims, shards, -0.22, 0.18) * result
    return jnp.clip(result, min=-most, max=most).astype(held_as)


def setup_inputs(seed: int = 0) -> dict:
    streams_of = jax.random.split(jax.random.key(seed), 17)
    media_tokens = scatter_about(streams_of[0], (IMAGES, PATCH, D), 1.0, 6.0, ((0, 32),))
    latents = scatter_about(streams_of[1], (IMAGES, LAT, D), 1.0, 6.0, ((0, 32),))
    cotangent = draw_cotangent(jax.random.fold_in(streams_of[16], 71), 0)
    counts = draw_counts(jax.random.fold_in(streams_of[16], 71), 0)
    attention_weights = draw_attention_weights(jax.random.fold_in(streams_of[16], 71), 0)
    attention_first = scatter_about(streams_of[5], (4, D, D), (0.0056 / (4 * D * D + 2 * D * FF + 6 * D) ** 0.5), 2.288818359375e-05, ((1, 8), (2, 4)), jnp.float32)
    attention_second = jnp.clip(jnp.exp(math.log(7.943407216715048e-13) - 1.3862944 * jax.random.uniform(streams_of[6], (4, D, D), jnp.float32) ** block_scale(streams_of[6], (4, D, D), ((1, 8), (2, 4)), -0.2, 0.2)), 1.985851804178762e-13, 7.943407216715048e-13)
    expand_weight = scatter_about(streams_of[7], (D, FF), D ** -0.5, 0.1875, ((0, 8), (1, 4)), jnp.float32)
    expand_first = scatter_about(streams_of[8], (D, FF), (0.0056 / (4 * D * D + 2 * D * FF + 6 * D) ** 0.5), 2.288818359375e-05, ((0, 8), (1, 4)), jnp.float32)
    expand_second = jnp.clip(jnp.exp(math.log(7.943407216715048e-13) - 1.3862944 * jax.random.uniform(streams_of[9], (D, FF), jnp.float32) ** block_scale(streams_of[9], (D, FF), ((0, 8), (1, 4)), -0.2, 0.2)), 1.985851804178762e-13, 7.943407216715048e-13)
    reduce_weight = scatter_about(streams_of[10], (FF, D), FF ** -0.5, 0.09375, ((0, 4), (1, 8)), jnp.float32)
    reduce_first = scatter_about(streams_of[11], (FF, D), (0.0056 / (4 * D * D + 2 * D * FF + 6 * D) ** 0.5), 2.288818359375e-05, ((0, 4), (1, 8)), jnp.float32)
    reduce_second = jnp.clip(jnp.exp(math.log(7.943407216715048e-13) - 1.3862944 * jax.random.uniform(streams_of[12], (FF, D), jnp.float32) ** block_scale(streams_of[12], (FF, D), ((0, 4), (1, 8)), -0.2, 0.2)), 1.985851804178762e-13, 7.943407216715048e-13)
    norm_params = draw_norm_params(jax.random.fold_in(streams_of[16], 71), 0)
    norm_first = scatter_about(streams_of[14], (6, D), (0.0224 / (4 * D * D + 2 * D * FF + 6 * D) ** 0.5), 9.1552734375e-05, (), jnp.float32)
    norm_second = jnp.clip(jnp.exp(jax.random.uniform(streams_of[15], (6, D), jnp.float32, math.log(3.1773628866860193e-12), math.log(1.2709451546744077e-11))), 3.1773628866860193e-12, 1.2709451546744077e-11)
    return dict(media_tokens=media_tokens, latents=latents, cotangent=cotangent, counts=counts, attention_weights=attention_weights, attention_first=attention_first, attention_second=attention_second, expand_weight=expand_weight, expand_first=expand_first, expand_second=expand_second, reduce_weight=reduce_weight, reduce_first=reduce_first, reduce_second=reduce_second, norm_params=norm_params, norm_first=norm_first, norm_second=norm_second)


LN_EPS = 1e-05
BETA_ONE = 0.9
BETA_TWO = 0.999
ADAM_EPS = 1e-08
MATRIX_RATE = 0.1
NORM_RATE = 0.6
DECAY_RATE = 0.1
MAX_NORM = 0.05
block_images = 4

@jax.custom_vjp
def low(v):
    return lax.optimization_barrier(v.astype(jnp.bfloat16)).astype(jnp.float32)

@jax.custom_vjp
def low_back(v):
    return v

def low_keep(v):
    return (low(v), None)

def low_pass(kept, grad):
    return (grad,)

def back_keep(v):
    return (v, None)

def back_low(kept, grad):
    return (low(grad),)
low.defvjp(low_keep, low_pass)
low_back.defvjp(back_keep, back_low)

def matmul(left, right):
    return jnp.einsum('...d,de->...e', left, right, precision=lax.Precision.HIGHEST)

def layer_norm(values, gain_row, shift_row):
    center = values - lax.optimization_barrier(jnp.mean(values, axis=-1, keepdims=True))
    scaled = lax.rsqrt(lax.optimization_barrier(jnp.mean(center * center, axis=-1, keepdims=True)) + LN_EPS)
    return center * scaled * gain_row + shift_row

def one_block(weights, norm_params, block):
    media_rows, latent_rows, lengths = block
    query_weight, key_weight, value_weight, output_weight, expand_low, reduce_low = weights
    count = media_rows.shape[0]
    head_size = D // HEADS
    key_span = PATCH + LAT
    media_low = low(layer_norm(media_rows, norm_params[0], norm_params[1]))
    latent_low = low(layer_norm(latent_rows, norm_params[2], norm_params[3]))
    pair_input = jnp.concatenate([media_low, latent_low], axis=1)
    keys = low_back(low(matmul(pair_input, key_weight)))
    values = low_back(low(matmul(pair_input, value_weight)))
    queries = low_back(low(matmul(latent_low, query_weight)))
    query_heads = queries.reshape(count, LAT, HEADS, head_size)
    key_heads = keys.reshape(count, key_span, HEADS, head_size)
    value_heads = values.reshape(count, key_span, HEADS, head_size)
    raw_scores = jnp.einsum('bqhc,bkhc->bhqk', query_heads, key_heads, precision=lax.Precision.HIGHEST) * head_size ** (-0.5)
    raw_scores = low_back(raw_scores)
    positions = jnp.arange(key_span, dtype=jnp.int32)
    visible = (positions[None, :] < lengths[:, None]) | (positions[None, :] >= PATCH)
    scores = jnp.where(visible[:, None, None, :], raw_scores, -1e+30)
    softened = low(jax.nn.softmax(scores, axis=-1))
    mixed = jnp.einsum('bhqk,bkhc->bqhc', softened, value_heads, precision=lax.Precision.HIGHEST).reshape(count, LAT, D)
    mixed = low_back(low(mixed))
    middle = latent_rows + low_back(matmul(mixed, output_weight))
    ff_low = low(layer_norm(middle, norm_params[4], norm_params[5]))
    before = low_back(matmul(ff_low, expand_low))
    hidden = low(jax.nn.gelu(before))
    return middle + low_back(matmul(hidden, reduce_low))

def forward(counts, media_tokens, latents, attention_weights, expand_weight, reduce_weight, norm_params):
    weights = (low(attention_weights[0]), low(attention_weights[1]), low(attention_weights[2]), low(attention_weights[3]), low(expand_weight), low(reduce_weight))
    blocks = (media_tokens.reshape(-1, block_images, PATCH, D), latents.reshape(-1, block_images, LAT, D), counts.reshape(-1, block_images))
    results = lax.map(jax.checkpoint(partial(one_block, weights, norm_params)), blocks)
    return results.reshape(IMAGES, LAT, D)

def adam_step(master, first, second, gradient, step_rate, decay_rate):
    first_new = BETA_ONE * first + (1.0 - BETA_ONE) * gradient
    second_new = BETA_TWO * second + (1.0 - BETA_TWO) * gradient * gradient
    first_hat = first_new / (1.0 - BETA_ONE ** STEP)
    second_hat = second_new / (1.0 - BETA_TWO ** STEP)
    master_new = master - step_rate * (first_hat / (jnp.sqrt(second_hat) + ADAM_EPS) + decay_rate * master)
    return (master_new, first_new, second_new)

def reference(media_tokens, latents, cotangent, counts, attention_weights, attention_first, attention_second, expand_weight, expand_first, expand_second, reduce_weight, reduce_first, reduce_second, norm_params, norm_first, norm_second):
    primals = (media_tokens.astype(jnp.float32), latents.astype(jnp.float32), attention_weights, expand_weight, reduce_weight, norm_params)
    resampled, pullback = jax.vjp(partial(forward, counts), *primals)
    media_grad, latent_grad, attention_grad, expand_grad, reduce_grad, norm_grad = pullback(cotangent)
    squares = jnp.sum(attention_grad * attention_grad) + jnp.sum(expand_grad * expand_grad) + jnp.sum(reduce_grad * reduce_grad) + jnp.sum(norm_grad * norm_grad)
    grad_norm = jnp.sqrt(squares)
    clip_factor = jnp.minimum(1.0, MAX_NORM / (grad_norm + 1e-06))
    attention_new, attention_first_new, attention_second_new = adam_step(attention_weights, attention_first, attention_second, attention_grad * clip_factor, MATRIX_RATE, DECAY_RATE)
    expand_new, expand_first_new, expand_second_new = adam_step(expand_weight, expand_first, expand_second, expand_grad * clip_factor, MATRIX_RATE, DECAY_RATE)
    reduce_new, reduce_first_new, reduce_second_new = adam_step(reduce_weight, reduce_first, reduce_second, reduce_grad * clip_factor, MATRIX_RATE, DECAY_RATE)
    norm_new, norm_first_new, norm_second_new = adam_step(norm_params, norm_first, norm_second, norm_grad * clip_factor, NORM_RATE, 0.0)
    return (resampled.astype(jnp.bfloat16), media_grad.astype(jnp.bfloat16), latent_grad.astype(jnp.bfloat16), grad_norm, attention_new, attention_first_new, attention_second_new, expand_new, expand_first_new, expand_second_new, reduce_new, reduce_first_new, reduce_second_new, norm_new, norm_first_new, norm_second_new)
```

```python
import functools

import jax
import jax.numpy as jnp
from jax import lax
from jax.experimental import pallas as pl
from jax.experimental.pallas import tpu as pltpu
from jax.sharding import PartitionSpec as P

D = 1024
HEADS = 16
HEAD = D // HEADS
GROUP = 256
GROUPS = D // GROUP
STEP = 10

LN_EPS = 1e-05
BETA_ONE = 0.9
BETA_TWO = 0.999
ADAM_EPS = 1e-08
MATRIX_RATE = 0.1
NORM_RATE = 0.6
DECAY_RATE = 0.1
MAX_NORM = 0.05

MESH = pl.DeviceIdType.MESH
F32 = jnp.float32
BF16 = jnp.bfloat16
MIB = 2**20


def grid_of(dp_count, head_count):
    x = 1
    while 4 * x * x <= dp_count:
        x *= 2
    return {"z": dp_count // x, "x": x, "y": head_count // 2, "c": 2}


class Links:
    def __init__(self, sizes, send, recv, local):
        self.sizes, self.send, self.recv, self.local = sizes, send, recv, local
        self.used = self.used_local = 0
        dp, head = lax.axis_index("dp"), lax.axis_index("head")
        self.at = {
            "z": lax.div(dp, sizes["x"]),
            "x": lax.rem(dp, sizes["x"]),
            "y": lax.div(head, sizes["c"]),
            "c": lax.rem(head, sizes["c"]),
        }
        self.head = head

    def place(self, axis, k):
        return lax.rem(self.at[axis] + k, self.sizes[axis])

    def peer(self, axis, k):
        at = dict(self.at)
        at[axis] = self.place(axis, k)
        return {
            "dp": at["z"] * self.sizes["x"] + at["x"],
            "head": at["y"] * self.sizes["c"] + at["c"],
        }

    def greet(self):
        barrier = pltpu.get_barrier_semaphore()
        for axis, n in self.sizes.items():
            for k in range(1, n):
                pl.semaphore_signal(
                    barrier, inc=1, device_id=self.peer(axis, k), device_id_type=MESH
                )

    def meet(self):
        barrier = pltpu.get_barrier_semaphore()
        pl.semaphore_wait(barrier, sum(n - 1 for n in self.sizes.values()))

    def copy(self, src, dst, slot, axis, k):
        return pltpu.make_async_remote_copy(
            src_ref=src,
            dst_ref=dst,
            send_sem=self.send.at[slot],
            recv_sem=self.recv.at[slot],
            device_id=self.peer(axis, k),
            device_id_type=MESH,
        )

    def take(self):
        self.used += 1
        return self.used - 1

    def move(self, src, dst):
        self.used_local += 1
        made = pltpu.make_async_copy(src, dst, self.local.at[self.used_local - 1])
        made.start()
        return made


class Gather:
    def __init__(self, links, order, view):
        self.links, self.order, self.view = links, order, view
        self.sent, self.coming = [], {}

    def region(self, step, place):
        at = dict(self.links.at)
        for axis in self.order[:step]:
            at[axis] = None
        at[self.order[step]] = place
        return self.view(at)

    def start(self, step):
        axis, links = self.order[step], self.links
        mine = self.region(step, links.at[axis])
        self.coming[step] = []
        for k in range(1, links.sizes[axis]):
            slot = links.take()
            copy = links.copy(mine, mine, slot, axis, k)
            copy.start()
            self.sent.append(copy)
            lands = self.region(step, links.place(axis, links.sizes[axis] - k))
            self.coming[step].append(links.copy(lands, lands, slot, axis, k))

    def wait(self, step):
        for copy in self.coming[step]:
            copy.wait_recv()

    def go(self, step):
        self.wait(step)
        if step + 1 < len(self.order):
            self.start(step + 1)

    def close(self):
        for copy in self.sent:
            copy.wait_send()


def some(place):
    return slice(None) if place is None else place


def dot(a, b):
    return lax.dot_general(a, b, (((1,), (0,)), ((), ())), preferred_element_type=F32)


def dot_nt(a, b):
    return lax.dot_general(a, b, (((1,), (1,)), ((), ())), preferred_element_type=F32)


def dot_tn(a, b):
    return lax.dot_general(a, b, (((0,), (0,)), ((), ())), preferred_element_type=F32)


def normed(values):
    center = values - jnp.mean(values, axis=-1, keepdims=True)
    scale = lax.rsqrt(jnp.mean(center * center, axis=-1, keepdims=True) + LN_EPS)
    return center * scale, scale


def diagonal(rows):
    n = GROUP // HEAD
    lat = rows.shape[0]
    tall = jnp.concatenate([rows] * n, axis=0)
    row = lax.broadcasted_iota(jnp.int32, tall.shape, 0) // lat
    col = lax.broadcasted_iota(jnp.int32, tall.shape, 1) // HEAD
    return jnp.where(row == col, tall, jnp.zeros_like(tall))


def undiagonal(tall):
    n = GROUP // HEAD
    lat = tall.shape[0] // n
    col = lax.broadcasted_iota(jnp.int32, (lat, GROUP), 1) // HEAD
    total = jnp.where(col == 0, tall[:lat], 0.0)
    for h in range(1, n):
        total = total + jnp.where(col == h, tall[h * lat : (h + 1) * lat], 0.0)
    return total


def weight_block(weights, m, g, sizes):
    block = weights.shape[-1]
    per = GROUP // block
    parts = []
    for s in range(per):
        h = g * per + s
        part = weights[m, lax.div(h, sizes["c"]), lax.rem(h, sizes["c"])]
        parts.append(part.reshape(D, block))
    return parts[0] if per == 1 else jnp.concatenate(parts, axis=1)


def softmax_columns(keys, spread_queries, seen):
    scores = dot_nt(keys, spread_queries)
    scores = jnp.where(seen, scores, -1e30)
    raised = jnp.exp(scores - jnp.max(scores, axis=0, keepdims=True))
    return raised * (1.0 / jnp.sum(raised, axis=0, keepdims=True))


def forward_kernel(
    sizes,
    att_ref,
    expand_ref,
    reduce_ref,
    tokens_ref,
    latents_ref,
    cotangent_ref,
    counts_ref,
    norm_ref,
    att_out,
    ff_out,
    pairs_out,
    turned_out,
    queries_out,
    mixed_out,
    middle_out,
    rows_out,
    back_out,
    att,
    ff,
    tokens,
    inputs,
    turned,
    pairs,
    queries,
    mixed,
    middle,
    rows,
    back,
    send,
    recv,
    local,
):
    links = Links(sizes, send, recv, local)
    links.greet()
    images, patches, _ = tokens.shape
    span = inputs.shape[1]
    lat = span - patches
    at = links.at
    outs = []

    loads = [links.move(tokens_ref.at[i], tokens.at[i]) for i in range(images)]
    for m in range(4):
        att[m, at["y"], at["c"], at["z"], at["x"]] = att_ref[m].astype(BF16)
    back[at["y"], at["c"]] = cotangent_ref[...].astype(BF16)
    ff[0, at["z"], at["x"]] = expand_ref[...].astype(BF16)
    ff[1, at["z"], at["x"]] = reduce_ref[...].astype(BF16)

    half = att.shape[5] // 2

    def att_view(m, s):
        def view(p):
            return att.at[m, some(p["y"]), some(p["c"]), some(p["z"]), some(p["x"]), pl.ds(s * half, half)]

        return view

    def ff_view(m, s):
        def view(p):
            return ff.at[m, some(p["z"]), some(p["x"]), pl.ds(s * half, half)]

        return view

    def back_view(p):
        return back.at[some(p["y"]), some(p["c"])]

    def row_view(i):
        def view(p):
            return rows.at[some(p["y"]), some(p["c"]), pl.ds(i * lat, lat)]

        return view

    query = [Gather(links, "zxyc", att_view(0, 0)), Gather(links, "yzxc", att_view(0, 1))]
    key = [Gather(links, "zxyc", att_view(1, 0)), Gather(links, "yzxc", att_view(1, 1))]
    value = [Gather(links, "zyxc", att_view(2, 0)), Gather(links, "xzyc", att_view(2, 1))]
    output = [Gather(links, "zyxc", att_view(3, 0)), Gather(links, "xzyc", att_view(3, 1))]
    hidden = [
        Gather(links, "zx", ff_view(0, 0)),
        Gather(links, "xz", ff_view(0, 1)),
        Gather(links, "zx", ff_view(1, 0)),
        Gather(links, "xz", ff_view(1, 1)),
    ]
    cotangent = [Gather(links, "yc", back_view)]
    ff_rows = [Gather(links, "yc", row_view(i)) for i in range(images)]
    everything = [*query, *key, *value, *output, *hidden, *cotangent, *ff_rows]

    def start(parts):
        for part in parts:
            part.start(0)

    def go(parts, step):
        for part in parts:
            part.go(step)

    links.meet()
    start(key + value)

    for i in range(images):
        low = normed(latents_ref[pl.ds(i * lat, lat)].astype(F32))[0] * norm_ref[2:3] + norm_ref[3:4]
        inputs[i, pl.ds(patches, lat)] = low.astype(BF16)

    def normalize(i):
        loads[i].wait()
        tile = 64

        def one(t, _):
            part = pl.ds(pl.multiple_of(t * tile, tile), tile)
            low = normed(tokens[i, part].astype(F32))[0] * norm_ref[0:1] + norm_ref[1:2]
            inputs[i, part] = low.astype(BF16)
            return 0

        lax.fori_loop(0, patches // tile, one, 0)

        def turn(t, _):
            part = pl.ds(pl.multiple_of(t * 128, 128), 128)
            turned[i, :, part] = inputs[i, part].T
            return 0

        lax.fori_loop(0, span // 128, turn, 0)
        outs.append(links.move(turned.at[i], turned_out.at[i]))

    normalize(0)
    go(key + value, 0)
    start(query + output)
    if images > 1:
        normalize(1)
    go(key + value, 1)
    go(query + output, 0)
    if images > 2:
        normalize(2)
    go(key + value, 2)
    go(query + output, 1)
    start(cotangent + hidden)
    for i in range(3, images):
        normalize(i)
    go(query + output, 2)
    go(key + value, 3)

    def project(i):
        def one(j, _):
            m = 1 + lax.div(j, GROUPS)
            weight = weight_block(att, m, lax.rem(j, GROUPS), sizes)
            pairs[i, j] = dot(inputs[i], weight).astype(BF16)
            return 0

        lax.fori_loop(0, 2 * GROUPS, one, 0)
        outs.append(links.move(pairs.at[i], pairs_out.at[i]))

    def attend(i):
        position = lax.broadcasted_iota(jnp.int32, (span, GROUP), 0)
        count = counts_ref[links.head * images + i]
        seen = (position < count) | (position >= patches)

        def one(g, _):
            spread = diagonal(queries[g, pl.ds(i * lat, lat)])
            probs = softmax_columns(pairs[i, g], spread, seen).astype(BF16)
            wide = dot_tn(probs, pairs[i, GROUPS + g])
            mixed[g, pl.ds(i * lat, lat)] = undiagonal(wide).astype(BF16)
            return 0

        lax.fori_loop(0, GROUPS, one, 0)

    def finish(i):
        part = pl.ds(i * lat, lat)
        whole = jnp.concatenate([mixed[g, part] for g in range(GROUPS)], axis=1)
        made = jnp.concatenate(
            [dot(whole, weight_block(att, 3, g, sizes)) for g in range(GROUPS)], axis=1
        )
        value = latents_ref[part].astype(F32) + made
        middle[part] = value
        low = normed(value)[0] * norm_ref[4:5] + norm_ref[5:6]
        rows[at["y"], at["c"], part] = low.astype(BF16)
        ff_rows[i].start(0)

    for i in range(images):
        project(i)
        if i == 0:
            go(query + output, 3)
            stack = inputs[:, patches:].reshape(images * lat, D)
            for g in range(GROUPS):
                made = dot(stack, weight_block(att, 0, g, sizes)) * HEAD ** (-0.5)
                queries[g] = made.astype(BF16)
            outs.append(links.move(queries, queries_out))
        if i == 1:
            go(cotangent + hidden, 0)
        attend(i)
        finish(i)
        if i >= 1:
            ff_rows[i - 1].go(0)
    if images == 1:
        go(cotangent + hidden, 0)
    outs.append(links.move(att, att_out))
    outs.append(links.move(mixed, mixed_out))
    outs.append(links.move(middle, middle_out))
    go(cotangent + hidden, 1)
    outs.append(links.move(back, back_out))
    outs.append(links.move(ff, ff_out))
    ff_rows[images - 1].go(0)
    for part in ff_rows:
        part.go(1)
    outs.append(links.move(rows, rows_out))
    for part in everything:
        part.close()
    for out in outs:
        out.wait()


def forward(att, expand, reduce_turned, tokens, latents, cotangent, counts, norm_params):
    sizes = grid_of(lax.axis_size("dp"), lax.axis_size("head"))
    z, x, y, c = (sizes[a] for a in "zxyc")
    images, patches, _ = tokens.shape
    lat = latents.shape[1]
    span = patches + lat
    n = images * lat
    _, row_block, col_block = att.shape
    ff_block = expand.shape[1]
    shapes = dict(
        att=((4, y, c, z, x, row_block, col_block), BF16),
        ff=((2, z, x, row_block, ff_block), BF16),
        pairs=((images, 2 * GROUPS, span, GROUP), BF16),
        turned=((images, D, span), BF16),
        queries=((GROUPS, n, GROUP), BF16),
        mixed=((GROUPS, n, GROUP), BF16),
        middle=((n, D), F32),
        rows=((y, c, n, D), BF16),
        back=((y, c, n, D), BF16),
        tokens=((images, patches, D), BF16),
        inputs=((images, span, D), BF16),
    )
    out_names = ("att", "ff", "pairs", "turned", "queries", "mixed", "middle", "rows", "back")
    scratch_names = (
        "att", "ff", "tokens", "inputs", "turned", "pairs", "queries", "mixed", "middle", "rows", "back",
    )
    per_att = sum(s - 1 for s in sizes.values())
    slots = 8 * per_att + 4 * (z + x - 2) + (1 + images) * (y + c - 2)
    vmem, anywhere = pl.BlockSpec(memory_space=pltpu.VMEM), pl.BlockSpec(memory_space=pl.ANY)
    made = pl.pallas_call(
        functools.partial(forward_kernel, sizes),
        out_shape=[jax.ShapeDtypeStruct(*shapes[k]) for k in out_names],
        in_specs=[vmem, vmem, vmem, anywhere, vmem, vmem, pl.BlockSpec(memory_space=pltpu.SMEM), vmem],
        out_specs=[anywhere] * len(out_names),
        scratch_shapes=[pltpu.VMEM(*shapes[k]) for k in scratch_names]
        + [
            pltpu.SemaphoreType.DMA((slots,)),
            pltpu.SemaphoreType.DMA((slots,)),
            pltpu.SemaphoreType.DMA((3 * images + 8,)),
        ],
        compiler_params=pltpu.CompilerParams(
            collective_id=0, has_side_effects=True, vmem_limit_bytes=58 * MIB
        ),
        name="gather_and_attend",
    )(att, expand, reduce_turned, tokens, latents.reshape(n, D), cotangent.reshape(n, D), counts, norm_params)
    return dict(zip(out_names, made))


def layer_norm(values):
    normed_values, scale = normed(values)
    return normed_values, scale


def norm_back(upstream, hat, scaled, gain_row):
    inner = upstream * gain_row
    result = scaled * (
        inner
        - jnp.mean(inner, axis=-1, keepdims=True)
        - hat * jnp.mean(inner * hat, axis=-1, keepdims=True)
    )
    lead_axes = tuple(range(upstream.ndim - 1))
    return (result, jnp.sum(upstream * hat, axis=lead_axes), jnp.sum(upstream, axis=lead_axes))


def adam_step(master, first, second, gradient, step_rate, decay_rate):
    first_new = BETA_ONE * first + (1.0 - BETA_ONE) * gradient
    second_new = BETA_TWO * second + (1.0 - BETA_TWO) * gradient * gradient
    first_hat = first_new / (1.0 - BETA_ONE**STEP)
    second_hat = second_new / (1.0 - BETA_TWO**STEP)
    master_new = master - step_rate * (
        first_hat / (jnp.sqrt(second_hat) + ADAM_EPS) + decay_rate * master
    )
    return (master_new, first_new, second_new)


def on_device(
    media_tokens, latents, cotangent, counts,
    attention_weights, attention_first, attention_second,
    expand_weight, expand_first, expand_second,
    reduce_weight, reduce_first, reduce_second,
    norm_params, norm_first, norm_second,
):
    dp_count = lax.axis_size("dp")
    head_count = lax.axis_size("head")
    images, patches, width = media_tokens.shape
    lat_rows = latents.shape[1]
    key_span = patches + lat_rows
    n = images * lat_rows
    row_block = attention_weights.shape[1]
    col_block = attention_weights.shape[2]
    got = forward(
        attention_weights, expand_weight, reduce_weight.T, media_tokens, latents, cotangent, counts, norm_params
    )
    full_weights = got["att"].reshape(4, head_count, width, col_block).transpose(0, 2, 1, 3).reshape(4, width, width)
    query_weight, key_weight, value_weight, output_weight = full_weights
    expand_full = got["ff"][0].reshape(width, -1)
    reduce_part = got["ff"][1].reshape(width, -1).T
    rows_all = got["rows"].reshape(-1, width)
    back_all = got["back"].reshape(-1, width)
    middle = got["middle"]
    ff_hat, ff_scale = layer_norm(middle)
    before = jnp.dot(rows_all, expand_full, preferred_element_type=jnp.float32)
    hidden, gelu_back = jax.vjp(jax.nn.gelu, before)
    hidden_low = hidden.astype(jnp.bfloat16)
    added = lax.psum_scatter(
        jnp.dot(hidden_low, reduce_part, preferred_element_type=jnp.float32).astype(jnp.bfloat16),
        "head", scatter_dimension=0, tiled=True,
    ).astype(jnp.float32)
    resampled = (middle + added).reshape(images, lat_rows, width).astype(jnp.bfloat16)
    reduce_grad = jnp.einsum("nf,nd->df", hidden_low, back_all, preferred_element_type=jnp.float32)
    hidden_grad = jnp.einsum("nd,fd->nf", back_all, reduce_part, preferred_element_type=jnp.float32)
    before_grad = gelu_back(hidden_grad)[0].astype(jnp.bfloat16)
    expand_grad = jnp.einsum("nd,nf->df", rows_all, before_grad, preferred_element_type=jnp.float32)
    ff_back = lax.psum_scatter(
        jnp.einsum("nf,df->nd", before_grad, expand_full, preferred_element_type=jnp.float32).astype(jnp.bfloat16),
        "head", scatter_dimension=0, tiled=True,
    ).astype(jnp.float32)
    middle_part, ff_gain_grad, ff_shift_grad = norm_back(ff_back, ff_hat, ff_scale, norm_params[4])
    middle_grad = cotangent.reshape(n, width) + middle_part
    expand_share = lax.psum_scatter(
        expand_grad.astype(jnp.bfloat16), "dp", scatter_dimension=0, tiled=True
    ).astype(jnp.float32)
    reduce_share = lax.psum_scatter(
        reduce_grad.astype(jnp.bfloat16), "dp", scatter_dimension=0, tiled=True
    ).astype(jnp.float32).T
    hidden_squares = jnp.sum(expand_share * expand_share) + jnp.sum(reduce_share * reduce_share)
    branch_low = middle_grad.astype(jnp.bfloat16)
    mixed = got["mixed"].transpose(1, 0, 2).reshape(n, width)
    output_grad = jnp.einsum("nc,nd->cd", mixed, branch_low, preferred_element_type=jnp.float32)
    mixed_grad = jnp.einsum("nd,cd->nc", branch_low, output_weight, preferred_element_type=jnp.float32).astype(jnp.bfloat16)
    pairs = got["pairs"].transpose(0, 2, 1, 3).reshape(images, key_span, 2, HEADS, HEAD)
    keys, values = pairs[:, :, 0], pairs[:, :, 1]
    queries = got["queries"].transpose(1, 0, 2).reshape(images, lat_rows, HEADS, HEAD)
    lengths = lax.dynamic_slice(counts, (lax.axis_index("head") * images,), (images,))
    positions = jnp.arange(key_span, dtype=jnp.int32)
    visible = (positions[None, :] < lengths[:, None]) | (positions[None, :] >= patches)
    scores = jnp.einsum("eqhc,ekhc->ehqk", queries, keys, preferred_element_type=jnp.float32)
    exact = jax.nn.softmax(jnp.where(visible[:, None, None, :], scores, -1e30), axis=-1)
    softened = exact.astype(jnp.bfloat16)
    mixed_heads = mixed_grad.reshape(images, lat_rows, HEADS, HEAD)
    prob_grad = jnp.einsum("eqhc,ekhc->ehqk", mixed_heads, values, preferred_element_type=jnp.float32)
    score_grad = (exact * (prob_grad - jnp.sum(exact * prob_grad, axis=-1, keepdims=True))).astype(jnp.bfloat16)
    query_rows = (jnp.einsum("ehqk,ekhc->eqhc", score_grad, keys, preferred_element_type=jnp.float32) * HEAD**-0.5).astype(jnp.bfloat16).reshape(n, width)
    key_back = jnp.einsum("ehqk,eqhc->ekhc", score_grad, queries, preferred_element_type=jnp.float32).astype(jnp.bfloat16).reshape(images * key_span, width)
    value_back = jnp.einsum("ehqk,eqhc->ekhc", softened, mixed_heads, preferred_element_type=jnp.float32).astype(jnp.bfloat16).reshape(images * key_span, width)
    inputs_turned = got["turned"].transpose(1, 0, 2).reshape(width, -1)
    key_grad = jnp.dot(inputs_turned, key_back, preferred_element_type=jnp.float32)
    value_grad = jnp.dot(inputs_turned, value_back, preferred_element_type=jnp.float32)
    latent_hat, latent_scale = layer_norm(latents.astype(jnp.float32))
    latent_low = got["turned"][:, :, patches:].transpose(0, 2, 1).reshape(n, width)
    query_grad = jnp.einsum("nd,ne->de", latent_low, query_rows, preferred_element_type=jnp.float32)
    pair_input_grad = (
        jnp.einsum("ne,de->nd", key_back, key_weight, preferred_element_type=jnp.float32)
        + jnp.einsum("ne,de->nd", value_back, value_weight, preferred_element_type=jnp.float32)
    ).reshape(images, key_span, width)
    latent_side = pair_input_grad[:, patches:] + jnp.einsum(
        "ne,de->nd", query_rows, query_weight, preferred_element_type=jnp.float32
    ).reshape(images, lat_rows, width)
    media_hat, media_scale = layer_norm(media_tokens.astype(jnp.float32))
    media_back, media_gain_grad, media_shift_grad = norm_back(pair_input_grad[:, :patches], media_hat, media_scale, norm_params[0])
    latent_back, latent_gain_grad, latent_shift_grad = norm_back(latent_side, latent_hat, latent_scale, norm_params[2])
    media_grad = media_back.astype(jnp.bfloat16)
    latent_grad = (middle_grad.reshape(images, lat_rows, width) + latent_back).astype(jnp.bfloat16)
    attention_local = jnp.stack([query_grad, key_grad, value_grad, output_grad])
    norm_local = jnp.stack([media_gain_grad, media_shift_grad, latent_gain_grad, latent_shift_grad, ff_gain_grad, ff_shift_grad])
    arranged = attention_local.astype(jnp.bfloat16).reshape(4, dp_count, row_block, head_count, col_block).transpose(1, 3, 0, 2, 4)
    arranged = arranged.reshape(dp_count * head_count, 4, row_block, col_block)
    attention_share = lax.psum_scatter(arranged, ("dp", "head"), scatter_dimension=0, tiled=True)[0].astype(jnp.float32)
    squares_here = hidden_squares + jnp.sum(attention_share * attention_share)
    norm_total, squares_total = lax.psum((norm_local, squares_here), ("dp", "head"))
    grad_norm = jnp.sqrt(squares_total + jnp.sum(norm_total * norm_total))
    clip_factor = jnp.minimum(1.0, MAX_NORM / (grad_norm + 1e-06))
    attention = adam_step(attention_weights, attention_first, attention_second, attention_share * clip_factor, MATRIX_RATE, DECAY_RATE)
    expand = adam_step(expand_weight, expand_first, expand_second, expand_share * clip_factor, MATRIX_RATE, DECAY_RATE)
    reduce = adam_step(reduce_weight, reduce_first, reduce_second, reduce_share * clip_factor, MATRIX_RATE, DECAY_RATE)
    norm = adam_step(norm_params, norm_first, norm_second, norm_total * clip_factor, NORM_RATE, 0.0)
    return (resampled, media_grad, latent_grad, grad_norm, *attention, *expand, *reduce, *norm)


def solution(mesh):
    in_specs = (
        P(("dp", "head"), None, None),
        P(("dp", "head"), None, None),
        P(("dp", "head"), None, None),
        P("dp"),
        P(None, "dp", "head"),
        P(None, "dp", "head"),
        P(None, "dp", "head"),
        P("dp", "head"),
        P("dp", "head"),
        P("dp", "head"),
        P("head", "dp"),
        P("head", "dp"),
        P("head", "dp"),
        P(),
        P(),
        P(),
    )
    out_specs = (
        P(("dp", "head"), None, None),
        P(("dp", "head"), None, None),
        P(("dp", "head"), None, None),
        P(),
        P(None, "dp", "head"),
        P(None, "dp", "head"),
        P(None, "dp", "head"),
        P("dp", "head"),
        P("dp", "head"),
        P("dp", "head"),
        P("head", "dp"),
        P("head", "dp"),
        P("head", "dp"),
        P(),
        P(),
        P(),
    )
    return jax.shard_map(
        on_device, mesh=mesh, in_specs=in_specs, out_specs=out_specs, check_vma=False
    )
```

```python
import functools
from types import SimpleNamespace

import jax
import jax.numpy as jnp
from jax import lax
from jax.experimental import pallas as pl
from jax.experimental.pallas import tpu as pltpu
from jax.sharding import PartitionSpec as P

D = 1024
HEADS = 16
HEAD = D // HEADS
GROUP = 256
GROUPS = D // GROUP
STEP = 10

LN_EPS = 1e-05
BETA_ONE = 0.9
BETA_TWO = 0.999
ADAM_EPS = 1e-08
MATRIX_RATE = 0.1
NORM_RATE = 0.6
DECAY_RATE = 0.1
MAX_NORM = 0.05

MESH = pl.DeviceIdType.MESH
F32 = jnp.float32
BF16 = jnp.bfloat16
MIB = 2**20


def grid_of(dp_count, head_count):
    x = 1
    while 4 * x * x <= dp_count:
        x *= 2
    return {"z": dp_count // x, "x": x, "y": head_count // 2, "c": 2}


class Links:
    def __init__(self, sizes, send, recv, local):
        self.sizes, self.send, self.recv, self.local = sizes, send, recv, local
        self.used = self.used_local = 0
        dp, head = lax.axis_index("dp"), lax.axis_index("head")
        self.at = {
            "z": lax.div(dp, sizes["x"]),
            "x": lax.rem(dp, sizes["x"]),
            "y": lax.div(head, sizes["c"]),
            "c": lax.rem(head, sizes["c"]),
        }
        self.head = head

    def place(self, axis, k):
        return lax.rem(self.at[axis] + k, self.sizes[axis])

    def peer(self, axis, k):
        at = dict(self.at)
        at[axis] = self.place(axis, k)
        return {
            "dp": at["z"] * self.sizes["x"] + at["x"],
            "head": at["y"] * self.sizes["c"] + at["c"],
        }

    def greet(self):
        barrier = pltpu.get_barrier_semaphore()
        for axis, n in self.sizes.items():
            for k in range(1, n):
                pl.semaphore_signal(
                    barrier, inc=1, device_id=self.peer(axis, k), device_id_type=MESH
                )

    def meet(self):
        barrier = pltpu.get_barrier_semaphore()
        pl.semaphore_wait(barrier, sum(n - 1 for n in self.sizes.values()))

    def copy(self, src, dst, slot, axis, k):
        return pltpu.make_async_remote_copy(
            src_ref=src,
            dst_ref=dst,
            send_sem=self.send.at[slot],
            recv_sem=self.recv.at[slot],
            device_id=self.peer(axis, k),
            device_id_type=MESH,
        )

    def take(self):
        self.used += 1
        return self.used - 1

    def move(self, src, dst):
        self.used_local += 1
        made = pltpu.make_async_copy(src, dst, self.local.at[self.used_local - 1])
        made.start()
        return made


class Gather:
    def __init__(self, links, order, view):
        self.links, self.order, self.view = links, order, view
        self.sent, self.coming = [], {}

    def region(self, step, place):
        at = dict(self.links.at)
        for axis in self.order[:step]:
            at[axis] = None
        at[self.order[step]] = place
        return self.view(at)

    def start(self, step):
        axis, links = self.order[step], self.links
        mine = self.region(step, links.at[axis])
        self.coming[step] = []
        for k in range(1, links.sizes[axis]):
            slot = links.take()
            copy = links.copy(mine, mine, slot, axis, k)
            copy.start()
            self.sent.append(copy)
            lands = self.region(step, links.place(axis, links.sizes[axis] - k))
            self.coming[step].append(links.copy(lands, lands, slot, axis, k))

    def wait(self, step):
        for copy in self.coming[step]:
            copy.wait_recv()

    def go(self, step):
        self.wait(step)
        if step + 1 < len(self.order):
            self.start(step + 1)

    def close(self):
        for copy in self.sent:
            copy.wait_send()


def some(place):
    return slice(None) if place is None else place


def dot(a, b):
    return lax.dot_general(a, b, (((1,), (0,)), ((), ())), preferred_element_type=F32)


def dot_nt(a, b):
    return lax.dot_general(a, b, (((1,), (1,)), ((), ())), preferred_element_type=F32)


def dot_tn(a, b):
    return lax.dot_general(a, b, (((0,), (0,)), ((), ())), preferred_element_type=F32)


def normed(values):
    center = values - jnp.mean(values, axis=-1, keepdims=True)
    scale = lax.rsqrt(jnp.mean(center * center, axis=-1, keepdims=True) + LN_EPS)
    return center * scale, scale


def diagonal(rows):
    n = GROUP // HEAD
    lat = rows.shape[0]
    tall = jnp.concatenate([rows] * n, axis=0)
    row = lax.broadcasted_iota(jnp.int32, tall.shape, 0) // lat
    col = lax.broadcasted_iota(jnp.int32, tall.shape, 1) // HEAD
    return jnp.where(row == col, tall, jnp.zeros_like(tall))


def undiagonal(tall):
    n = GROUP // HEAD
    lat = tall.shape[0] // n
    col = lax.broadcasted_iota(jnp.int32, (lat, GROUP), 1) // HEAD
    total = jnp.where(col == 0, tall[:lat], 0.0)
    for h in range(1, n):
        total = total + jnp.where(col == h, tall[h * lat : (h + 1) * lat], 0.0)
    return total


def weight_block(weights, m, g, sizes):
    block = weights.shape[-1]
    per = GROUP // block
    parts = []
    for s in range(per):
        h = g * per + s
        part = weights[m, lax.div(h, sizes["c"]), lax.rem(h, sizes["c"])]
        parts.append(part.reshape(D, block))
    return parts[0] if per == 1 else jnp.concatenate(parts, axis=1)


def softmax_columns(keys, spread_queries, seen):
    scores = dot_nt(keys, spread_queries)
    scores = jnp.where(seen, scores, -1e30)
    raised = jnp.exp(scores - jnp.max(scores, axis=0, keepdims=True))
    return raised * (1.0 / jnp.sum(raised, axis=0, keepdims=True))


def forward_kernel(
    sizes,
    att_ref,
    expand_ref,
    reduce_ref,
    tokens_ref,
    latents_ref,
    cotangent_ref,
    counts_ref,
    norm_ref,
    att_out,
    ff_out,
    pairs_out,
    turned_out,
    queries_out,
    mixed_out,
    middle_out,
    rows_out,
    back_out,
    att,
    ff,
    pairs,
    turned,
    queries,
    mixed,
    middle,
    rows,
    back,
    tokens,
    inputs,
    send,
    recv,
    local,
):
    links = Links(sizes, send, recv, local)
    links.greet()
    images, patches, _ = tokens.shape
    span = inputs.shape[1]
    lat = span - patches
    at = links.at
    outs = []

    loads = [links.move(tokens_ref.at[i], tokens.at[i]) for i in range(images)]
    for m in range(4):
        att[m, at["y"], at["c"], at["z"], at["x"]] = att_ref[m].astype(BF16)
    back[at["y"], at["c"]] = cotangent_ref[...].astype(BF16)
    ff[0, at["z"], at["x"]] = expand_ref[...].astype(BF16)
    ff[1, at["z"], at["x"]] = reduce_ref[...].astype(BF16)

    half = att.shape[5] // 2

    def att_view(m, s):
        def view(p):
            return att.at[m, some(p["y"]), some(p["c"]), some(p["z"]), some(p["x"]), pl.ds(s * half, half)]

        return view

    piece = max(16, att.shape[5] // 4)
    pieces = att.shape[5] // piece

    def ff_view(m, s):
        def view(p):
            return ff.at[m, some(p["z"]), some(p["x"]), pl.ds(s * piece, piece)]

        return view

    def back_view(p):
        return back.at[some(p["y"]), some(p["c"])]

    def row_view(i):
        def view(p):
            return rows.at[some(p["y"]), some(p["c"]), pl.ds(i * lat, lat)]

        return view

    query = [Gather(links, "zxyc", att_view(0, s)) for s in range(2)]
    key = [Gather(links, "zxyc", att_view(1, 0)), Gather(links, "yzxc", att_view(1, 1))]
    value = [Gather(links, "zyxc", att_view(2, 0)), Gather(links, "xzyc", att_view(2, 1))]
    output = [Gather(links, "zxyc", att_view(3, s)) for s in range(2)]
    hidden = [Gather(links, "zx", ff_view(m, s)) for m in range(2) for s in range(pieces)]
    cotangent = [Gather(links, "yc", back_view)]
    ff_rows = [Gather(links, "yc", row_view(i)) for i in range(images)]
    everything = [*query, *key, *value, *output, *hidden, *cotangent, *ff_rows]

    def start(parts):
        for part in parts:
            part.start(0)

    def go(parts, step):
        for part in parts:
            part.go(step)

    links.meet()
    start(key + value)

    for i in range(images):
        low = normed(latents_ref[pl.ds(i * lat, lat)].astype(F32))[0] * norm_ref[2:3] + norm_ref[3:4]
        inputs[i, pl.ds(patches, lat)] = low.astype(BF16)

    def normalize(i):
        loads[i].wait()
        tile = 64

        def one(t, _):
            part = pl.ds(pl.multiple_of(t * tile, tile), tile)
            low = normed(tokens[i, part].astype(F32))[0] * norm_ref[0:1] + norm_ref[1:2]
            inputs[i, part] = low.astype(BF16)
            return 0

        lax.fori_loop(0, patches // tile, one, 0)

    def turn(i):
        def one(t, _):
            part = pl.ds(pl.multiple_of(t * 128, 128), 128)
            turned[:, pl.ds(pl.multiple_of(i * span + t * 128, 128), 128)] = inputs[i, part].T
            return 0

        lax.fori_loop(0, span // 128, one, 0)

    steps = [
        lambda: (go(key, 0), go(value, 0), start(query + output)),
        lambda: None,
        lambda: (go(key, 1), go(value, 1), start(hidden)),
        lambda: None,
        lambda: (go(key, 2), go(value, 2)),
        lambda: go(query + output, 0),
        lambda: None,
        lambda: go(query, 1),
    ]

    def tick():
        if steps:
            steps.pop(0)()

    for i in range(images):
        normalize(i)
        tick()
        turn(i)
        tick()
    while steps:
        tick()
    outs.append(links.move(turned, turned_out))
    go(key, 3)

    def project(i, m):
        def one(g, _):
            weight = weight_block(att, m, g, sizes)
            pairs[i, (m - 1) * GROUPS + g] = dot(inputs[i], weight).astype(BF16)
            return 0

        lax.fori_loop(0, GROUPS, one, 0)

    def attend(i):
        position = lax.broadcasted_iota(jnp.int32, (span, GROUP), 0)
        count = counts_ref[links.head * images + i]
        seen = (position < count) | (position >= patches)

        def one(g, _):
            spread = diagonal(queries[g, pl.ds(i * lat, lat)])
            probs = softmax_columns(pairs[i, g], spread, seen).astype(BF16)
            wide = dot_tn(probs, pairs[i, GROUPS + g])
            mixed[g, pl.ds(i * lat, lat)] = undiagonal(wide).astype(BF16)
            return 0

        lax.fori_loop(0, GROUPS, one, 0)

    def finish(i):
        part = pl.ds(i * lat, lat)
        whole = jnp.concatenate([mixed[g, part] for g in range(GROUPS)], axis=1)
        made = jnp.concatenate(
            [dot(whole, weight_block(att, 3, g, sizes)) for g in range(GROUPS)], axis=1
        )
        value = latents_ref[part].astype(F32) + made
        middle[part] = value
        low = normed(value)[0] * norm_ref[4:5] + norm_ref[5:6]
        rows[at["y"], at["c"], part] = low.astype(BF16)
        ff_rows[i].start(0)

    def near(p):
        return lambda: go(hidden[p : p + 1], 0)

    steps += [
        lambda: go(output, 1),
        lambda: go(value, 3),
        near(0),
        lambda: None,
        lambda: go(query, 2),
        near(1),
        lambda: None,
        near(2),
    ]
    for i in range(images):
        project(i, 1)
        tick()
    if images < 2:
        tick()
    for i in range(images):
        project(i, 2)
        outs.append(links.move(pairs.at[i], pairs_out.at[i]))
        tick()
    while steps:
        tick()
    go(query, 3)
    stack = inputs[:, patches:].reshape(images * lat, D)
    for g in range(GROUPS):
        made = dot(stack, weight_block(att, 0, g, sizes)) * HEAD ** (-0.5)
        queries[g] = made.astype(BF16)
    outs.append(links.move(queries, queries_out))
    steps += [
        lambda: (go(output, 2), start(cotangent)),
        near(3),
        lambda: go(output, 3),
        near(4),
    ]
    for i in range(images):
        attend(i)
        tick()
    while steps:
        tick()
    steps += [
        near(5),
        lambda: (go(ff_rows[:1], 0), go(cotangent, 0)),
        near(6),
        lambda: go(ff_rows[1:2], 0),
    ]
    for i in range(images):
        finish(i)
        tick()
    while steps:
        tick()
    go(hidden[7:], 0)
    outs.append(links.move(att, att_out))
    outs.append(links.move(mixed, mixed_out))
    outs.append(links.move(middle, middle_out))
    go(ff_rows[2:], 0)
    go(cotangent, 1)
    outs.append(links.move(back, back_out))
    go(ff_rows, 1)
    outs.append(links.move(rows, rows_out))
    go(hidden, 1)
    outs.append(links.move(ff, ff_out))
    for part in everything:
        part.close()
    for out in outs:
        out.wait()


def forward(att, expand, reduce_turned, tokens, latents, cotangent, counts, norm_params):
    sizes = grid_of(lax.axis_size("dp"), lax.axis_size("head"))
    z, x, y, c = (sizes[a] for a in "zxyc")
    images, patches, _ = tokens.shape
    lat = latents.shape[1]
    span = patches + lat
    n = images * lat
    _, row_block, col_block = att.shape
    ff_block = expand.shape[1]
    shapes = dict(
        att=((4, y, c, z, x, row_block, col_block), BF16),
        ff=((2, z, x, row_block, ff_block), BF16),
        pairs=((images, 2 * GROUPS, span, GROUP), BF16),
        turned=((D, images * span), BF16),
        queries=((GROUPS, n, GROUP), BF16),
        mixed=((GROUPS, n, GROUP), BF16),
        middle=((n, D), F32),
        rows=((y, c, n, D), BF16),
        back=((y, c, n, D), BF16),
    )
    inside = [((images, patches, D), BF16), ((images, span, D), BF16)]
    per_att = sum(s - 1 for s in sizes.values())
    slots = 8 * per_att + 8 * (z + x - 2) + (1 + images) * (y + c - 2)
    vmem, anywhere = pl.BlockSpec(memory_space=pltpu.VMEM), pl.BlockSpec(memory_space=pl.ANY)
    made = pl.pallas_call(
        functools.partial(forward_kernel, sizes),
        out_shape=[jax.ShapeDtypeStruct(*v) for v in shapes.values()],
        in_specs=[vmem, vmem, vmem, anywhere, vmem, vmem, pl.BlockSpec(memory_space=pltpu.SMEM), vmem],
        out_specs=[anywhere] * len(shapes),
        scratch_shapes=[pltpu.VMEM(*v) for v in [*shapes.values(), *inside]]
        + [
            pltpu.SemaphoreType.DMA((slots,)),
            pltpu.SemaphoreType.DMA((slots,)),
            pltpu.SemaphoreType.DMA((3 * images + 8,)),
        ],
        compiler_params=pltpu.CompilerParams(
            collective_id=0, has_side_effects=True, vmem_limit_bytes=58 * MIB
        ),
        name="gather_and_attend",
    )(att, expand, reduce_turned, tokens, latents.reshape(n, D), cotangent.reshape(n, D), counts, norm_params)
    return SimpleNamespace(**dict(zip(shapes, made)))


class Scatter:
    def __init__(self, links, order, view, lands):
        self.links, self.order, self.view, self.lands = links, order, view, lands
        self.slots = {}

    def region(self, step, place):
        at = dict(self.links.at)
        for axis in self.order[step + 1 :]:
            at[axis] = None
        at[self.order[step]] = place
        return self.view(at)

    def copies(self, step):
        axis, links = self.order[step], self.links
        for k, slot in enumerate(self.slots[step], 1):
            yield links.copy(self.region(step, links.place(axis, k)), self.lands[step][k - 1], slot, axis, k)

    def start(self, step):
        self.slots[step] = [self.links.take() for _ in range(1, self.links.sizes[self.order[step]])]
        for copy in self.copies(step):
            copy.start()

    def wait(self, step):
        for k, slot in enumerate(self.slots[step], 1):
            land = self.lands[step][k - 1]
            self.links.copy(land, land, slot, self.order[step], k).wait_recv()

    def add(self, step, out=None):
        mine = self.region(step, self.links.at[self.order[step]])
        lands = self.lands[step]
        lead = mine.shape[0] if len(mine.shape) > 2 else None

        def total(at):
            value = mine[at].astype(F32)
            for land in lands:
                value = value + land[at].astype(F32)
            return value

        if out is not None:
            out[...] = total(Ellipsis)
        elif lead is None:
            mine[...] = total(Ellipsis).astype(BF16)
        else:

            def one(t, _):
                mine[t] = total(t).astype(BF16)
                return 0

            lax.fori_loop(0, lead, one, 0)

    def go(self, step, out=None):
        self.wait(step)
        self.add(step, out)
        if step + 1 < len(self.order):
            self.start(step + 1)

    def close(self):
        for step in self.slots:
            for copy in self.copies(step):
                copy.wait_send()


def norm_back(up, hat, scale, gain):
    inner = up * gain
    return scale * (
        inner
        - jnp.mean(inner, axis=-1, keepdims=True)
        - hat * jnp.mean(inner * hat, axis=-1, keepdims=True)
    )


def fold(rows):
    return jnp.sum(rows.reshape(rows.shape[0] // 8, 8, rows.shape[1]), axis=0)


def gelu_and_slope(v):
    root = 0.7978845608028654
    square = v * v
    t = jnp.tanh(root * v * (1.0 + 0.044715 * square))
    half = 0.5 + 0.5 * t
    slope = half + (0.5 * root) * v * (1.0 - t * t) * (1.0 + (3.0 * 0.044715) * square)
    return v * half, slope


ATT_ORDERS = {0: ("yxz", "yxz"), 1: ("yxz", "xyz"), 2: ("yxz", "yxz"), 3: ("yxz", "yxz")}


def land_shapes(sizes, order, axes, tail):
    shapes, left = [], list(axes)
    for axis in order:
        left.remove(axis)
        shapes.append((sizes[axis] - 1, *(sizes[a] for a in left), *tail))
    return shapes


def backward_kernel(sizes, dims, *refs):
    names, keys, images, patches, lat, ff_block = dims
    r = SimpleNamespace(**dict(zip(names, refs)))
    total_lands = dict(zip("cyxz", refs[len(names) :]))
    att_lands = dict(zip(keys, refs[len(names) + 4 :]))
    links = Links(sizes, r.send, r.recv, r.local)
    links.greet()
    at = links.at
    sib = links.place("c", 1)
    n = images * lat
    span = patches + lat
    zs, xs, ys, cs = (sizes[a] for a in "zxyc")
    row_block, col_block = r.att_share.shape[1:]
    xr = xs * row_block
    heads = ys * cs
    half = row_block // 2
    norm_ref, middle, cotangent, latents = r.norm, r.middle, r.cotangent, r.latents
    queries, mixed = r.queries, r.mixed
    grads_ff = r.grads_ff
    middle_grad, branch, mixed_grad, query_back = r.middle_grad, r.branch, r.mixed_grad, r.query_back
    outs = []

    units = [(m, k) for k in [*range(1, zs), 0] for m in (1, 0)]
    x_slots = {unit: [links.take() for _ in range(1, xs)] for unit in units}
    z_slots = {unit: links.take() for unit in units if unit[1]}

    def x_copies(unit):
        m, k = unit
        z = links.place("z", k)
        for j, slot in enumerate(x_slots[unit], 1):
            yield links.copy(
                grads_ff.at[m, z, links.place("x", j)], r.ff_land_x.at[m, z, j - 1], slot, "x", j
            )

    def z_copy(unit):
        m, k = unit
        return links.copy(
            grads_ff.at[m, links.place("z", k), at["x"]], r.ff_land_z.at[m, k - 1], z_slots[unit], "z", k
        )

    def ff_along(unit):
        m, k = unit
        z = links.place("z", k)
        for copy in x_copies(unit):
            copy.wait_recv()
        total = grads_ff[m, z, at["x"]].astype(F32)
        for j in range(xs - 1):
            total = total + r.ff_land_x[m, z, j].astype(F32)
        if k:
            grads_ff[m, z, at["x"]] = total.astype(BF16)
            z_copy(unit).start()
        else:
            r.ff_share[m] = total

    def ff_finish():
        for m in range(2):
            for k in range(1, zs):
                z_copy((m, k)).wait_recv()
            total = r.ff_share[m]
            for k in range(1, zs):
                total = total + r.ff_land_z[m, k - 1].astype(F32)
            r.ff_share[m] = total

    pairs = r.pairs_here
    early = [links.move(r.pairs.at[i], pairs.at[i]) for i in range(images)]

    def feed_forward(ffw, rows, back, hidden, bg, part):
        loads = [links.move(r.ff, ffw), links.move(r.rows, rows), links.move(r.back, back)]
        links.meet()
        for load in loads:
            load.wait()
        tile = min(GROUP, ff_block)

        def first(yi):
            def one(t, _):
                cols = pl.ds(pl.multiple_of(t * tile, tile), tile)
                before = dot(rows[yi].reshape(cs * n, D), ffw[0, :, :, :, cols].reshape(D, tile))
                up = dot(back[yi].reshape(cs * n, D), ffw[1, :, :, :, cols].reshape(D, tile))
                made, slope = gelu_and_slope(before)
                hidden[yi, :, :, cols] = made.astype(BF16).reshape(cs, n, tile)
                bg[yi, :, :, cols] = (up * slope).astype(BF16).reshape(cs, n, tile)
                return 0

            lax.fori_loop(0, ff_block // tile, one, 0)

        def second(kind, yi):
            left = hidden if kind else bg

            def one(z, _):
                cols = pl.ds(pl.multiple_of(z * xr, xr), xr)
                made = dot_nt(left[yi].reshape(cs * n, ff_block), ffw[kind, z].reshape(xr, ff_block))
                part[kind, yi, :, :, cols] = made.astype(BF16).reshape(cs, n, xr)
                return 0

            lax.fori_loop(0, zs, one, 0)

        sent, chip, along = [], {}, {}

        def to_sibling(kind, k):
            yi = links.place("y", k)
            slot = links.take()
            land = r.land_c.at[kind, yi]
            copy = links.copy(part.at[kind, yi, sib], land, slot, "c", 1)
            copy.start()
            sent.append(copy)
            chip[kind, k] = links.copy(land, land, slot, "c", 1)

        def along_y(kind, k):
            yi = links.place("y", k)
            chip[kind, k].wait_recv()
            summed = part[kind, yi, at["c"]].astype(F32) + r.land_c[kind, yi].astype(F32)
            r.sum_y[kind, k - 1] = summed.astype(BF16)
            slot = links.take()
            land = r.land_y.at[kind, k - 1]
            copy = links.copy(r.sum_y.at[kind, k - 1], land, slot, "y", k)
            copy.start()
            along[kind, k] = (copy, links.copy(land, land, slot, "y", k))

        for k in range(1, ys):
            yi = links.place("y", k)
            first(yi)
            second(0, yi)
            to_sibling(0, k)
            second(1, yi)
            to_sibling(1, k)
        first(at["y"])
        for k in range(1, ys):
            along_y(0, k)
        second(0, at["y"])
        to_sibling(0, 0)
        second(1, at["y"])
        to_sibling(1, 0)
        for k in range(1, ys):
            along_y(1, k)

        def gradient(unit):
            m, k = unit
            z = links.place("z", k)
            cols = pl.ds(pl.multiple_of(z * xr, xr), xr)
            left, right = (back, hidden) if m else (rows, bg)
            made = dot_tn(left[:, :, :, cols].reshape(heads * n, xr), right[...].reshape(heads * n, ff_block))
            grads_ff[m, z] = made.astype(BF16).reshape(xs, row_block, ff_block)
            for copy in x_copies(unit):
                copy.start()

        for unit in units:
            gradient(unit)
        chip[0, 0].wait_recv()
        for k in range(1, ys):
            along[0, k][1].wait_recv()

        def back_one(t, carry):
            gain, shift = carry
            rws = pl.ds(pl.multiple_of(t * lat, lat), lat)
            up = part[0, at["y"], at["c"], rws].astype(F32) + r.land_c[0, at["y"], rws].astype(F32)
            for k in range(1, ys):
                up = up + r.land_y[0, k - 1, rws].astype(F32)
            hat, scale = normed(middle[rws])
            value = cotangent[rws] + norm_back(up, hat, scale, norm_ref[4:5])
            middle_grad[rws] = value
            branch[rws] = value.astype(BF16)
            return gain + fold(up * hat), shift + fold(up)

        zero = jnp.zeros((8, D), F32)
        ff_gain, ff_shift = lax.fori_loop(0, images, back_one, (zero, zero))
        r.norm_parts[4] = ff_gain
        r.norm_parts[5] = ff_shift
        chip[1, 0].wait_recv()
        for k in range(1, ys):
            along[1, k][1].wait_recv()

        def out_one(t, _):
            rws = pl.ds(pl.multiple_of(t * lat, lat), lat)
            up = part[1, at["y"], at["c"], rws].astype(F32) + r.land_c[1, at["y"], rws].astype(F32)
            for k in range(1, ys):
                up = up + r.land_y[1, k - 1, rws].astype(F32)
            rows[at["y"], at["c"], rws] = (middle[rws] + up).astype(BF16)
            return 0

        lax.fori_loop(0, images, out_one, 0)
        leaving = links.move(rows.at[at["y"], at["c"]], r.resampled)
        for copy in sent:
            copy.wait_send()
        for copy, _ in along.values():
            copy.wait_send()
        leaving.wait()

    pl.run_scoped(
        feed_forward,
        pltpu.VMEM((2, zs, xs, row_block, ff_block), BF16),
        pltpu.VMEM((ys, cs, n, D), BF16),
        pltpu.VMEM((ys, cs, n, D), BF16),
        pltpu.VMEM((ys, cs, n, ff_block), BF16),
        pltpu.VMEM((ys, cs, n, ff_block), BF16),
        pltpu.VMEM((2, ys, cs, n, D), BF16),
    )

    steps = []

    def tick():
        if steps:
            steps.pop(0)()

    def later(f, *args):
        steps.append(lambda: f(*args))

    def attention(grads, turned_left):
        per = GROUP // col_block
        block_slots = {m: [links.take() for _ in range(ys)] for m in range(4)}

        def block_copy(m, yi):
            slot = block_slots[m][0] + yi
            return links.copy(grads.at[m, yi, sib], r.att_land_c.at[m, yi], slot, "c", 1)

        def att_scatter(m, s):
            def view(p):
                return grads.at[m, some(p["y"]), at["c"], some(p["z"]), some(p["x"]), pl.ds(s * half, half)]

            order = ATT_ORDERS[m][s]
            lands = [
                [att_lands[m, s, step].at[k] for k in range(sizes[axis] - 1)]
                for step, axis in enumerate(order)
            ]
            return Scatter(links, order, view, lands)

        scatter = {m: [att_scatter(m, s) for s in range(2)] for m in range(4)}

        def go(m, step):
            for s, part in enumerate(scatter[m]):
                part.go(step, r.att_share.at[m, pl.ds(s * half, half)] if step == 2 else None)

        def chip_sum(m):
            for yi in range(ys):
                block_copy(m, yi).wait_recv()

                def one(z, _):
                    value = grads[m, yi, at["c"], z].astype(F32) + r.att_land_c[m, yi, z].astype(F32)
                    grads[m, yi, at["c"], z] = value.astype(BF16)
                    return 0

                lax.fori_loop(0, zs, one, 0)
            for part in scatter[m]:
                part.start(0)

        def products(m, left, right, between=None):
            def of(ci, send):
                def one(yi, _):
                    made = dot(left(), right(yi * cs + ci)).astype(BF16)
                    grads[m, yi, ci] = made.reshape(zs, xs, row_block, col_block)
                    if send:
                        block_copy(m, yi).start()
                    return 0

                lax.fori_loop(0, ys, one, 0)

            of(sib, True)
            if between is not None:
                between()
            of(at["c"], False)

        def query_columns(h):
            j = lax.div(h * col_block, GROUP)
            if per == 1:
                return query_back[j]
            off = pl.multiple_of(lax.rem(h, per) * col_block, col_block)
            return query_back[j, :, pl.ds(off, col_block)]

        def columns(m):
            def right(h):
                j = lax.div(h * col_block, GROUP) + (m - 1) * GROUPS
                if per == 1:
                    return pairs[:, j].reshape(images * span, GROUP)
                off = pl.multiple_of(lax.rem(h, per) * col_block, col_block)
                return pairs[:, j, :, pl.ds(off, col_block)].reshape(images * span, col_block)

            return right

        def attend(i):
            position = lax.broadcasted_iota(jnp.int32, (span, GROUP), 0)
            count = r.counts[links.head * images + i]
            seen = (position < count) | (position >= patches)
            rws = pl.ds(i * lat, lat)

            def one(g, _):
                keys, values = pairs[i, g], pairs[i, GROUPS + g]
                spread = diagonal(queries[g, rws])
                probs = softmax_columns(keys, spread, seen)
                upstream = diagonal(mixed_grad[g, rws])
                prob_grad = dot_nt(values, upstream)
                inner = jnp.sum(probs * prob_grad, axis=0, keepdims=True)
                score_grad = (probs * (prob_grad - inner)).astype(BF16)
                back = undiagonal(dot_tn(score_grad, keys)) * HEAD ** (-0.5)
                query_back[g, rws] = back.astype(BF16)
                pairs[i, GROUPS + g] = dot(probs.astype(BF16), upstream).astype(BF16)
                pairs[i, g] = dot(score_grad, spread).astype(BF16)
                return 0

            lax.fori_loop(0, GROUPS, one, 0)

        def weights(turned, weight):
            load_weight = links.move(r.att.at[3], weight)
            load_turned = links.move(r.turned, turned)
            for g in range(GROUPS):
                turned_left[pl.ds(g * GROUP, GROUP)] = mixed[g].T
            products(
                3,
                lambda: turned_left[...],
                lambda h: branch[:, pl.ds(pl.multiple_of(h * col_block, col_block), col_block)],
            )
            load_weight.wait()
            for g in range(GROUPS):
                first = g * GROUP // row_block
                wide = []
                for h in range(heads):
                    blocks = [
                        weight[h // cs, h % cs, b // xs, b % xs] for b in range(first, first + GROUP // row_block)
                    ]
                    wide.append(jnp.concatenate(blocks, axis=0))
                mixed_grad[g] = dot_nt(branch[...], jnp.concatenate(wide, axis=1)).astype(BF16)
            ff_steps = [lambda u=u: ff_along(u) for u in units]
            steps.append(lambda: (chip_sum(3), ff_steps[0]()))
            steps.extend(ff_steps[1:])
            for i in range(images):
                attend(i)
                tick()
            load_turned.wait()
            for i in range(images):
                turned_left[:, pl.ds(i * lat, lat)] = turned[:, i * span + patches : (i + 1) * span]
            products(0, lambda: turned_left[...], query_columns)
            steps.insert(0, lambda: go(3, 0))
            steps.insert(2, lambda: chip_sum(0))
            tick()
            products(2, lambda: turned[...], columns(2), tick)
            steps.insert(1, lambda: chip_sum(2))
            tick()
            products(1, lambda: turned[...], columns(1), tick)
            tick()

        pl.run_scoped(
            weights,
            pltpu.VMEM((D, images * span), BF16),
            pltpu.VMEM((ys, cs, zs, xs, row_block, col_block), BF16),
        )

        def inputs(att, tokens, pair_grad):
            weight_loads = [links.move(r.att.at[m], att.at[m]) for m in (1, 2, 0)]
            loads = {}

            def fetch(i):
                loads[i] = links.move(r.tokens.at[i], tokens.at[i % 2])

            media_out = {}
            fetch(0)
            tick()
            steps.insert(0, lambda: chip_sum(1))
            for m, step in ((3, 1), (0, 0), (2, 0), (1, 0), (3, 2), (0, 1), (2, 1), (1, 1), (0, 2), (2, 2)):
                later(go, m, step)
            zero = jnp.zeros((8, D), F32)
            sums = (zero, zero, zero, zero)
            for load in weight_loads:
                load.wait()
            for i in range(images):
                stacked = jnp.concatenate([pairs[i, j] for j in range(2 * GROUPS)], axis=1)
                asked = jnp.concatenate([query_back[g, pl.ds(i * lat, lat)] for g in range(GROUPS)], axis=1)

                def one(z, _):
                    cols = pl.ds(pl.multiple_of(z * xr, xr), xr)
                    wide = jnp.concatenate(
                        [att[m, h // cs, h % cs, z].reshape(xr, col_block) for m in (1, 2) for h in range(heads)], axis=1
                    )
                    narrow = jnp.concatenate(
                        [att[0, h // cs, h % cs, z].reshape(xr, col_block) for h in range(heads)], axis=1
                    )
                    pair_grad[:, cols] = dot_nt(stacked, wide)
                    pair_grad[patches:, cols] += dot_nt(asked, narrow)
                    return 0

                lax.fori_loop(0, zs, one, 0)
                tick()
                tick()
                if i + 1 < images:
                    if i >= 1:
                        media_out[i - 1].wait()
                    fetch(i + 1)
                loads[i].wait()
                slot = i % 2
                tile = 64

                def media(t, carry):
                    gain, shift = carry
                    rws = pl.ds(pl.multiple_of(t * tile, tile), tile)
                    hat, scale = normed(tokens[slot, rws].astype(F32))
                    up = pair_grad[rws]
                    tokens[slot, rws] = norm_back(up, hat, scale, norm_ref[0:1]).astype(BF16)
                    return gain + fold(up * hat), shift + fold(up)

                gain, shift = lax.fori_loop(0, patches // tile, media, (sums[0], sums[1]))
                media_out[i] = links.move(tokens.at[slot], r.media_grad.at[i])
                rws = pl.ds(i * lat, lat)
                hat, scale = normed(latents[rws].astype(F32))
                up = pair_grad[patches:]
                made = middle_grad[rws] + norm_back(up, hat, scale, norm_ref[2:3])
                branch[rws] = made.astype(BF16)
                sums = (gain, shift, sums[2] + fold(up * hat), sums[3] + fold(up))
                tick()
                tick()
            for k, value in enumerate(sums):
                r.norm_parts[k] = value
            for i in range(max(0, images - 2), images):
                media_out[i].wait()

        pl.run_scoped(
            inputs,
            pltpu.VMEM((3, ys, cs, zs, xs, row_block, col_block), BF16),
            pltpu.VMEM((2, patches, D), BF16),
            pltpu.VMEM((span, D), F32),
        )
        while steps:
            tick()
        go(1, 2)
        ff_finish()
        for m in range(4):
            for yi in range(ys):
                block_copy(m, yi).wait_send()
            for part in scatter[m]:
                part.close()
        for unit in units:
            for copy in x_copies(unit):
                copy.wait_send()
            if unit[1]:
                z_copy(unit).wait_send()

    for load in early:
        load.wait()
    pl.run_scoped(
        attention,
        pltpu.VMEM((4, ys, cs, zs, xs, row_block, col_block), BF16),
        pltpu.VMEM((D, n), BF16),
    )

    outs.append(links.move(branch, r.latent_grad))
    squares = jnp.sum(r.att_share[...] * r.att_share[...]) + jnp.sum(r.ff_share[...] * r.ff_share[...])
    rows = [jnp.sum(r.norm_parts[k], axis=0, keepdims=True) for k in range(6)]
    value = jnp.concatenate([*rows, jnp.full((2, D), squares, F32)], axis=0)
    last = []
    for axis in "cyxz":
        lands = total_lands[axis]
        lands[at[axis]] = value
        coming = []
        for k in range(1, sizes[axis]):
            slot = links.take()
            mine = lands.at[at[axis]]
            copy = links.copy(mine, mine, slot, axis, k)
            copy.start()
            last.append(copy)
            land = lands.at[links.place(axis, sizes[axis] - k)]
            coming.append(links.copy(land, land, slot, axis, k))
        for copy in coming:
            copy.wait_recv()
        value = lands[0]
        for k in range(1, sizes[axis]):
            value = value + lands[k]
    r.totals[...] = value
    for copy in last:
        copy.wait_send()
    for out in outs:
        out.wait()


def backward(got, tokens, latents, cotangent, counts, norm_params, row_block, col_block, ff_block):
    sizes = grid_of(lax.axis_size("dp"), lax.axis_size("head"))
    zs, xs, ys, cs = (sizes[a] for a in "zxyc")
    images, patches, _ = tokens.shape
    lat = latents.shape[1]
    n = images * lat
    half = row_block // 2
    vmem, anywhere = pl.BlockSpec(memory_space=pltpu.VMEM), pl.BlockSpec(memory_space=pl.ANY)
    smem = pl.BlockSpec(memory_space=pltpu.SMEM)
    inputs = dict(
        att=(got.att, anywhere),
        ff=(got.ff, anywhere),
        rows=(got.rows, anywhere),
        back=(got.back, anywhere),
        pairs=(got.pairs, anywhere),
        turned=(got.turned, anywhere),
        tokens=(tokens, anywhere),
        queries=(got.queries, vmem),
        mixed=(got.mixed, vmem),
        middle=(got.middle, vmem),
        latents=(latents.reshape(n, D), vmem),
        cotangent=(cotangent.reshape(n, D), vmem),
        norm=(norm_params, vmem),
        counts=(counts, smem),
    )
    outputs = dict(
        resampled=((n, D), BF16, anywhere),
        media_grad=((images, patches, D), BF16, anywhere),
        latent_grad=((n, D), BF16, anywhere),
        att_share=((4, row_block, col_block), F32, vmem),
        ff_share=((2, row_block, ff_block), F32, vmem),
        totals=((8, D), F32, vmem),
    )
    scratch = dict(
        grads_ff=((2, zs, xs, row_block, ff_block), BF16),
        ff_land_x=((2, zs, xs - 1, row_block, ff_block), BF16),
        ff_land_z=((2, zs - 1, row_block, ff_block), BF16),
        att_land_c=((4, ys, zs, xs, row_block, col_block), BF16),
        pairs_here=(got.pairs.shape, BF16),
        land_c=((2, ys, n, D), BF16),
        land_y=((2, ys - 1, n, D), BF16),
        sum_y=((2, ys - 1, n, D), BF16),
        middle_grad=((n, D), F32),
        branch=((n, D), BF16),
        mixed_grad=((GROUPS, n, GROUP), BF16),
        query_back=((GROUPS, n, GROUP), BF16),
        norm_parts=((6, 8, D), F32),
    )
    totals = [((sizes[axis], 8, D), F32) for axis in "cyxz"]
    lands = {}
    for m, orders in ATT_ORDERS.items():
        for s, order in enumerate(orders):
            for step, shape in enumerate(land_shapes(sizes, order, "yzx", (half, col_block))):
                lands[m, s, step] = (shape, BF16)
    steps = sum(v - 1 for v in sizes.values())
    slots = 9 * steps + 2 * (zs * xs + zs) + 6 * ys
    semaphores = dict(send=slots, recv=slots, local=3 * images + 16)
    names = [*inputs, *outputs, *semaphores, *scratch]
    made = pl.pallas_call(
        functools.partial(backward_kernel, sizes, (names, tuple(lands), images, patches, lat, ff_block)),
        out_shape=[jax.ShapeDtypeStruct(shape, dtype) for shape, dtype, _ in outputs.values()],
        in_specs=[spec for _, spec in inputs.values()],
        out_specs=[spec for _, _, spec in outputs.values()],
        scratch_shapes=[pltpu.SemaphoreType.DMA((v,)) for v in semaphores.values()]
        + [pltpu.VMEM(*v) for v in [*scratch.values(), *totals, *lands.values()]],
        compiler_params=pltpu.CompilerParams(
            collective_id=1, has_side_effects=True, vmem_limit_bytes=63 * MIB + 900 * 1024
        ),
        name="backward_and_scatter",
    )(*(value for value, _ in inputs.values()))
    return SimpleNamespace(**dict(zip(outputs, made)))


def adam_step(master, first, second, gradient, step_rate, decay_rate):
    first_new = BETA_ONE * first + (1.0 - BETA_ONE) * gradient
    second_new = BETA_TWO * second + (1.0 - BETA_TWO) * gradient * gradient
    first_hat = first_new / (1.0 - BETA_ONE**STEP)
    second_hat = second_new / (1.0 - BETA_TWO**STEP)
    master_new = master - step_rate * (
        first_hat / (jnp.sqrt(second_hat) + ADAM_EPS) + decay_rate * master
    )
    return (master_new, first_new, second_new)


def on_device(
    media_tokens,
    latents,
    cotangent,
    counts,
    attention_weights,
    attention_first,
    attention_second,
    expand_weight,
    expand_first,
    expand_second,
    reduce_weight,
    reduce_first,
    reduce_second,
    norm_params,
    norm_first,
    norm_second,
):
    _, row_block, col_block = attention_weights.shape
    got = forward(
        attention_weights,
        expand_weight,
        reduce_weight.T,
        media_tokens,
        latents,
        cotangent,
        counts,
        norm_params,
    )
    back = backward(
        got, media_tokens, latents, cotangent, counts, norm_params, row_block, col_block, expand_weight.shape[1]
    )
    norm_total, squares_total = back.totals[:6], back.totals[6, 0]
    grad_norm = jnp.sqrt(squares_total + jnp.sum(norm_total * norm_total))
    clip_factor = jnp.minimum(1.0, MAX_NORM / (grad_norm + 1e-06))
    attention = adam_step(
        attention_weights,
        attention_first,
        attention_second,
        back.att_share * clip_factor,
        MATRIX_RATE,
        DECAY_RATE,
    )
    expand = adam_step(
        expand_weight, expand_first, expand_second, back.ff_share[0] * clip_factor, MATRIX_RATE, DECAY_RATE
    )
    reduce = adam_step(
        reduce_weight, reduce_first, reduce_second, back.ff_share[1].T * clip_factor, MATRIX_RATE, DECAY_RATE
    )
    norm = adam_step(norm_params, norm_first, norm_second, norm_total * clip_factor, NORM_RATE, 0.0)
    return (
        back.resampled.reshape(latents.shape),
        back.media_grad,
        back.latent_grad.reshape(latents.shape),
        grad_norm,
        *attention,
        *expand,
        *reduce,
        *norm,
    )


def solution(mesh):
    in_specs = (
        P(("dp", "head"), None, None),
        P(("dp", "head"), None, None),
        P(("dp", "head"), None, None),
        P("dp"),
        P(None, "dp", "head"),
        P(None, "dp", "head"),
        P(None, "dp", "head"),
        P("dp", "head"),
        P("dp", "head"),
        P("dp", "head"),
        P("head", "dp"),
        P("head", "dp"),
        P("head", "dp"),
        P(),
        P(),
        P(),
    )
    out_specs = (
        P(("dp", "head"), None, None),
        P(("dp", "head"), None, None),
        P(("dp", "head"), None, None),
        P(),
        P(None, "dp", "head"),
        P(None, "dp", "head"),
        P(None, "dp", "head"),
        P("dp", "head"),
        P("dp", "head"),
        P("dp", "head"),
        P("head", "dp"),
        P("head", "dp"),
        P("head", "dp"),
        P(),
        P(),
        P(),
    )
    return jax.shard_map(
        on_device, mesh=mesh, in_specs=in_specs, out_specs=out_specs, check_vma=False
    )
```

```python
import functools
from types import SimpleNamespace

import jax
import jax.numpy as jnp
from jax import lax
from jax.experimental import pallas as pl
from jax.experimental.pallas import tpu as pltpu
from jax.sharding import PartitionSpec as P

D = 1024
HEADS = 16
HEAD = D // HEADS
GROUP = 256
GROUPS = D // GROUP
STEP = 10

LN_EPS = 1e-05
BETA_ONE = 0.9
BETA_TWO = 0.999
ADAM_EPS = 1e-08
MATRIX_RATE = 0.1
NORM_RATE = 0.6
DECAY_RATE = 0.1
MAX_NORM = 0.05

MESH = pl.DeviceIdType.MESH
F32 = jnp.float32
BF16 = jnp.bfloat16
MIB = 2**20


def grid_of(dp_count, head_count):
    x = 1
    while 4 * x * x <= dp_count:
        x *= 2
    return {"z": dp_count // x, "x": x, "y": head_count // 2, "c": 2}


class Links:
    def __init__(self, sizes, send, recv, local):
        self.sizes, self.send, self.recv, self.local = sizes, send, recv, local
        self.used = self.used_local = 0
        dp, head = lax.axis_index("dp"), lax.axis_index("head")
        self.at = {
            "z": lax.div(dp, sizes["x"]),
            "x": lax.rem(dp, sizes["x"]),
            "y": lax.div(head, sizes["c"]),
            "c": lax.rem(head, sizes["c"]),
        }
        self.head = head

    def place(self, axis, k):
        return lax.rem(self.at[axis] + k, self.sizes[axis])

    def peer(self, axis, k):
        at = dict(self.at)
        at[axis] = self.place(axis, k)
        return {
            "dp": at["z"] * self.sizes["x"] + at["x"],
            "head": at["y"] * self.sizes["c"] + at["c"],
        }

    def greet(self):
        barrier = pltpu.get_barrier_semaphore()
        for axis, n in self.sizes.items():
            for k in range(1, n):
                pl.semaphore_signal(
                    barrier, inc=1, device_id=self.peer(axis, k), device_id_type=MESH
                )

    def meet(self):
        barrier = pltpu.get_barrier_semaphore()
        pl.semaphore_wait(barrier, sum(n - 1 for n in self.sizes.values()))

    def copy(self, src, dst, slot, axis, k):
        return pltpu.make_async_remote_copy(
            src_ref=src,
            dst_ref=dst,
            send_sem=self.send.at[slot],
            recv_sem=self.recv.at[slot],
            device_id=self.peer(axis, k),
            device_id_type=MESH,
        )

    def take(self):
        self.used += 1
        return self.used - 1

    def move(self, src, dst):
        self.used_local += 1
        made = pltpu.make_async_copy(src, dst, self.local.at[self.used_local - 1])
        made.start()
        return made


class Gather:
    def __init__(self, links, order, view):
        self.links, self.order, self.view = links, order, view
        self.sent, self.coming = [], {}

    def region(self, step, place):
        at = dict(self.links.at)
        for axis in self.order[:step]:
            at[axis] = None
        at[self.order[step]] = place
        return self.view(at)

    def start(self, step):
        axis, links = self.order[step], self.links
        mine = self.region(step, links.at[axis])
        self.coming[step] = []
        for k in range(1, links.sizes[axis]):
            slot = links.take()
            copy = links.copy(mine, mine, slot, axis, k)
            copy.start()
            self.sent.append(copy)
            lands = self.region(step, links.place(axis, links.sizes[axis] - k))
            self.coming[step].append(links.copy(lands, lands, slot, axis, k))

    def wait(self, step):
        for copy in self.coming[step]:
            copy.wait_recv()

    def go(self, step):
        self.wait(step)
        if step + 1 < len(self.order):
            self.start(step + 1)

    def close(self):
        for copy in self.sent:
            copy.wait_send()


def some(place):
    return slice(None) if place is None else place


def dot(a, b):
    return lax.dot_general(a, b, (((1,), (0,)), ((), ())), preferred_element_type=F32)


def dot_nt(a, b):
    return lax.dot_general(a, b, (((1,), (1,)), ((), ())), preferred_element_type=F32)


def dot_tn(a, b):
    return lax.dot_general(a, b, (((0,), (0,)), ((), ())), preferred_element_type=F32)


def normed(values):
    center = values - jnp.mean(values, axis=-1, keepdims=True)
    scale = lax.rsqrt(jnp.mean(center * center, axis=-1, keepdims=True) + LN_EPS)
    return center * scale, scale


def norm_back(up, hat, scale, gain):
    inner = up * gain
    return scale * (
        inner
        - jnp.mean(inner, axis=-1, keepdims=True)
        - hat * jnp.mean(inner * hat, axis=-1, keepdims=True)
    )


def fold(rows):
    return jnp.sum(rows.reshape(rows.shape[0] // 8, 8, rows.shape[1]), axis=0)


def gelu_and_slope(v):
    root = 0.7978845608028654
    square = v * v
    t = jnp.tanh(root * v * (1.0 + 0.044715 * square))
    half = 0.5 + 0.5 * t
    slope = half + (0.5 * root) * v * (1.0 - t * t) * (1.0 + (3.0 * 0.044715) * square)
    return v * half, slope


def diagonal(rows):
    n = GROUP // HEAD
    lat = rows.shape[0]
    tall = jnp.concatenate([rows] * n, axis=0)
    row = lax.broadcasted_iota(jnp.int32, tall.shape, 0) // lat
    col = lax.broadcasted_iota(jnp.int32, tall.shape, 1) // HEAD
    return jnp.where(row == col, tall, jnp.zeros_like(tall))


def undiagonal(tall):
    n = GROUP // HEAD
    lat = tall.shape[0] // n
    col = lax.broadcasted_iota(jnp.int32, (lat, GROUP), 1) // HEAD
    total = jnp.where(col == 0, tall[:lat], 0.0)
    for h in range(1, n):
        total = total + jnp.where(col == h, tall[h * lat : (h + 1) * lat], 0.0)
    return total


def weight_block(weights, m, g, sizes):
    block = weights.shape[-1]
    per = GROUP // block
    parts = []
    for s in range(per):
        h = g * per + s
        part = weights[m, lax.div(h, sizes["c"]), lax.rem(h, sizes["c"])]
        parts.append(part.reshape(D, block))
    return parts[0] if per == 1 else jnp.concatenate(parts, axis=1)


def softmax_columns(keys, spread_queries, seen):
    scores = dot_nt(keys, spread_queries)
    scores = jnp.where(seen, scores, -1e30)
    raised = jnp.exp(scores - jnp.max(scores, axis=0, keepdims=True))
    return raised * (1.0 / jnp.sum(raised, axis=0, keepdims=True))


def forward_kernel(
    sizes,
    att_ref,
    expand_ref,
    reduce_ref,
    tokens_ref,
    latents_ref,
    cotangent_ref,
    counts_ref,
    norm_ref,
    att_out,
    pairs_out,
    turned_out,
    queries_out,
    mixed_out,
    ff_grad_out,
    added_out,
    middle_out,
    middle_grad_out,
    branch_out,
    ff_norm_out,
    att,
    pairs,
    turned,
    queries,
    mixed,
    ff,
    added,
    middle,
    middle_grad,
    branch,
    ff_norm,
    rows,
    back,
    hid,
    bg,
    part,
    land_c,
    land_y,
    tokens,
    inputs,
    send,
    recv,
    local,
):
    links = Links(sizes, send, recv, local)
    links.greet()
    images, span, _ = inputs.shape
    patches = tokens_ref.shape[1]
    lat = span - patches
    at = links.at
    outs = []

    loads = {}

    def fetch(i):
        if i < images:
            loads[i] = links.move(tokens_ref.at[i], tokens.at[i % 2])

    fetch(0)
    fetch(1)
    for m in range(4):
        att[m, at["y"], at["c"], at["z"], at["x"]] = att_ref[m].astype(BF16)
    back[at["y"], at["c"]] = cotangent_ref[...].astype(BF16)
    quarters, tile = ff.shape[0], ff.shape[-1]
    for q in range(quarters):
        ff[q, 0, at["z"], at["x"]] = expand_ref[:, q * tile : (q + 1) * tile].astype(BF16)
        ff[q, 1, at["z"], at["x"]] = reduce_ref[q * tile : (q + 1) * tile].T.astype(BF16)

    half = att.shape[5] // 2

    def att_view(m, s):
        def view(p):
            return att.at[m, some(p["y"]), some(p["c"]), some(p["z"]), some(p["x"]), pl.ds(s * half, half)]

        return view

    def ff_view(q, m):
        def view(p):
            return ff.at[q, m, some(p["z"]), some(p["x"])]

        return view

    def back_view(p):
        return back.at[some(p["y"]), some(p["c"])]

    def row_view(i):
        def view(p):
            return rows.at[some(p["y"]), some(p["c"]), pl.ds(i * lat, lat)]

        return view

    query, key, value, output = ([Gather(links, "zxyc", att_view(m, s)) for s in range(2)] for m in range(4))
    hidden = [Gather(links, "zx", ff_view(q, m)) for q in range(quarters) for m in range(2)]
    cotangent = [Gather(links, "yc", back_view)]
    ff_rows = [Gather(links, "yc", row_view(i)) for i in range(images)]
    everything = [*query, *key, *value, *output, *hidden, *cotangent, *ff_rows]

    def start(parts):
        for part in parts:
            part.start(0)

    def go(parts, step):
        for part in parts:
            part.go(step)

    links.meet()
    start(key + value + hidden[:1] + query + hidden[1:2] + output)

    for i in range(images):
        low = normed(latents_ref[pl.ds(i * lat, lat)].astype(F32))[0] * norm_ref[2:3] + norm_ref[3:4]
        inputs[i, pl.ds(patches, lat)] = low.astype(BF16)

    def normalize(i):
        loads[i].wait()
        some_rows = 64

        def one(t, _):
            part = pl.ds(pl.multiple_of(t * some_rows, some_rows), some_rows)
            low = normed(tokens[i % 2, part].astype(F32))[0] * norm_ref[0:1] + norm_ref[1:2]
            inputs[i, part] = low.astype(BF16)
            return 0

        lax.fori_loop(0, patches // some_rows, one, 0)
        fetch(i + 2)

    turning = {}

    def turn(i):
        if i >= 2:
            turning[i - 2].wait()

        def one(t, _):
            part = pl.ds(pl.multiple_of(t * 128, 128), 128)
            turned[i % 2, :, part] = inputs[i, part].T
            return 0

        lax.fori_loop(0, span // 128, one, 0)
        turning[i] = links.move(turned.at[i % 2], turned_out.at[:, pl.ds(i * span, span)])

    k0, k1, v0, v1, q0, q1, o0, o1 = *key, *value, *query, *output
    f = [*hidden, *[None] * (8 - len(hidden))]
    steps = []

    def plan(*ticks):
        steps.extend(ticks)

    plan(
        [(k0, 0)],
        [(k1, 0)],
        [(k0, 1), (v0, 0)],
        [(k1, 1), (v1, 0)],
        [(v0, 1)],
        [(k0, 2), (v1, 1)],
        [(f[0], 0)],
        [(k1, 2), (q0, 0)],
    )

    def tick():
        for part, step in steps.pop(0) if steps else ():
            if part is not None:
                part.go(step)
            if part in hidden:
                start(hidden[hidden.index(part) + 2 :][:1])

    def rest():
        while steps:
            tick()

    for i in range(images):
        normalize(i)
        tick()
        turn(i)
        tick()
    plan([(q1, 0), (v0, 2), (q0, 1)])
    rest()
    for i in range(max(0, images - 2), images):
        turning[i].wait()
    go(key, 3)

    def project(i, m):
        def one(g, _):
            weight = weight_block(att, m, g, sizes)
            pairs[i, (m - 1) * GROUPS + g] = dot(inputs[i], weight).astype(BF16)
            return 0

        lax.fori_loop(0, GROUPS, one, 0)

    def attend(i):
        position = lax.broadcasted_iota(jnp.int32, (span, GROUP), 0)
        count = counts_ref[links.head * images + i]
        seen = (position < count) | (position >= patches)

        def one(g, _):
            spread = diagonal(queries[g, pl.ds(i * lat, lat)])
            probs = softmax_columns(pairs[i, g], spread, seen).astype(BF16)
            wide = dot_tn(probs, pairs[i, GROUPS + g])
            mixed[g, pl.ds(i * lat, lat)] = undiagonal(wide).astype(BF16)
            return 0

        lax.fori_loop(0, GROUPS, one, 0)

    def finish(i):
        part = pl.ds(i * lat, lat)
        whole = jnp.concatenate([mixed[g, part] for g in range(GROUPS)], axis=1)
        made = jnp.concatenate(
            [dot(whole, weight_block(att, 3, g, sizes)) for g in range(GROUPS)], axis=1
        )
        value = latents_ref[part].astype(F32) + made
        middle[part] = value
        low = normed(value)[0] * norm_ref[4:5] + norm_ref[5:6]
        rows[at["y"], at["c"], part] = low.astype(BF16)
        ff_rows[i].start(0)

    plan([], [(q1, 1)], [(f[1], 0)], [(v1, 2)])
    for i in range(images):
        project(i, 1)
        tick()
    plan([(o0, 0), (q0, 2), (o1, 0)])
    rest()
    go(value, 3)
    plan([(o0, 1)], [(q1, 2)], [(f[2], 0), (o1, 1)], [(f[3], 0)])
    for i in range(images):
        project(i, 2)
        outs.append(links.move(pairs.at[i], pairs_out.at[i]))
        tick()
    plan([(o0, 2)])
    rest()
    go(query, 3)
    stack = inputs[:, patches:].reshape(images * lat, D)
    for g in range(GROUPS):
        made = dot(stack, weight_block(att, 0, g, sizes)) * HEAD ** (-0.5)
        queries[g] = made.astype(BF16)
    outs.append(links.move(queries, queries_out))
    plan([(f[4], 0)], [(o1, 2)], [(f[5], 0)])
    for i in range(images):
        attend(i)
        tick()
        if i == 0:
            start(cotangent)
    rest()
    go(output, 3)
    outs.append(links.move(att, att_out))
    outs.append(links.move(mixed, mixed_out))
    plan([], [(f[6], 0)], [(cotangent[0], 0)], [(f[7], 0)])
    for i in range(images):
        finish(i)
        tick()
    rest()
    outs.append(links.move(middle, middle_out))
    go(cotangent, 1)
    go(ff_rows, 0)
    n = images * lat
    cs, ys, zs = (sizes[a] for a in "cyz")
    sib = links.place("c", 1)
    xr = sizes["x"] * att.shape[5]

    def first(q):
        def one(yi, _):
            before = dot(rows[yi].reshape(cs * n, D), ff[q, 0].reshape(D, tile))
            up = dot(back[yi].reshape(cs * n, D), ff[q, 1].reshape(D, tile))
            made, slope = gelu_and_slope(before)
            hid[yi, :, :, q * tile : (q + 1) * tile] = made.astype(BF16).reshape(cs, n, tile)
            bg[yi, :, :, q * tile : (q + 1) * tile] = (up * slope).astype(BF16).reshape(cs, n, tile)
            return 0

        lax.fori_loop(0, ys, one, 0)

    go(ff_rows, 1)
    for q in range(quarters):
        go(hidden[2 * q : 2 * q + 2], 1)
        first(q)

    ff_block = quarters * tile

    def second(kind, yi):
        wide = (hid if kind else bg)[yi].reshape(cs * n, ff_block)
        made = added if kind else part

        def one(z, _):
            cols = pl.ds(pl.multiple_of(z * xr, xr), xr)
            weight = jnp.concatenate([ff[q, kind, z].reshape(xr, tile) for q in range(quarters)], axis=1)
            made[yi, :, :, cols] = dot_nt(wide, weight).astype(BF16).reshape(cs, n, xr)
            return 0

        lax.fori_loop(0, zs, one, 0)

    sent, chip, along = [], {}, {}
    for k in [*range(1, ys), 0]:
        yi = links.place("y", k)
        second(0, yi)
        slot = links.take()
        land = land_c.at[yi]
        copy = links.copy(part.at[yi, sib], land, slot, "c", 1)
        copy.start()
        sent.append(copy)
        chip[k] = links.copy(land, land, slot, "c", 1)
    for k in range(1, ys):
        yi = links.place("y", k)
        chip[k].wait_recv()
        summed = part[yi, at["c"]].astype(F32) + land_c[yi].astype(F32)
        part[yi, at["c"]] = summed.astype(BF16)
        slot = links.take()
        land = land_y.at[k - 1]
        copy = links.copy(part.at[yi, at["c"]], land, slot, "y", k)
        copy.start()
        sent.append(copy)
        along[k] = links.copy(land, land, slot, "y", k)
    for yi in range(ys):
        second(1, yi)
    outs.append(links.move(added, added_out))
    for gather in hidden:
        gather.close()

    for m, (left, right) in ((1, (back, hid)), (0, (rows, bg))):

        def one(z, _):
            cols = pl.ds(pl.multiple_of(z * xr, xr), xr)
            made = dot_tn(
                left[:, :, :, cols].reshape(ys * cs * n, xr), right[...].reshape(ys * cs * n, ff_block)
            ).astype(BF16)
            for q in range(quarters):
                ff[q, m, z] = made[:, q * tile : (q + 1) * tile].reshape(*ff.shape[3:5], tile)
            return 0

        lax.fori_loop(0, zs, one, 0)
    outs.append(links.move(ff, ff_grad_out))
    chip[0].wait_recv()
    for k in range(1, ys):
        along[k].wait_recv()

    def back_one(t, carry):
        gain, shift = carry
        rws = pl.ds(pl.multiple_of(t * lat, lat), lat)
        up = part[at["y"], at["c"], rws].astype(F32) + land_c[at["y"], rws].astype(F32)
        for k in range(1, ys):
            up = up + land_y[k - 1, rws].astype(F32)
        hat, scale = normed(middle[rws])
        value = cotangent_ref[rws] + norm_back(up, hat, scale, norm_ref[4:5])
        middle_grad[rws] = value
        branch[rws] = value.astype(BF16)
        return gain + fold(up * hat), shift + fold(up)

    zero = jnp.zeros((8, D), F32)
    ff_norm[0], ff_norm[1] = lax.fori_loop(0, images, back_one, (zero, zero))
    outs.append(links.move(middle_grad, middle_grad_out))
    outs.append(links.move(branch, branch_out))
    outs.append(links.move(ff_norm, ff_norm_out))
    for copy in sent:
        copy.wait_send()
    for gather in everything:
        if gather not in hidden:
            gather.close()
    for out in outs:
        out.wait()


def forward(att, expand, reduce, tokens, latents, cotangent, counts, norm_params):
    sizes = grid_of(lax.axis_size("dp"), lax.axis_size("head"))
    z, x, y, c = (sizes[a] for a in "zxyc")
    images, patches, _ = tokens.shape
    lat = latents.shape[1]
    span = patches + lat
    n = images * lat
    _, row_block, col_block = att.shape
    ff_block = expand.shape[1]
    tile = min(GROUP, ff_block)
    quarters = ff_block // tile
    shapes = dict(
        att=((4, y, c, z, x, row_block, col_block), BF16),
        pairs=((images, 2 * GROUPS, span, GROUP), BF16),
        turned=((D, images * span), BF16),
        queries=((GROUPS, n, GROUP), BF16),
        mixed=((GROUPS, n, GROUP), BF16),
        ff=((quarters, 2, z, x, row_block, tile), BF16),
        added=((y, c, n, D), BF16),
        middle=((n, D), F32),
        middle_grad=((n, D), F32),
        branch=((n, D), BF16),
        ff_norm=((2, 8, D), F32),
    )
    held = dict(shapes)
    held.update(turned=((2, D, span), BF16))
    inside = [
        ((y, c, n, D), BF16),
        ((y, c, n, D), BF16),
        ((y, c, n, ff_block), BF16),
        ((y, c, n, ff_block), BF16),
        ((y, c, n, D), BF16),
        ((y, n, D), BF16),
        ((y - 1, n, D), BF16),
        ((2, patches, D), BF16),
        ((images, span, D), BF16),
    ]
    per_att = sum(s - 1 for s in sizes.values())
    slots = 8 * per_att + 8 * (z + x - 2) + (1 + images) * (y + c - 2) + 2 * y
    vmem, anywhere = pl.BlockSpec(memory_space=pltpu.VMEM), pl.BlockSpec(memory_space=pl.ANY)
    made = pl.pallas_call(
        functools.partial(forward_kernel, sizes),
        out_shape=[jax.ShapeDtypeStruct(*v) for v in shapes.values()],
        in_specs=[vmem, vmem, vmem, anywhere, vmem, vmem, pl.BlockSpec(memory_space=pltpu.SMEM), vmem],
        out_specs=[anywhere] * len(shapes),
        scratch_shapes=[pltpu.VMEM(*v) for v in [*held.values(), *inside]]
        + [
            pltpu.SemaphoreType.DMA((slots,)),
            pltpu.SemaphoreType.DMA((slots,)),
            pltpu.SemaphoreType.DMA((2 * images + 20,)),
        ],
        compiler_params=pltpu.CompilerParams(
            collective_id=0, has_side_effects=True, vmem_limit_bytes=63 * MIB + 900 * 1024
        ),
        name="gather_and_attend",
    )(att, expand, reduce, tokens, latents.reshape(n, D), cotangent.reshape(n, D), counts, norm_params)
    return SimpleNamespace(**dict(zip(shapes, made)))


class Scatter:
    def __init__(self, links, order, view, lands):
        self.links, self.order, self.view, self.lands = links, order, view, lands
        self.slots = {}

    def region(self, step, place):
        at = dict(self.links.at)
        for axis in self.order[step + 1 :]:
            at[axis] = None
        at[self.order[step]] = place
        return self.view(at)

    def copies(self, step):
        axis, links = self.order[step], self.links
        for k, slot in enumerate(self.slots[step], 1):
            yield links.copy(self.region(step, links.place(axis, k)), self.lands[step][k - 1], slot, axis, k)

    def start(self, step):
        self.slots[step] = [self.links.take() for _ in range(1, self.links.sizes[self.order[step]])]
        for copy in self.copies(step):
            copy.start()

    def wait(self, step):
        for k, slot in enumerate(self.slots[step], 1):
            land = self.lands[step][k - 1]
            self.links.copy(land, land, slot, self.order[step], k).wait_recv()

    def add(self, step, out=None):
        mine = self.region(step, self.links.at[self.order[step]])
        lands = self.lands[step]
        lead = mine.shape[0] if len(mine.shape) > 2 else None

        def total(at):
            value = mine[at].astype(F32)
            for land in lands:
                value = value + land[at].astype(F32)
            return value

        if out is not None:
            out[...] = total(Ellipsis)
        elif lead is None:
            mine[...] = total(Ellipsis).astype(BF16)
        else:

            def one(t, _):
                mine[t] = total(t).astype(BF16)
                return 0

            lax.fori_loop(0, lead, one, 0)

    def go(self, step, out=None):
        self.wait(step)
        self.add(step, out)
        if step + 1 < len(self.order):
            self.start(step + 1)

    def close(self):
        for step in self.slots:
            for copy in self.copies(step):
                copy.wait_send()


ATT_ORDERS = {0: ("yxz", "yxz"), 1: ("yxz", "xyz"), 2: ("yxz", "yxz"), 3: ("yxz", "yxz")}


def land_shapes(sizes, order, axes, tail):
    shapes, left = [], list(axes)
    for axis in order:
        left.remove(axis)
        shapes.append((sizes[axis] - 1, *(sizes[a] for a in left), *tail))
    return shapes


def backward_kernel(sizes, dims, *refs):
    names, keys, images, patches, lat, ff_block = dims
    r = SimpleNamespace(**dict(zip(names, refs)))
    total_lands = dict(zip("cyxz", refs[len(names) :]))
    att_lands = dict(zip(keys, refs[len(names) + 4 :]))
    links = Links(sizes, r.send, r.recv, r.local)
    links.greet()
    at = links.at
    sib = links.place("c", 1)
    n = images * lat
    span = patches + lat
    zs, xs, ys, cs = (sizes[a] for a in "zxyc")
    row_block, col_block = r.att_share.shape[1:]
    xr = xs * row_block
    heads = ys * cs
    half = row_block // 2
    norm_ref, latents = r.norm, r.latents
    queries, mixed = r.queries, r.mixed
    grads_ff = r.grads_ff
    middle_grad, branch, latent_low = r.middle_grad, r.branch, r.latent_low
    mixed_grad, query_back = r.mixed_grad, r.query_back
    outs = []

    units = [(m, k) for k in [*range(1, zs), 0] for m in (1, 0)]
    x_slots = {unit: [links.take() for _ in range(1, xs)] for unit in units}
    z_slots = {unit: links.take() for unit in units if unit[1]}

    def x_copies(unit):
        m, k = unit
        z = links.place("z", k)
        for j, slot in enumerate(x_slots[unit], 1):
            yield links.copy(
                grads_ff.at[:, m, z, links.place("x", j)], r.ff_land_x.at[m, z, j - 1], slot, "x", j
            )

    def z_copy(unit):
        m, k = unit
        return links.copy(
            grads_ff.at[:, m, links.place("z", k), at["x"]], r.ff_land_z.at[m, k - 1], z_slots[unit], "z", k
        )

    quarters, tile = grads_ff.shape[0], grads_ff.shape[-1]

    def ff_along(unit):
        m, k = unit
        z = links.place("z", k)
        for copy in x_copies(unit):
            copy.wait_recv()
        for q in range(quarters):
            total = grads_ff[q, m, z, at["x"]].astype(F32)
            for j in range(xs - 1):
                total = total + r.ff_land_x[m, z, j, q].astype(F32)
            if k:
                grads_ff[q, m, z, at["x"]] = total.astype(BF16)
            else:
                r.ff_share[m, :, q * tile : (q + 1) * tile] = total
        if k:
            z_copy(unit).start()

    def ff_finish():
        for m in range(2):
            for k in range(1, zs):
                z_copy((m, k)).wait_recv()
            for q in range(quarters):
                cols = pl.ds(q * tile, tile)
                total = r.ff_share[m, :, cols]
                for k in range(1, zs):
                    total = total + r.ff_land_z[m, k - 1, q].astype(F32)
                r.ff_share[m, :, cols] = total

    pairs = r.pairs_here
    early = [links.move(r.pairs.at[i], pairs.at[i]) for i in range(images)]

    load = links.move(r.ff_grad, grads_ff)
    own = links.move(r.added.at[:, at["c"]], r.added_here)
    links.meet()
    load.wait()
    for unit in units:
        for copy in x_copies(unit):
            copy.start()

    c_slots = [links.take() for _ in range(ys)]
    y_slots = [links.take() for _ in range(1, ys)]

    def added_chip(k):
        yi = links.place("y", k)
        return links.copy(r.added.at[yi, sib], r.added_land_c.at[yi], c_slots[k], "c", 1)

    def added_along(k):
        return links.copy(r.added_here.at[links.place("y", k)], r.added_land_y.at[k - 1], y_slots[k - 1], "y", k)

    for k in range(ys):
        added_chip(k).start()
    own.wait()

    def added_out():
        for k in range(1, ys):
            yi = links.place("y", k)
            added_chip(k).wait_recv()
            summed = r.added_here[yi].astype(F32) + r.added_land_c[yi].astype(F32)
            r.added_here[yi] = summed.astype(BF16)
            added_along(k).start()

    def added_finish():
        added_chip(0).wait_recv()
        for k in range(1, ys):
            added_along(k).wait_recv()

        def one(t, _):
            rws = pl.ds(pl.multiple_of(t * lat, lat), lat)
            up = r.added_here[at["y"], rws].astype(F32) + r.added_land_c[at["y"], rws].astype(F32)
            for k in range(1, ys):
                up = up + r.added_land_y[k - 1, rws].astype(F32)
            latent_low[rws] = (r.middle[rws] + up).astype(BF16)
            return 0

        lax.fori_loop(0, images, one, 0)
        for k in range(ys):
            added_chip(k).wait_send()
        for k in range(1, ys):
            added_along(k).wait_send()
        return links.move(latent_low, r.resampled)

    r.norm_parts[4] = r.ff_norm[0]
    r.norm_parts[5] = r.ff_norm[1]

    steps = []

    def tick():
        if steps:
            steps.pop(0)()

    def later(f, *args):
        steps.append(lambda: f(*args))

    def attention(grads, turned_left):
        per = GROUP // col_block
        block_slots = {m: [links.take() for _ in range(ys)] for m in range(4)}

        def block_copy(m, yi):
            slot = block_slots[m][0] + yi
            return links.copy(grads.at[m, yi, sib], r.att_land_c.at[m, yi], slot, "c", 1)

        def att_scatter(m, s):
            def view(p):
                return grads.at[m, some(p["y"]), at["c"], some(p["z"]), some(p["x"]), pl.ds(s * half, half)]

            order = ATT_ORDERS[m][s]
            lands = [
                [att_lands[m, s, step].at[k] for k in range(sizes[axis] - 1)]
                for step, axis in enumerate(order)
            ]
            return Scatter(links, order, view, lands)

        scatter = {m: [att_scatter(m, s) for s in range(2)] for m in range(4)}

        def go(m, step):
            for s, part in enumerate(scatter[m]):
                part.go(step, r.att_share.at[m, pl.ds(s * half, half)] if step == 2 else None)

        def chip_sum(m):
            for yi in range(ys):
                block_copy(m, yi).wait_recv()

                def one(z, _):
                    value = grads[m, yi, at["c"], z].astype(F32) + r.att_land_c[m, yi, z].astype(F32)
                    grads[m, yi, at["c"], z] = value.astype(BF16)
                    return 0

                lax.fori_loop(0, zs, one, 0)
            for part in scatter[m]:
                part.start(0)

        def products(m, left, right, between=None):
            def of(ci, send):
                def one(yi, _):
                    made = dot(left(), right(yi * cs + ci)).astype(BF16)
                    grads[m, yi, ci] = made.reshape(zs, xs, row_block, col_block)
                    if send:
                        block_copy(m, yi).start()
                    return 0

                lax.fori_loop(0, ys, one, 0)

            of(sib, True)
            if between is not None:
                between()
            of(at["c"], False)

        def query_columns(h):
            j = lax.div(h * col_block, GROUP)
            if per == 1:
                return query_back[j]
            off = pl.multiple_of(lax.rem(h, per) * col_block, col_block)
            return query_back[j, :, pl.ds(off, col_block)]

        def columns(m):
            def right(h):
                j = lax.div(h * col_block, GROUP) + (m - 1) * GROUPS
                if per == 1:
                    return pairs[:, j].reshape(images * span, GROUP)
                off = pl.multiple_of(lax.rem(h, per) * col_block, col_block)
                return pairs[:, j, :, pl.ds(off, col_block)].reshape(images * span, col_block)

            return right

        def attend(i):
            position = lax.broadcasted_iota(jnp.int32, (span, GROUP), 0)
            count = r.counts[links.head * images + i]
            seen = (position < count) | (position >= patches)
            rws = pl.ds(i * lat, lat)

            def one(g, _):
                keys, values = pairs[i, g], pairs[i, GROUPS + g]
                spread = diagonal(queries[g, rws])
                probs = softmax_columns(keys, spread, seen)
                upstream = diagonal(mixed_grad[g, rws])
                prob_grad = dot_nt(values, upstream)
                inner = jnp.sum(probs * prob_grad, axis=0, keepdims=True)
                score_grad = (probs * (prob_grad - inner)).astype(BF16)
                back = undiagonal(dot_tn(score_grad, keys)) * HEAD ** (-0.5)
                query_back[g, rws] = back.astype(BF16)
                pairs[i, GROUPS + g] = dot(probs.astype(BF16), upstream).astype(BF16)
                pairs[i, g] = dot(score_grad, spread).astype(BF16)
                return 0

            lax.fori_loop(0, GROUPS, one, 0)

        def weights(turned, weight):
            load_weight = links.move(r.att.at[3], weight)
            load_turned = links.move(r.turned, turned)
            for g in range(GROUPS):
                turned_left[pl.ds(g * GROUP, GROUP)] = mixed[g].T
            products(
                3,
                lambda: turned_left[...],
                lambda h: branch[:, pl.ds(pl.multiple_of(h * col_block, col_block), col_block)],
            )
            load_weight.wait()
            for g in range(GROUPS):
                first = g * GROUP // row_block
                wide = []
                for h in range(heads):
                    blocks = [
                        weight[h // cs, h % cs, b // xs, b % xs] for b in range(first, first + GROUP // row_block)
                    ]
                    wide.append(jnp.concatenate(blocks, axis=0))
                mixed_grad[g] = dot_nt(branch[...], jnp.concatenate(wide, axis=1)).astype(BF16)
            ff_steps = [lambda u=u: ff_along(u) for u in units]
            steps.append(lambda: (chip_sum(3), ff_steps[0](), added_out()))
            steps.extend(ff_steps[1:])
            for i in range(images):
                attend(i)
                tick()
            load_turned.wait()
            for i in range(images):
                turned_left[:, pl.ds(i * lat, lat)] = turned[:, i * span + patches : (i + 1) * span]
            products(0, lambda: turned_left[...], query_columns)
            resampled = added_finish()
            steps.insert(0, lambda: go(3, 0))
            steps.insert(2, lambda: chip_sum(0))
            tick()
            products(2, lambda: turned[...], columns(2), tick)
            steps.insert(1, lambda: chip_sum(2))
            tick()
            products(1, lambda: turned[...], columns(1), tick)
            tick()
            resampled.wait()

        pl.run_scoped(
            weights,
            pltpu.VMEM((D, images * span), BF16),
            pltpu.VMEM((ys, cs, zs, xs, row_block, col_block), BF16),
        )

        def inputs(att, tokens, pair_grad):
            weight_loads = [links.move(r.att.at[m], att.at[m]) for m in (1, 2, 0)]
            loads = {}

            def fetch(i):
                loads[i] = links.move(r.tokens.at[i], tokens.at[i % 2])

            media_out = {}
            fetch(0)
            tick()
            steps.insert(0, lambda: chip_sum(1))
            for m, step in ((3, 1), (0, 0), (2, 0), (1, 0), (3, 2), (0, 1), (2, 1), (1, 1), (0, 2), (2, 2)):
                later(go, m, step)
            zero = jnp.zeros((8, D), F32)
            sums = (zero, zero, zero, zero)
            for load in weight_loads:
                load.wait()
            for i in range(images):
                stacked = jnp.concatenate([pairs[i, j] for j in range(2 * GROUPS)], axis=1)
                asked = jnp.concatenate([query_back[g, pl.ds(i * lat, lat)] for g in range(GROUPS)], axis=1)

                def one(z, _):
                    cols = pl.ds(pl.multiple_of(z * xr, xr), xr)
                    wide = jnp.concatenate(
                        [att[m, h // cs, h % cs, z].reshape(xr, col_block) for m in (1, 2) for h in range(heads)], axis=1
                    )
                    narrow = jnp.concatenate(
                        [att[0, h // cs, h % cs, z].reshape(xr, col_block) for h in range(heads)], axis=1
                    )
                    pair_grad[:, cols] = dot_nt(stacked, wide)
                    pair_grad[patches:, cols] += dot_nt(asked, narrow)
                    return 0

                lax.fori_loop(0, zs, one, 0)
                tick()
                tick()
                if i + 1 < images:
                    if i >= 1:
                        media_out[i - 1].wait()
                    fetch(i + 1)
                loads[i].wait()
                slot = i % 2
                tile = 64

                def media(t, carry):
                    gain, shift = carry
                    rws = pl.ds(pl.multiple_of(t * tile, tile), tile)
                    hat, scale = normed(tokens[slot, rws].astype(F32))
                    up = pair_grad[rws]
                    tokens[slot, rws] = norm_back(up, hat, scale, norm_ref[0:1]).astype(BF16)
                    return gain + fold(up * hat), shift + fold(up)

                gain, shift = lax.fori_loop(0, patches // tile, media, (sums[0], sums[1]))
                media_out[i] = links.move(tokens.at[slot], r.media_grad.at[i])
                rws = pl.ds(i * lat, lat)
                hat, scale = normed(latents[rws].astype(F32))
                up = pair_grad[patches:]
                made = middle_grad[rws] + norm_back(up, hat, scale, norm_ref[2:3])
                latent_low[rws] = made.astype(BF16)
                sums = (gain, shift, sums[2] + fold(up * hat), sums[3] + fold(up))
                tick()
                tick()
            for k, value in enumerate(sums):
                r.norm_parts[k] = value
            for i in range(max(0, images - 2), images):
                media_out[i].wait()

        pl.run_scoped(
            inputs,
            pltpu.VMEM((3, ys, cs, zs, xs, row_block, col_block), BF16),
            pltpu.VMEM((2, patches, D), BF16),
            pltpu.VMEM((span, D), F32),
        )
        while steps:
            tick()
        go(1, 2)
        ff_finish()
        for m in range(4):
            for yi in range(ys):
                block_copy(m, yi).wait_send()
            for part in scatter[m]:
                part.close()
        for unit in units:
            for copy in x_copies(unit):
                copy.wait_send()
            if unit[1]:
                z_copy(unit).wait_send()

    for load in early:
        load.wait()
    pl.run_scoped(
        attention,
        pltpu.VMEM((4, ys, cs, zs, xs, row_block, col_block), BF16),
        pltpu.VMEM((D, n), BF16),
    )

    outs.append(links.move(latent_low, r.latent_grad))
    squares = jnp.sum(r.att_share[...] * r.att_share[...]) + jnp.sum(r.ff_share[...] * r.ff_share[...])
    rows = [jnp.sum(r.norm_parts[k], axis=0, keepdims=True) for k in range(6)]
    value = jnp.concatenate([*rows, jnp.full((2, D), squares, F32)], axis=0)
    last = []
    for axis in "cyxz":
        lands = total_lands[axis]
        lands[at[axis]] = value
        coming = []
        for k in range(1, sizes[axis]):
            slot = links.take()
            mine = lands.at[at[axis]]
            copy = links.copy(mine, mine, slot, axis, k)
            copy.start()
            last.append(copy)
            land = lands.at[links.place(axis, sizes[axis] - k)]
            coming.append(links.copy(land, land, slot, axis, k))
        for copy in coming:
            copy.wait_recv()
        value = lands[0]
        for k in range(1, sizes[axis]):
            value = value + lands[k]
    r.totals[...] = value
    for copy in last:
        copy.wait_send()
    for out in outs:
        out.wait()


def backward(got, tokens, latents, counts, norm_params, row_block, col_block, ff_block):
    sizes = grid_of(lax.axis_size("dp"), lax.axis_size("head"))
    zs, xs, ys, cs = (sizes[a] for a in "zxyc")
    images, patches, _ = tokens.shape
    lat = latents.shape[1]
    n = images * lat
    half = row_block // 2
    vmem, anywhere = pl.BlockSpec(memory_space=pltpu.VMEM), pl.BlockSpec(memory_space=pl.ANY)
    smem = pl.BlockSpec(memory_space=pltpu.SMEM)
    inputs = dict(
        att=(got.att, anywhere),
        ff_grad=(got.ff, anywhere),
        added=(got.added, anywhere),
        middle=(got.middle, vmem),
        pairs=(got.pairs, anywhere),
        turned=(got.turned, anywhere),
        tokens=(tokens, anywhere),
        queries=(got.queries, vmem),
        mixed=(got.mixed, vmem),
        middle_grad=(got.middle_grad, vmem),
        branch=(got.branch, vmem),
        ff_norm=(got.ff_norm, vmem),
        latents=(latents.reshape(n, D), vmem),
        norm=(norm_params, vmem),
        counts=(counts, smem),
    )
    outputs = dict(
        resampled=((n, D), BF16, anywhere),
        media_grad=((images, patches, D), BF16, anywhere),
        latent_grad=((n, D), BF16, anywhere),
        att_share=((4, row_block, col_block), F32, vmem),
        ff_share=((2, row_block, ff_block), F32, vmem),
        totals=((8, D), F32, vmem),
    )
    scratch = dict(
        grads_ff=(got.ff.shape, BF16),
        ff_land_x=((2, zs, xs - 1, got.ff.shape[0], row_block, got.ff.shape[-1]), BF16),
        ff_land_z=((2, zs - 1, got.ff.shape[0], row_block, got.ff.shape[-1]), BF16),
        added_here=((ys, n, D), BF16),
        added_land_c=((ys, n, D), BF16),
        added_land_y=((ys - 1, n, D), BF16),
        att_land_c=((4, ys, zs, xs, row_block, col_block), BF16),
        pairs_here=(got.pairs.shape, BF16),
        latent_low=((n, D), BF16),
        mixed_grad=((GROUPS, n, GROUP), BF16),
        query_back=((GROUPS, n, GROUP), BF16),
        norm_parts=((6, 8, D), F32),
    )
    totals = [((sizes[axis], 8, D), F32) for axis in "cyxz"]
    lands = {}
    for m, orders in ATT_ORDERS.items():
        for s, order in enumerate(orders):
            for step, shape in enumerate(land_shapes(sizes, order, "yzx", (half, col_block))):
                lands[m, s, step] = (shape, BF16)
    steps = sum(v - 1 for v in sizes.values())
    slots = 9 * steps + 2 * (zs * xs + zs) + 6 * ys
    semaphores = dict(send=slots, recv=slots, local=3 * images + 30)
    names = [*inputs, *outputs, *semaphores, *scratch]
    made = pl.pallas_call(
        functools.partial(backward_kernel, sizes, (names, tuple(lands), images, patches, lat, ff_block)),
        out_shape=[jax.ShapeDtypeStruct(shape, dtype) for shape, dtype, _ in outputs.values()],
        in_specs=[spec for _, spec in inputs.values()],
        out_specs=[spec for _, _, spec in outputs.values()],
        scratch_shapes=[pltpu.SemaphoreType.DMA((v,)) for v in semaphores.values()]
        + [pltpu.VMEM(*v) for v in [*scratch.values(), *totals, *lands.values()]],
        compiler_params=pltpu.CompilerParams(
            collective_id=1, has_side_effects=True, vmem_limit_bytes=63 * MIB + 900 * 1024
        ),
        name="backward_and_scatter",
    )(*(value for value, _ in inputs.values()))
    return SimpleNamespace(**dict(zip(outputs, made)))


def adam_step(master, first, second, gradient, step_rate, decay_rate):
    first_new = BETA_ONE * first + (1.0 - BETA_ONE) * gradient
    second_new = BETA_TWO * second + (1.0 - BETA_TWO) * gradient * gradient
    first_hat = first_new / (1.0 - BETA_ONE**STEP)
    second_hat = second_new / (1.0 - BETA_TWO**STEP)
    master_new = master - step_rate * (
        first_hat / (jnp.sqrt(second_hat) + ADAM_EPS) + decay_rate * master
    )
    return (master_new, first_new, second_new)


def update_kernel(cuts, *refs):
    shares, refs = refs[:4], refs[4:]
    att, expand, reduce, norm, refs = refs[:3], refs[3:6], refs[6:9], refs[9:12], refs[12:]
    carried, refs = refs[:3], refs[3:]
    att_out, expand_out, reduce_out, norm_out, refs = refs[:3], refs[3:6], refs[6:9], refs[9:12], refs[12:]
    size_out, carried_out = refs[0], refs[1:4]
    att_share, expand_share, reduce_share, totals = shares
    step = pl.program_id(0)
    for a, b in zip(carried, carried_out):
        b[...] = a[...]
    norm_total = totals[:6]
    squares = totals[6:7, :1] + jnp.sum(norm_total * norm_total).reshape(1, 1)
    size = jnp.sqrt(squares)
    clip = jnp.minimum(1.0, MAX_NORM / (size + 1e-06))

    def write(outs, values):
        for out, value in zip(outs, values):
            out[...] = value

    write(att_out, adam_step(*(v[...] for v in att), att_share[...] * clip[None], MATRIX_RATE, DECAY_RATE))
    write(expand_out, adam_step(*(v[...] for v in expand), expand_share[0] * clip, MATRIX_RATE, DECAY_RATE))
    write(reduce_out, adam_step(*(v[...] for v in reduce), reduce_share[0].T * clip, MATRIX_RATE, DECAY_RATE))

    @pl.when(step == cuts - 1)
    def _():
        size_out[...] = size
        write(norm_out, adam_step(*(v[...] for v in norm), norm_total * clip, NORM_RATE, 0.0))


def update(back, attention, expand, reduce, norm):
    cuts = 4
    _, row_block, col_block = attention[0].shape
    ff_block = expand[0].shape[1]
    att_spec = pl.BlockSpec((1, row_block, col_block), lambda j: (j, 0, 0))
    expand_spec = pl.BlockSpec((row_block // cuts, ff_block), lambda j: (j, 0))
    reduce_spec = pl.BlockSpec((ff_block // cuts, row_block), lambda j: (j, 0))
    norm_spec = pl.BlockSpec(norm[0].shape, lambda j: (0, 0))
    shapes = [*attention, *expand, *reduce, *norm]
    specs = [att_spec] * 3 + [expand_spec] * 3 + [reduce_spec] * 3 + [norm_spec] * 3
    carried = [back.resampled, back.media_grad.reshape(-1, D), back.latent_grad]
    carried_specs = [pl.BlockSpec((v.shape[0] // cuts, D), lambda j: (j, 0)) for v in carried]
    out_shape = [jax.ShapeDtypeStruct(v.shape, v.dtype) for v in shapes]
    out_shape += [jax.ShapeDtypeStruct((1, 1), F32)]
    out_shape += [jax.ShapeDtypeStruct(v.shape, v.dtype) for v in carried]
    made = pl.pallas_call(
        functools.partial(update_kernel, cuts),
        grid=(cuts,),
        out_shape=out_shape,
        in_specs=[
            att_spec,
            pl.BlockSpec((1, row_block // cuts, ff_block), lambda j: (0, j, 0)),
            pl.BlockSpec((1, row_block, ff_block // cuts), lambda j: (1, 0, j)),
            pl.BlockSpec((8, D), lambda j: (0, 0)),
            *specs,
            *carried_specs,
        ],
        out_specs=[*specs, pl.BlockSpec((1, 1), lambda j: (0, 0)), *carried_specs],
        compiler_params=pltpu.CompilerParams(vmem_limit_bytes=63 * MIB),
        name="update_kernel",
    )(back.att_share, back.ff_share, back.ff_share, back.totals, *shapes, *carried)
    return made[:12], made[12], made[13:]


def on_device(
    media_tokens,
    latents,
    cotangent,
    counts,
    attention_weights,
    attention_first,
    attention_second,
    expand_weight,
    expand_first,
    expand_second,
    reduce_weight,
    reduce_first,
    reduce_second,
    norm_params,
    norm_first,
    norm_second,
):
    _, row_block, col_block = attention_weights.shape
    got = forward(
        attention_weights,
        expand_weight,
        reduce_weight,
        media_tokens,
        latents,
        cotangent,
        counts,
        norm_params,
    )
    back = backward(
        got, media_tokens, latents, counts, norm_params, row_block, col_block, expand_weight.shape[1]
    )
    made, size, (resampled, media_grad, latent_grad) = update(
        back,
        (attention_weights, attention_first, attention_second),
        (expand_weight, expand_first, expand_second),
        (reduce_weight, reduce_first, reduce_second),
        (norm_params, norm_first, norm_second),
    )
    return (
        resampled.reshape(latents.shape),
        media_grad.reshape(media_tokens.shape),
        latent_grad.reshape(latents.shape),
        size.reshape(()),
        *made,
    )


def solution(mesh):
    in_specs = (
        P(("dp", "head"), None, None),
        P(("dp", "head"), None, None),
        P(("dp", "head"), None, None),
        P("dp"),
        P(None, "dp", "head"),
        P(None, "dp", "head"),
        P(None, "dp", "head"),
        P("dp", "head"),
        P("dp", "head"),
        P("dp", "head"),
        P("head", "dp"),
        P("head", "dp"),
        P("head", "dp"),
        P(),
        P(),
        P(),
    )
    out_specs = (
        P(("dp", "head"), None, None),
        P(("dp", "head"), None, None),
        P(("dp", "head"), None, None),
        P(),
        P(None, "dp", "head"),
        P(None, "dp", "head"),
        P(None, "dp", "head"),
        P("dp", "head"),
        P("dp", "head"),
        P("dp", "head"),
        P("head", "dp"),
        P("head", "dp"),
        P("head", "dp"),
        P(),
        P(),
        P(),
    )
    return jax.shard_map(
        on_device, mesh=mesh, in_specs=in_specs, out_specs=out_specs, check_vma=False
    )
```

```python
import functools
from types import SimpleNamespace

import jax
import jax.numpy as jnp
from jax import lax
from jax.experimental import pallas as pl
from jax.experimental.pallas import tpu as pltpu
from jax.sharding import PartitionSpec as P

D = 1024
HEADS = 16
HEAD = D // HEADS
GROUP = 256
GROUPS = D // GROUP
STEP = 10

LN_EPS = 1e-05
BETA_ONE = 0.9
BETA_TWO = 0.999
ADAM_EPS = 1e-08
MATRIX_RATE = 0.1
NORM_RATE = 0.6
DECAY_RATE = 0.1
MAX_NORM = 0.05

MESH = pl.DeviceIdType.MESH
F32 = jnp.float32
BF16 = jnp.bfloat16
MIB = 2**20
EARLY = 2


def grid_of(dp_count, head_count):
    x = 1
    while 4 * x * x <= dp_count:
        x *= 2
    return {"z": dp_count // x, "x": x, "y": head_count // 2, "c": 2}


class Links:
    def __init__(self, sizes, send, recv, local):
        self.sizes, self.send, self.recv, self.local = sizes, send, recv, local
        self.used = self.used_local = 0
        dp, head = lax.axis_index("dp"), lax.axis_index("head")
        self.at = {
            "z": lax.div(dp, sizes["x"]),
            "x": lax.rem(dp, sizes["x"]),
            "y": lax.div(head, sizes["c"]),
            "c": lax.rem(head, sizes["c"]),
        }
        self.head = head

    def place(self, axis, k):
        return lax.rem(self.at[axis] + k, self.sizes[axis])

    def peer(self, steps):
        at = dict(self.at)
        for axis, k in steps.items():
            at[axis] = self.place(axis, k)
        return {
            "dp": at["z"] * self.sizes["x"] + at["x"],
            "head": at["y"] * self.sizes["c"] + at["c"],
        }

    def around(self, axes):
        ways = [{}]
        for axis in axes:
            ways = [{**way, axis: k} for way in ways for k in range(self.sizes[axis])]
        return ways[1:]

    def greet(self, *groups):
        barrier = pltpu.get_barrier_semaphore()
        self.met = [way for axes in groups for way in self.around(axes)]
        for way in self.met:
            pl.semaphore_signal(barrier, inc=1, device_id=self.peer(way), device_id_type=MESH)

    def meet(self):
        pl.semaphore_wait(pltpu.get_barrier_semaphore(), len(self.met))

    def copy(self, src, dst, slot, axis, k):
        return self.send_to(src, dst, slot, {axis: k})

    def send_to(self, src, dst, slot, way):
        return pltpu.make_async_remote_copy(
            src_ref=src,
            dst_ref=dst,
            send_sem=self.send.at[slot],
            recv_sem=self.recv.at[slot],
            device_id=self.peer(way),
            device_id_type=MESH,
        )

    def take(self):
        self.used += 1
        return self.used - 1

    def move(self, src, dst):
        self.used_local += 1
        made = pltpu.make_async_copy(src, dst, self.local.at[self.used_local - 1])
        made.start()
        return made


class Gather:
    def __init__(self, links, order, view):
        self.links, self.order, self.view = links, order, view
        self.sent, self.coming = [], {}

    def region(self, step, place):
        at = dict(self.links.at)
        for axis in self.order[:step]:
            at[axis] = None
        at[self.order[step]] = place
        return self.view(at)

    def start(self, step):
        axis, links = self.order[step], self.links
        mine = self.region(step, links.at[axis])
        self.coming[step] = []
        for k in range(1, links.sizes[axis]):
            slot = links.take()
            copy = links.copy(mine, mine, slot, axis, k)
            copy.start()
            self.sent.append(copy)
            lands = self.region(step, links.place(axis, links.sizes[axis] - k))
            self.coming[step].append(links.copy(lands, lands, slot, axis, k))

    def wait(self, step):
        for copy in self.coming[step]:
            copy.wait_recv()

    def go(self, step):
        self.wait(step)
        if step + 1 < len(self.order):
            self.start(step + 1)

    def close(self):
        for copy in self.sent:
            copy.wait_send()


def some(place):
    return slice(None) if place is None else place


def dot(a, b):
    return lax.dot_general(a, b, (((1,), (0,)), ((), ())), preferred_element_type=F32)


def dot_nt(a, b):
    return lax.dot_general(a, b, (((1,), (1,)), ((), ())), preferred_element_type=F32)


def dot_tn(a, b):
    return lax.dot_general(a, b, (((0,), (0,)), ((), ())), preferred_element_type=F32)


def normed(values):
    center = values - jnp.mean(values, axis=-1, keepdims=True)
    scale = lax.rsqrt(jnp.mean(center * center, axis=-1, keepdims=True) + LN_EPS)
    return center * scale, scale


def norm_back(up, hat, scale, gain):
    inner = up * gain
    return scale * (
        inner
        - jnp.mean(inner, axis=-1, keepdims=True)
        - hat * jnp.mean(inner * hat, axis=-1, keepdims=True)
    )


def fold(rows):
    return jnp.sum(rows.reshape(rows.shape[0] // 8, 8, rows.shape[1]), axis=0)


def gelu_and_slope(v):
    root = 0.7978845608028654
    square = v * v
    t = jnp.tanh(root * v * (1.0 + 0.044715 * square))
    half = 0.5 + 0.5 * t
    slope = half + (0.5 * root) * v * (1.0 - t * t) * (1.0 + (3.0 * 0.044715) * square)
    return v * half, slope


def diagonal(rows):
    n = GROUP // HEAD
    lat = rows.shape[0]
    tall = jnp.concatenate([rows] * n, axis=0)
    row = lax.broadcasted_iota(jnp.int32, tall.shape, 0) // lat
    col = lax.broadcasted_iota(jnp.int32, tall.shape, 1) // HEAD
    return jnp.where(row == col, tall, jnp.zeros_like(tall))


def undiagonal(tall):
    n = GROUP // HEAD
    lat = tall.shape[0] // n
    col = lax.broadcasted_iota(jnp.int32, (lat, GROUP), 1) // HEAD
    total = jnp.where(col == 0, tall[:lat], 0.0)
    for h in range(1, n):
        total = total + jnp.where(col == h, tall[h * lat : (h + 1) * lat], 0.0)
    return total


def weight_block(weights, m, g, sizes):
    block = weights.shape[-1]
    per = GROUP // block
    parts = []
    for s in range(per):
        h = g * per + s
        part = weights[m, lax.div(h, sizes["c"]), lax.rem(h, sizes["c"])]
        parts.append(part.reshape(D, block))
    return parts[0] if per == 1 else jnp.concatenate(parts, axis=1)


def softmax_columns(keys, spread_queries, seen):
    scores = dot_nt(keys, spread_queries)
    scores = jnp.where(seen, scores, -1e30)
    raised = jnp.exp(scores - jnp.max(scores, axis=0, keepdims=True))
    return raised * (1.0 / jnp.sum(raised, axis=0, keepdims=True))


def forward_kernel(
    sizes,
    att_ref,
    expand_ref,
    reduce_ref,
    tokens_ref,
    latents_ref,
    cotangent_ref,
    counts_ref,
    norm_ref,
    att_out,
    pairs_out,
    turned_out,
    queries_out,
    mixed_out,
    ff_grad_out,
    added_out,
    middle_out,
    middle_grad_out,
    branch_out,
    ff_norm_out,
    att,
    pairs,
    turned,
    queries,
    mixed,
    ff,
    added,
    middle,
    middle_grad,
    branch,
    ff_norm,
    rows,
    back,
    hid,
    bg,
    part,
    land_c,
    land_y,
    land_x,
    tokens,
    inputs,
    send,
    recv,
    local,
):
    links = Links(sizes, send, recv, local)
    links.greet(*"zxyc")
    images, span, _ = inputs.shape
    patches = tokens_ref.shape[1]
    lat = span - patches
    at = links.at
    outs = []

    loads = {}

    def fetch(i):
        if i < images:
            loads[i] = links.move(tokens_ref.at[i], tokens.at[i % 2])

    fetch(0)
    fetch(1)
    for m in range(4):
        att[m, at["y"], at["c"], at["z"], at["x"]] = att_ref[m].astype(BF16)
    back[at["y"], at["c"]] = cotangent_ref[...].astype(BF16)
    quarters, tile = ff.shape[0], ff.shape[-1]
    for q in range(quarters):
        ff[q, 0, at["z"], at["x"]] = expand_ref[:, q * tile : (q + 1) * tile].astype(BF16)
        ff[q, 1, at["z"], at["x"]] = reduce_ref[q * tile : (q + 1) * tile].T.astype(BF16)

    half = att.shape[5] // 2

    def att_view(m, s):
        def view(p):
            return att.at[m, some(p["y"]), some(p["c"]), some(p["z"]), some(p["x"]), pl.ds(s * half, half)]

        return view

    def ff_view(q, m):
        def view(p):
            return ff.at[q, m, some(p["z"]), some(p["x"])]

        return view

    def back_view(p):
        return back.at[some(p["y"]), some(p["c"])]

    def row_view(i):
        def view(p):
            return rows.at[some(p["y"]), some(p["c"]), pl.ds(i * lat, lat)]

        return view

    query, key, value, output = ([Gather(links, "zxyc", att_view(m, s)) for s in range(2)] for m in range(4))
    hidden = [Gather(links, "zx", ff_view(q, m)) for q in range(quarters) for m in range(2)]
    cotangent = [Gather(links, "yc", back_view)]
    ff_rows = [Gather(links, "yc", row_view(i)) for i in range(images)]
    everything = [*query, *key, *value, *output, *hidden, *cotangent, *ff_rows]

    def start(parts):
        for part in parts:
            part.start(0)

    def go(parts, step):
        for part in parts:
            part.go(step)

    links.meet()
    start(key + value + hidden[:1] + query + hidden[1:2] + output)

    for i in range(images):
        low = normed(latents_ref[pl.ds(i * lat, lat)].astype(F32))[0] * norm_ref[2:3] + norm_ref[3:4]
        inputs[i, pl.ds(patches, lat)] = low.astype(BF16)

    def normalize(i):
        loads[i].wait()
        some_rows = 64

        def one(t, _):
            part = pl.ds(pl.multiple_of(t * some_rows, some_rows), some_rows)
            low = normed(tokens[i % 2, part].astype(F32))[0] * norm_ref[0:1] + norm_ref[1:2]
            inputs[i, part] = low.astype(BF16)
            return 0

        lax.fori_loop(0, patches // some_rows, one, 0)
        fetch(i + 2)

    turning = {}

    def turn(i):
        if i >= 2:
            turning[i - 2].wait()

        def one(t, _):
            part = pl.ds(pl.multiple_of(t * 128, 128), 128)
            turned[i % 2, :, part] = inputs[i, part].T
            return 0

        lax.fori_loop(0, span // 128, one, 0)
        turning[i] = links.move(turned.at[i % 2], turned_out.at[:, pl.ds(i * span, span)])

    k0, k1, v0, v1, q0, q1, o0, o1 = *key, *value, *query, *output
    f = [*hidden, *[None] * (8 - len(hidden))]
    steps = []

    def plan(*ticks):
        steps.extend(ticks)

    plan(
        [(k0, 0)],
        [(k1, 0)],
        [(k0, 1), (v0, 0)],
        [(k1, 1), (v1, 0)],
        [(v0, 1)],
        [(k0, 2), (v1, 1)],
        [(f[0], 0)],
        [(k1, 2), (q0, 0)],
    )

    def tick():
        for part, step in steps.pop(0) if steps else ():
            if part is not None:
                part.go(step)
            if part in hidden:
                start(hidden[hidden.index(part) + 2 :][:1])

    def rest():
        while steps:
            tick()

    for i in range(images):
        normalize(i)
        tick()
        turn(i)
        tick()
    plan([(q1, 0), (v0, 2), (q0, 1)])
    rest()
    for i in range(max(0, images - 2), images):
        turning[i].wait()
    go(key, 3)

    def project(i, m):
        def one(g, _):
            weight = weight_block(att, m, g, sizes)
            pairs[i, (m - 1) * GROUPS + g] = dot(inputs[i], weight).astype(BF16)
            return 0

        lax.fori_loop(0, GROUPS, one, 0)

    def attend(i):
        position = lax.broadcasted_iota(jnp.int32, (span, GROUP), 0)
        count = counts_ref[links.head * images + i]
        seen = (position < count) | (position >= patches)

        def one(g, _):
            spread = diagonal(queries[g, pl.ds(i * lat, lat)])
            probs = softmax_columns(pairs[i, g], spread, seen).astype(BF16)
            wide = dot_tn(probs, pairs[i, GROUPS + g])
            mixed[g, pl.ds(i * lat, lat)] = undiagonal(wide).astype(BF16)
            return 0

        lax.fori_loop(0, GROUPS, one, 0)

    def finish(i):
        part = pl.ds(i * lat, lat)
        whole = jnp.concatenate([mixed[g, part] for g in range(GROUPS)], axis=1)
        made = jnp.concatenate(
            [dot(whole, weight_block(att, 3, g, sizes)) for g in range(GROUPS)], axis=1
        )
        value = latents_ref[part].astype(F32) + made
        middle[part] = value
        low = normed(value)[0] * norm_ref[4:5] + norm_ref[5:6]
        rows[at["y"], at["c"], part] = low.astype(BF16)
        ff_rows[i].start(0)

    plan([], [(q1, 1)], [(f[1], 0)], [(v1, 2)])
    for i in range(images):
        project(i, 1)
        tick()
    plan([(o0, 0), (q0, 2), (o1, 0)])
    rest()
    go(value, 3)
    plan([(o0, 1)], [(q1, 2)], [(f[2], 0), (o1, 1)], [(f[3], 0)])
    for i in range(images):
        project(i, 2)
        outs.append(links.move(pairs.at[i], pairs_out.at[i]))
        tick()
    plan([(o0, 2)])
    rest()
    go(query, 3)
    stack = inputs[:, patches:].reshape(images * lat, D)
    for g in range(GROUPS):
        made = dot(stack, weight_block(att, 0, g, sizes)) * HEAD ** (-0.5)
        queries[g] = made.astype(BF16)
    outs.append(links.move(queries, queries_out))
    plan([(f[4], 0)], [(o1, 2)], [(f[5], 0)])
    for i in range(images):
        attend(i)
        tick()
        if i == 0:
            start(cotangent)
    rest()
    go(output, 3)
    outs.append(links.move(att, att_out))
    outs.append(links.move(mixed, mixed_out))
    plan([], [(f[6], 0)], [(cotangent[0], 0)], [(f[7], 0)])
    for i in range(images):
        finish(i)
        tick()
    rest()
    outs.append(links.move(middle, middle_out))
    go(cotangent, 1)
    go(ff_rows, 0)
    n = images * lat
    cs, ys, zs = (sizes[a] for a in "cyz")
    sib = links.place("c", 1)
    xr = sizes["x"] * att.shape[5]

    def first(q):
        def one(yi, _):
            before = dot(rows[yi].reshape(cs * n, D), ff[q, 0].reshape(D, tile))
            up = dot(back[yi].reshape(cs * n, D), ff[q, 1].reshape(D, tile))
            made, slope = gelu_and_slope(before)
            hid[yi, :, :, q * tile : (q + 1) * tile] = made.astype(BF16).reshape(cs, n, tile)
            bg[yi, :, :, q * tile : (q + 1) * tile] = (up * slope).astype(BF16).reshape(cs, n, tile)
            return 0

        lax.fori_loop(0, ys, one, 0)

    go(ff_rows, 1)
    for q in range(quarters):
        go(hidden[2 * q : 2 * q + 2], 1)
        first(q)

    ff_block = quarters * tile

    def second(kind, yi):
        wide = (hid if kind else bg)[yi].reshape(cs * n, ff_block)
        made = added if kind else part

        def one(z, _):
            cols = pl.ds(pl.multiple_of(z * xr, xr), xr)
            weight = jnp.concatenate([ff[q, kind, z].reshape(xr, tile) for q in range(quarters)], axis=1)
            made[yi, :, :, cols] = dot_nt(wide, weight).astype(BF16).reshape(cs, n, xr)
            return 0

        lax.fori_loop(0, zs, one, 0)

    sent, chip, along = [], {}, {}
    for k in [*range(1, ys), 0]:
        yi = links.place("y", k)
        second(0, yi)
        slot = links.take()
        land = land_c.at[yi]
        copy = links.copy(part.at[yi, sib], land, slot, "c", 1)
        copy.start()
        sent.append(copy)
        chip[k] = links.copy(land, land, slot, "c", 1)
    for k in range(1, ys):
        yi = links.place("y", k)
        chip[k].wait_recv()
        summed = part[yi, at["c"]].astype(F32) + land_c[yi].astype(F32)
        part[yi, at["c"]] = summed.astype(BF16)
        slot = links.take()
        land = land_y.at[k - 1]
        copy = links.copy(part.at[yi, at["c"]], land, slot, "y", k)
        copy.start()
        sent.append(copy)
        along[k] = links.copy(land, land, slot, "y", k)
    for gather in hidden:
        gather.close()

    def gradient(m, z):
        left, right = (back, hid) if m else (rows, bg)
        cols = pl.ds(pl.multiple_of(z * xr, xr), xr)
        made = dot_tn(
            left[:, :, :, cols].reshape(ys * cs * n, xr), right[...].reshape(ys * cs * n, ff_block)
        ).astype(BF16)
        for q in range(quarters):
            ff[q, m, z] = made[:, q * tile : (q + 1) * tile].reshape(*ff.shape[3:5], tile)

    xs = sizes["x"]
    early = range(1, 1 + land_x.shape[0])
    x_slots = {k: [links.take() for _ in range(1, xs)] for k in early}

    def x_copies(k):
        for j, slot in enumerate(x_slots[k], 1):
            block = ff.at[:, 0, links.place("z", k), links.place("x", j)]
            yield links.copy(block, land_x.at[k - 1, j - 1], slot, "x", j)

    for k in early:
        gradient(0, links.place("z", k))
        for copy in x_copies(k):
            copy.start()
    for yi in range(ys):
        second(1, yi)
    outs.append(links.move(added, added_out))

    def other(k, _):
        gradient(0, links.place("z", k))
        return 0

    lax.fori_loop(1 + len(early), zs + 1, other, 0)

    def both(z, _):
        gradient(1, z)
        return 0

    lax.fori_loop(0, zs, both, 0)
    chip[0].wait_recv()
    for k in range(1, ys):
        along[k].wait_recv()

    def back_one(t, carry):
        gain, shift = carry
        rws = pl.ds(pl.multiple_of(t * lat, lat), lat)
        up = part[at["y"], at["c"], rws].astype(F32) + land_c[at["y"], rws].astype(F32)
        for k in range(1, ys):
            up = up + land_y[k - 1, rws].astype(F32)
        hat, scale = normed(middle[rws])
        value = cotangent_ref[rws] + norm_back(up, hat, scale, norm_ref[4:5])
        middle_grad[rws] = value
        branch[rws] = value.astype(BF16)
        return gain + fold(up * hat), shift + fold(up)

    zero = jnp.zeros((8, D), F32)
    ff_norm[0], ff_norm[1] = lax.fori_loop(0, images, back_one, (zero, zero))
    outs.append(links.move(middle_grad, middle_grad_out))
    outs.append(links.move(branch, branch_out))
    outs.append(links.move(ff_norm, ff_norm_out))
    for k in early:
        for copy in x_copies(k):
            copy.wait_recv()
        z = links.place("z", k)
        for q in range(quarters):
            total = ff[q, 0, z, at["x"]].astype(F32)
            for j in range(xs - 1):
                total = total + land_x[k - 1, j, q].astype(F32)
            ff[q, 0, z, at["x"]] = total.astype(BF16)
        for copy in x_copies(k):
            copy.wait_send()
    outs.append(links.move(ff, ff_grad_out))
    for copy in sent:
        copy.wait_send()
    for gather in everything:
        if gather not in hidden:
            gather.close()
    for out in outs:
        out.wait()


def forward(att, expand, reduce, tokens, latents, cotangent, counts, norm_params):
    sizes = grid_of(lax.axis_size("dp"), lax.axis_size("head"))
    z, x, y, c = (sizes[a] for a in "zxyc")
    images, patches, _ = tokens.shape
    lat = latents.shape[1]
    span = patches + lat
    n = images * lat
    _, row_block, col_block = att.shape
    ff_block = expand.shape[1]
    tile = min(GROUP, ff_block)
    quarters = ff_block // tile
    shapes = dict(
        att=((4, y, c, z, x, row_block, col_block), BF16),
        pairs=((images, 2 * GROUPS, span, GROUP), BF16),
        turned=((D, images * span), BF16),
        queries=((GROUPS, n, GROUP), BF16),
        mixed=((GROUPS, n, GROUP), BF16),
        ff=((quarters, 2, z, x, row_block, tile), BF16),
        added=((y, c, n, D), BF16),
        middle=((n, D), F32),
        middle_grad=((n, D), F32),
        branch=((n, D), BF16),
        ff_norm=((2, 8, D), F32),
    )
    held = dict(shapes)
    held.update(turned=((2, D, span), BF16))
    inside = [
        ((y, c, n, D), BF16),
        ((y, c, n, D), BF16),
        ((y, c, n, ff_block), BF16),
        ((y, c, n, ff_block), BF16),
        ((y, c, n, D), BF16),
        ((y, n, D), BF16),
        ((y - 1, n, D), BF16),
        ((EARLY, x - 1, quarters, row_block, tile), BF16),
        ((2, patches, D), BF16),
        ((images, span, D), BF16),
    ]
    per_att = sum(s - 1 for s in sizes.values())
    slots = 8 * per_att + 8 * (z + x - 2) + (1 + images) * (y + c - 2) + 2 * y + EARLY * x
    vmem, anywhere = pl.BlockSpec(memory_space=pltpu.VMEM), pl.BlockSpec(memory_space=pl.ANY)
    made = pl.pallas_call(
        functools.partial(forward_kernel, sizes),
        out_shape=[jax.ShapeDtypeStruct(*v) for v in shapes.values()],
        in_specs=[vmem, vmem, vmem, anywhere, vmem, vmem, pl.BlockSpec(memory_space=pltpu.SMEM), vmem],
        out_specs=[anywhere] * len(shapes),
        scratch_shapes=[pltpu.VMEM(*v) for v in [*held.values(), *inside]]
        + [
            pltpu.SemaphoreType.DMA((slots,)),
            pltpu.SemaphoreType.DMA((slots,)),
            pltpu.SemaphoreType.DMA((2 * images + 20,)),
        ],
        compiler_params=pltpu.CompilerParams(
            collective_id=0, has_side_effects=True, vmem_limit_bytes=63 * MIB + 900 * 1024
        ),
        name="gather_and_attend",
    )(att, expand, reduce, tokens, latents.reshape(n, D), cotangent.reshape(n, D), counts, norm_params)
    return SimpleNamespace(**dict(zip(shapes, made)))


class Scatter:
    def __init__(self, links, order, view, lands):
        self.links, self.order, self.view, self.lands = links, order, view, lands
        self.slots = {}

    def region(self, step, place):
        at = dict(self.links.at)
        for axis in self.order[step + 1 :]:
            at[axis] = None
        at[self.order[step]] = place
        return self.view(at)

    def copies(self, step):
        axis, links = self.order[step], self.links
        for k, slot in enumerate(self.slots[step], 1):
            yield links.copy(self.region(step, links.place(axis, k)), self.lands[step][k - 1], slot, axis, k)

    def start(self, step):
        self.slots[step] = [self.links.take() for _ in range(1, self.links.sizes[self.order[step]])]
        for copy in self.copies(step):
            copy.start()

    def wait(self, step):
        for k, slot in enumerate(self.slots[step], 1):
            land = self.lands[step][k - 1]
            self.links.copy(land, land, slot, self.order[step], k).wait_recv()

    def add(self, step, out=None):
        mine = self.region(step, self.links.at[self.order[step]])
        lands = self.lands[step]
        lead = mine.shape[0] if len(mine.shape) > 2 else None

        def total(at):
            value = mine[at].astype(F32)
            for land in lands:
                value = value + land[at].astype(F32)
            return value

        if out is not None:
            out[...] = total(Ellipsis)
        elif lead is None:
            mine[...] = total(Ellipsis).astype(BF16)
        else:

            def one(t, _):
                mine[t] = total(t).astype(BF16)
                return 0

            lax.fori_loop(0, lead, one, 0)

    def go(self, step, out=None):
        self.wait(step)
        self.add(step, out)
        if step + 1 < len(self.order):
            self.start(step + 1)

    def close(self):
        for step in self.slots:
            for copy in self.copies(step):
                copy.wait_send()


ATT_ORDERS = {0: ("yxz", "yxz"), 1: ("yxz", "xyz"), 2: ("yxz", "xyz"), 3: ("yxz", "yxz")}


def land_shapes(sizes, order, axes, tail):
    shapes, left = [], list(axes)
    for axis in order:
        left.remove(axis)
        shapes.append((sizes[axis] - 1, *(sizes[a] for a in left), *tail))
    return shapes


def backward_kernel(sizes, dims, *refs):
    names, keys, images, patches, lat, ff_block = dims
    r = SimpleNamespace(**dict(zip(names, refs)))
    total_lands = dict(zip("cyxz", refs[len(names) :]))
    r.square_lands = refs[len(names) + 4 : len(names) + 6]
    att_lands = dict(zip(keys, refs[len(names) + 6 :]))
    links = Links(sizes, r.send, r.recv, r.local)
    links.greet("zx", "yc")
    at = links.at
    sib = links.place("c", 1)
    n = images * lat
    span = patches + lat
    zs, xs, ys, cs = (sizes[a] for a in "zxyc")
    row_block, col_block = r.att_share.shape[1:]
    xr = xs * row_block
    heads = ys * cs
    half = row_block // 2
    norm_ref, latents = r.norm, r.latents
    queries, mixed = r.queries, r.mixed
    grads_ff = r.grads_ff
    middle_grad, branch, latent_low = r.middle_grad, r.branch, r.latent_low
    mixed_grad, query_back = r.mixed_grad, r.query_back
    outs = []

    units = [(m, k) for k in [*range(1, zs), 0] for m in range(2)]
    ready = [(0, k) for k in range(1, 1 + EARLY)]
    units = [unit for unit in units if unit not in ready]
    x_slots = {unit: [links.take() for _ in range(1, xs)] for unit in units}
    z_slots = {unit: links.take() for unit in units + ready if unit[1]}

    def x_copies(unit):
        m, k = unit
        z = links.place("z", k)
        for j, slot in enumerate(x_slots[unit], 1):
            yield links.copy(
                grads_ff.at[:, m, z, links.place("x", j)], r.ff_land_x.at[m, z, j - 1], slot, "x", j
            )

    def z_copy(unit):
        m, k = unit
        return links.copy(
            grads_ff.at[:, m, links.place("z", k), at["x"]], r.ff_land_z.at[m, k - 1], z_slots[unit], "z", k
        )

    quarters, tile = grads_ff.shape[0], grads_ff.shape[-1]

    def ff_along(unit):
        m, k = unit
        z = links.place("z", k)
        for copy in x_copies(unit):
            copy.wait_recv()
        for q in range(quarters):
            total = grads_ff[q, m, z, at["x"]].astype(F32)
            for j in range(xs - 1):
                total = total + r.ff_land_x[m, z, j, q].astype(F32)
            if k:
                grads_ff[q, m, z, at["x"]] = total.astype(BF16)
            else:
                r.ff_share[m, :, q * tile : (q + 1) * tile] = total
        if k:
            z_copy(unit).start()

    def ff_finish():
        for m in range(2):
            for k in range(1, zs):
                z_copy((m, k)).wait_recv()
            for q in range(quarters):
                cols = pl.ds(q * tile, tile)
                total = r.ff_share[m, :, cols]
                for k in range(1, zs):
                    total = total + r.ff_land_z[m, k - 1, q].astype(F32)
                r.ff_share[m, :, cols] = total

    pairs = r.pairs_here
    early = [links.move(r.pairs.at[i], pairs.at[i]) for i in range(images)]

    load = links.move(r.ff_grad, grads_ff)
    own = links.move(r.added.at[:, at["c"]], r.added_here)
    links.meet()
    load.wait()
    for unit in units:
        for copy in x_copies(unit):
            copy.start()
    for unit in ready:
        z_copy(unit).start()

    c_slots = [links.take() for _ in range(ys)]
    y_slots = [links.take() for _ in range(1, ys)]

    def added_chip(k):
        yi = links.place("y", k)
        return links.copy(r.added.at[yi, sib], r.added_land_c.at[yi], c_slots[k], "c", 1)

    def added_along(k):
        return links.copy(r.added_here.at[links.place("y", k)], r.added_land_y.at[k - 1], y_slots[k - 1], "y", k)

    for k in range(ys):
        added_chip(k).start()
    own.wait()

    def added_out():
        for k in range(1, ys):
            yi = links.place("y", k)
            added_chip(k).wait_recv()
            summed = r.added_here[yi].astype(F32) + r.added_land_c[yi].astype(F32)
            r.added_here[yi] = summed.astype(BF16)
            added_along(k).start()

    resampled_low = r.added_here.at[at["y"]]

    def added_finish():
        added_chip(0).wait_recv()
        for k in range(1, ys):
            added_along(k).wait_recv()

        def one(t, _):
            rws = pl.ds(pl.multiple_of(t * lat, lat), lat)
            up = r.added_here[at["y"], rws].astype(F32) + r.added_land_c[at["y"], rws].astype(F32)
            for k in range(1, ys):
                up = up + r.added_land_y[k - 1, rws].astype(F32)
            resampled_low[rws] = (r.middle[rws] + up).astype(BF16)
            return 0

        lax.fori_loop(0, images, one, 0)
        for k in range(ys):
            added_chip(k).wait_send()
        for k in range(1, ys):
            added_along(k).wait_send()
        return links.move(resampled_low, r.resampled)

    r.norm_parts[4] = r.ff_norm[0]
    r.norm_parts[5] = r.ff_norm[1]

    steps = []

    def tick():
        if steps:
            steps.pop(0)()

    def plan(*calls):
        steps.append(lambda: [f(*args) for f, *args in calls])

    waiting = []

    def attention(grads, turned_left):
        per = GROUP // col_block
        block_slots = {m: [links.take() for _ in range(ys)] for m in range(4)}

        def block_copy(m, yi):
            slot = block_slots[m][0] + yi
            return links.copy(grads.at[m, yi, sib], r.att_land_c.at[m, yi], slot, "c", 1)

        def att_scatter(m, s):
            def view(p):
                return grads.at[m, some(p["y"]), at["c"], some(p["z"]), some(p["x"]), pl.ds(s * half, half)]

            order = ATT_ORDERS[m][s]
            lands = [
                [att_lands[m, s, step].at[k] for k in range(sizes[axis] - 1)]
                for step, axis in enumerate(order)
            ]
            return Scatter(links, order, view, lands)

        scatter = {m: [att_scatter(m, s) for s in range(2)] for m in range(4)}

        def go(m, step):
            for s, part in enumerate(scatter[m]):
                part.go(step, r.att_share.at[m, pl.ds(s * half, half)] if step == 2 else None)

        def chip_sum(m):
            for yi in range(ys):
                block_copy(m, yi).wait_recv()

                def one(z, _):
                    value = grads[m, yi, at["c"], z].astype(F32) + r.att_land_c[m, yi, z].astype(F32)
                    grads[m, yi, at["c"], z] = value.astype(BF16)
                    return 0

                lax.fori_loop(0, zs, one, 0)
            for part in scatter[m]:
                part.start(0)

        def products(m, left, right, between=None):
            def of(ci, send):
                def one(yi, _):
                    made = dot(left(), right(yi * cs + ci)).astype(BF16)
                    grads[m, yi, ci] = made.reshape(zs, xs, row_block, col_block)
                    if send:
                        block_copy(m, yi).start()
                    return 0

                lax.fori_loop(0, ys, one, 0)

            of(sib, True)
            if between is not None:
                between()
            of(at["c"], False)

        def query_columns(h):
            j = lax.div(h * col_block, GROUP)
            if per == 1:
                return query_back[j]
            off = pl.multiple_of(lax.rem(h, per) * col_block, col_block)
            return query_back[j, :, pl.ds(off, col_block)]

        def columns(m):
            def right(h):
                j = lax.div(h * col_block, GROUP) + (m - 1) * GROUPS
                if per == 1:
                    return pairs[:, j].reshape(images * span, GROUP)
                off = pl.multiple_of(lax.rem(h, per) * col_block, col_block)
                return pairs[:, j, :, pl.ds(off, col_block)].reshape(images * span, col_block)

            return right

        def attend(i):
            position = lax.broadcasted_iota(jnp.int32, (span, GROUP), 0)
            count = r.counts[links.head * images + i]
            seen = (position < count) | (position >= patches)
            rws = pl.ds(i * lat, lat)

            def one(g, _):
                keys, values = pairs[i, g], pairs[i, GROUPS + g]
                spread = diagonal(queries[g, rws])
                probs = softmax_columns(keys, spread, seen)
                upstream = diagonal(mixed_grad[g, rws])
                prob_grad = dot_nt(values, upstream)
                inner = jnp.sum(probs * prob_grad, axis=0, keepdims=True)
                score_grad = (probs * (prob_grad - inner)).astype(BF16)
                back = undiagonal(dot_tn(score_grad, keys)) * HEAD ** (-0.5)
                query_back[g, rws] = back.astype(BF16)
                pairs[i, GROUPS + g] = dot(probs.astype(BF16), upstream).astype(BF16)
                pairs[i, g] = dot(score_grad, spread).astype(BF16)
                return 0

            lax.fori_loop(0, GROUPS, one, 0)

        def weights(turned, weight):
            load_weight = links.move(r.att.at[3], weight)
            load_turned = links.move(r.turned, turned)
            for g in range(GROUPS):
                turned_left[pl.ds(g * GROUP, GROUP)] = mixed[g].T
            products(
                3,
                lambda: turned_left[...],
                lambda h: branch[:, pl.ds(pl.multiple_of(h * col_block, col_block), col_block)],
            )
            load_weight.wait()
            for g in range(GROUPS):
                first = g * GROUP // row_block
                wide = []
                for h in range(heads):
                    blocks = [
                        weight[h // cs, h % cs, b // xs, b % xs] for b in range(first, first + GROUP // row_block)
                    ]
                    wide.append(jnp.concatenate(blocks, axis=0))
                mixed_grad[g] = dot_nt(branch[...], jnp.concatenate(wide, axis=1)).astype(BF16)
            ff_steps = [lambda u=u: ff_along(u) for u in units]
            plan((chip_sum, 3), (ff_steps[0],))
            plan((ff_steps[1],))
            plan()
            plan((ff_steps[2],))
            for i in range(images):
                attend(i)
                tick()
            while steps:
                tick()
            load_turned.wait()
            for i in range(images):
                turned_left[:, pl.ds(i * lat, lat)] = turned[:, i * span + patches : (i + 1) * span]
            products(0, lambda: turned_left[...], query_columns)
            late = ff_steps[3:]
            plan((late.pop(0),), (chip_sum, 0))
            products(2, lambda: turned[...], columns(2), tick)
            plan((late.pop(0),), (chip_sum, 2), (go, 3, 0))
            products(1, lambda: turned[...], columns(1), tick)
            waiting.extend(late)

        pl.run_scoped(
            weights,
            pltpu.VMEM((D, images * span), BF16),
            pltpu.VMEM((ys, cs, zs, xs, row_block, col_block), BF16),
        )

        def inputs(att, tokens, pair_grad):
            weight_loads = [links.move(r.att.at[m], att.at[m]) for m in (1, 2, 0)]
            loads = {}

            def fetch(i):
                loads[i] = links.move(r.tokens.at[i], tokens.at[i % 2])

            media_out = {}
            fetch(0)
            few = len(waiting) // 2
            plan((chip_sum, 1), (added_out,), *[(f,) for f in waiting[:few]])
            plan((go, 0, 0))
            plan(*[(f,) for f in waiting[few:]])
            plan((go, 3, 1), (go, 2, 0))
            plan((go, 0, 1))
            plan((go, 1, 0), (go, 3, 2))
            plan((go, 2, 1))
            plan((go, 0, 2))
            zero = jnp.zeros((8, D), F32)
            sums = (zero, zero, zero, zero)
            for load in weight_loads:
                load.wait()
            for i in range(images):
                stacked = jnp.concatenate([pairs[i, j] for j in range(2 * GROUPS)], axis=1)
                asked = jnp.concatenate([query_back[g, pl.ds(i * lat, lat)] for g in range(GROUPS)], axis=1)

                def one(z, _):
                    cols = pl.ds(pl.multiple_of(z * xr, xr), xr)
                    wide = jnp.concatenate(
                        [att[m, h // cs, h % cs, z].reshape(xr, col_block) for m in (1, 2) for h in range(heads)], axis=1
                    )
                    narrow = jnp.concatenate(
                        [att[0, h // cs, h % cs, z].reshape(xr, col_block) for h in range(heads)], axis=1
                    )
                    pair_grad[:, cols] = dot_nt(stacked, wide)
                    pair_grad[patches:, cols] += dot_nt(asked, narrow)
                    return 0

                lax.fori_loop(0, zs, one, 0)
                tick()
                if i + 1 < images:
                    if i >= 1:
                        media_out[i - 1].wait()
                    fetch(i + 1)
                loads[i].wait()
                slot = i % 2
                tile = 64

                def media(t, carry):
                    gain, shift = carry
                    rws = pl.ds(pl.multiple_of(t * tile, tile), tile)
                    hat, scale = normed(tokens[slot, rws].astype(F32))
                    up = pair_grad[rws]
                    tokens[slot, rws] = norm_back(up, hat, scale, norm_ref[0:1]).astype(BF16)
                    return gain + fold(up * hat), shift + fold(up)

                gain, shift = lax.fori_loop(0, patches // tile, media, (sums[0], sums[1]))
                media_out[i] = links.move(tokens.at[slot], r.media_grad.at[i])
                rws = pl.ds(i * lat, lat)
                hat, scale = normed(latents[rws].astype(F32))
                up = pair_grad[patches:]
                made = middle_grad[rws] + norm_back(up, hat, scale, norm_ref[2:3])
                latent_low[rws] = made.astype(BF16)
                sums = (gain, shift, sums[2] + fold(up * hat), sums[3] + fold(up))
                tick()
            for k, value in enumerate(sums):
                r.norm_parts[k] = value
            for i in range(max(0, images - 2), images):
                media_out[i].wait()

        pl.run_scoped(
            inputs,
            pltpu.VMEM((3, ys, cs, zs, xs, row_block, col_block), BF16),
            pltpu.VMEM((2, patches, D), BF16),
            pltpu.VMEM((span, D), F32),
        )
        sums = [jnp.sum(r.norm_parts[k], axis=0, keepdims=True) for k in range(6)]
        r.totals[...] = jnp.concatenate([*sums, jnp.zeros((2, D), F32)], axis=0)
        total_slots = {axis: [links.take() for _ in range(1, sizes[axis])] for axis in "cyxz"}

        def total_copies(axis):
            mine = total_lands[axis].at[at[axis]]
            for k, slot in enumerate(total_slots[axis], 1):
                yield links.copy(mine, mine, slot, axis, k)

        def total_start(axis):
            total_lands[axis][at[axis]] = r.totals[...]
            for copy in total_copies(axis):
                copy.start()

        def total_finish(axis):
            lands = total_lands[axis]
            for k, slot in enumerate(total_slots[axis], 1):
                land = lands.at[links.place(axis, sizes[axis] - k)]
                links.copy(land, land, slot, axis, k).wait_recv()
            value = lands[0]
            for k in range(1, sizes[axis]):
                value = value + lands[k]
            r.totals[...] = value

        total_start("c")
        while steps:
            tick()
        total_finish("c")
        total_start("y")
        go(1, 1)
        total_finish("y")
        total_start("x")
        go(2, 2)
        total_finish("x")
        total_start("z")
        ff_finish()
        go(1, 2)
        resampled = added_finish()
        total_finish("z")
        for axis in "cyxz":
            for copy in total_copies(axis):
                copy.wait_send()
        resampled.wait()
        for m in range(4):
            for yi in range(ys):
                block_copy(m, yi).wait_send()
            for part in scatter[m]:
                part.close()
        for unit in units:
            for copy in x_copies(unit):
                copy.wait_send()
            if unit[1]:
                z_copy(unit).wait_send()
        for unit in ready:
            z_copy(unit).wait_send()

    for load in early:
        load.wait()
    pl.run_scoped(
        attention,
        pltpu.VMEM((4, ys, cs, zs, xs, row_block, col_block), BF16),
        pltpu.VMEM((D, n), BF16),
    )

    outs.append(links.move(latent_low, r.latent_grad))
    squares = jnp.sum(r.att_share[...] * r.att_share[...]) + jnp.sum(r.ff_share[...] * r.ff_share[...])
    value = jnp.full((8, 128), squares, F32)
    last = []
    for axes, lands in zip(("yc", "zx"), r.square_lands):
        first, second = axes

        def spot(way):
            return links.place(first, way.get(first, 0)) * sizes[second] + links.place(second, way.get(second, 0))

        mine = lands.at[spot({})]
        mine[...] = value
        coming = []
        for way in links.around(axes):
            slot = links.take()
            copy = links.send_to(mine, mine, slot, way)
            copy.start()
            last.append(copy)
            land = lands.at[spot({axis: sizes[axis] - k for axis, k in way.items()})]
            coming.append(links.send_to(land, land, slot, way))
        for copy in coming:
            copy.wait_recv()
        value = lands[0]
        for k in range(1, lands.shape[0]):
            value = value + lands[k]
    r.squares[...] = value
    for copy in last:
        copy.wait_send()
    for out in outs:
        out.wait()


def backward(got, tokens, latents, counts, norm_params, row_block, col_block, ff_block):
    sizes = grid_of(lax.axis_size("dp"), lax.axis_size("head"))
    zs, xs, ys, cs = (sizes[a] for a in "zxyc")
    images, patches, _ = tokens.shape
    lat = latents.shape[1]
    n = images * lat
    half = row_block // 2
    vmem, anywhere = pl.BlockSpec(memory_space=pltpu.VMEM), pl.BlockSpec(memory_space=pl.ANY)
    smem = pl.BlockSpec(memory_space=pltpu.SMEM)
    inputs = dict(
        att=(got.att, anywhere),
        ff_grad=(got.ff, anywhere),
        added=(got.added, anywhere),
        middle=(got.middle, vmem),
        pairs=(got.pairs, anywhere),
        turned=(got.turned, anywhere),
        tokens=(tokens, anywhere),
        queries=(got.queries, vmem),
        mixed=(got.mixed, vmem),
        middle_grad=(got.middle_grad, vmem),
        branch=(got.branch, vmem),
        ff_norm=(got.ff_norm, vmem),
        latents=(latents.reshape(n, D), vmem),
        norm=(norm_params, vmem),
        counts=(counts, smem),
    )
    outputs = dict(
        resampled=((n, D), BF16, anywhere),
        media_grad=((images, patches, D), BF16, anywhere),
        latent_grad=((n, D), BF16, anywhere),
        att_share=((4, row_block, col_block), F32, vmem),
        ff_share=((2, row_block, ff_block), F32, vmem),
        totals=((8, D), F32, vmem),
        squares=((8, 128), F32, vmem),
    )
    scratch = dict(
        grads_ff=(got.ff.shape, BF16),
        ff_land_x=((2, zs, xs - 1, got.ff.shape[0], row_block, got.ff.shape[-1]), BF16),
        ff_land_z=((2, zs - 1, got.ff.shape[0], row_block, got.ff.shape[-1]), BF16),
        added_here=((ys, n, D), BF16),
        added_land_c=((ys, n, D), BF16),
        added_land_y=((ys - 1, n, D), BF16),
        att_land_c=((4, ys, zs, xs, row_block, col_block), BF16),
        pairs_here=(got.pairs.shape, BF16),
        latent_low=((n, D), BF16),
        mixed_grad=((GROUPS, n, GROUP), BF16),
        query_back=((GROUPS, n, GROUP), BF16),
        norm_parts=((6, 8, D), F32),
    )
    totals = [((sizes[axis], 8, D), F32) for axis in "cyxz"]
    totals += [((sizes[a] * sizes[b], 8, 128), F32) for a, b in ("yc", "zx")]
    lands = {}
    for m, orders in ATT_ORDERS.items():
        for s, order in enumerate(orders):
            for step, shape in enumerate(land_shapes(sizes, order, "yzx", (half, col_block))):
                lands[m, s, step] = (shape, BF16)
    steps = sum(v - 1 for v in sizes.values())
    slots = 9 * steps + 2 * (zs * xs + zs) + 6 * ys + zs * xs + ys * cs
    semaphores = dict(send=slots, recv=slots, local=3 * images + 30)
    names = [*inputs, *outputs, *semaphores, *scratch]
    made = pl.pallas_call(
        functools.partial(backward_kernel, sizes, (names, tuple(lands), images, patches, lat, ff_block)),
        out_shape=[jax.ShapeDtypeStruct(shape, dtype) for shape, dtype, _ in outputs.values()],
        in_specs=[spec for _, spec in inputs.values()],
        out_specs=[spec for _, _, spec in outputs.values()],
        scratch_shapes=[pltpu.SemaphoreType.DMA((v,)) for v in semaphores.values()]
        + [pltpu.VMEM(*v) for v in [*scratch.values(), *totals, *lands.values()]],
        compiler_params=pltpu.CompilerParams(
            collective_id=1, has_side_effects=True, vmem_limit_bytes=63 * MIB + 900 * 1024
        ),
        name="backward_and_scatter",
    )(*(value for value, _ in inputs.values()))
    return SimpleNamespace(**dict(zip(outputs, made)))


def adam_step(master, first, second, gradient, step_rate, decay_rate):
    first_new = BETA_ONE * first + (1.0 - BETA_ONE) * gradient
    second_new = BETA_TWO * second + (1.0 - BETA_TWO) * gradient * gradient
    first_hat = first_new / (1.0 - BETA_ONE**STEP)
    second_hat = second_new / (1.0 - BETA_TWO**STEP)
    master_new = master - step_rate * (
        first_hat / (jnp.sqrt(second_hat) + ADAM_EPS) + decay_rate * master
    )
    return (master_new, first_new, second_new)


def update_kernel(cuts, *refs):
    shares, refs = refs[:5], refs[5:]
    att, expand, reduce, norm, refs = refs[:3], refs[3:6], refs[6:9], refs[9:12], refs[12:]
    carried, refs = refs[:3], refs[3:]
    att_out, expand_out, reduce_out, norm_out, refs = refs[:3], refs[3:6], refs[6:9], refs[9:12], refs[12:]
    size_out, carried_out = refs[0], refs[1:4]
    att_share, expand_share, reduce_share, totals, local_squares = shares
    step = pl.program_id(0)
    for a, b in zip(carried, carried_out):
        b[...] = a[...]
    norm_total = totals[:6]
    squares = local_squares[:1, :1] + jnp.sum(norm_total * norm_total).reshape(1, 1)
    size = jnp.sqrt(squares)
    clip = jnp.minimum(1.0, MAX_NORM / (size + 1e-06))

    def write(outs, values):
        for out, value in zip(outs, values):
            out[...] = value

    write(att_out, adam_step(*(v[...] for v in att), att_share[...] * clip[None], MATRIX_RATE, DECAY_RATE))
    write(expand_out, adam_step(*(v[...] for v in expand), expand_share[0] * clip, MATRIX_RATE, DECAY_RATE))
    write(reduce_out, adam_step(*(v[...] for v in reduce), reduce_share[0].T * clip, MATRIX_RATE, DECAY_RATE))

    @pl.when(step == cuts - 1)
    def _():
        size_out[...] = size
        write(norm_out, adam_step(*(v[...] for v in norm), norm_total * clip, NORM_RATE, 0.0))


def update(back, attention, expand, reduce, norm):
    cuts = 4
    _, row_block, col_block = attention[0].shape
    ff_block = expand[0].shape[1]
    att_spec = pl.BlockSpec((1, row_block, col_block), lambda j: (j, 0, 0))
    expand_spec = pl.BlockSpec((row_block // cuts, ff_block), lambda j: (j, 0))
    reduce_spec = pl.BlockSpec((ff_block // cuts, row_block), lambda j: (j, 0))
    norm_spec = pl.BlockSpec(norm[0].shape, lambda j: (0, 0))
    shapes = [*attention, *expand, *reduce, *norm]
    specs = [att_spec] * 3 + [expand_spec] * 3 + [reduce_spec] * 3 + [norm_spec] * 3
    carried = [back.resampled, back.media_grad.reshape(-1, D), back.latent_grad]
    carried_specs = [pl.BlockSpec((v.shape[0] // cuts, D), lambda j: (j, 0)) for v in carried]
    out_shape = [jax.ShapeDtypeStruct(v.shape, v.dtype) for v in shapes]
    out_shape += [jax.ShapeDtypeStruct((1, 1), F32)]
    out_shape += [jax.ShapeDtypeStruct(v.shape, v.dtype) for v in carried]
    made = pl.pallas_call(
        functools.partial(update_kernel, cuts),
        grid=(cuts,),
        out_shape=out_shape,
        in_specs=[
            att_spec,
            pl.BlockSpec((1, row_block // cuts, ff_block), lambda j: (0, j, 0)),
            pl.BlockSpec((1, row_block, ff_block // cuts), lambda j: (1, 0, j)),
            pl.BlockSpec((8, D), lambda j: (0, 0)),
            pl.BlockSpec((8, 128), lambda j: (0, 0)),
            *specs,
            *carried_specs,
        ],
        out_specs=[*specs, pl.BlockSpec((1, 1), lambda j: (0, 0)), *carried_specs],
        compiler_params=pltpu.CompilerParams(vmem_limit_bytes=63 * MIB),
        name="update_kernel",
    )(back.att_share, back.ff_share, back.ff_share, back.totals, back.squares, *shapes, *carried)
    return made[:12], made[12], made[13:]


def on_device(
    media_tokens,
    latents,
    cotangent,
    counts,
    attention_weights,
    attention_first,
    attention_second,
    expand_weight,
    expand_first,
    expand_second,
    reduce_weight,
    reduce_first,
    reduce_second,
    norm_params,
    norm_first,
    norm_second,
):
    _, row_block, col_block = attention_weights.shape
    got = forward(
        attention_weights,
        expand_weight,
        reduce_weight,
        media_tokens,
        latents,
        cotangent,
        counts,
        norm_params,
    )
    back = backward(
        got, media_tokens, latents, counts, norm_params, row_block, col_block, expand_weight.shape[1]
    )
    made, size, (resampled, media_grad, latent_grad) = update(
        back,
        (attention_weights, attention_first, attention_second),
        (expand_weight, expand_first, expand_second),
        (reduce_weight, reduce_first, reduce_second),
        (norm_params, norm_first, norm_second),
    )
    return (
        resampled.reshape(latents.shape),
        media_grad.reshape(media_tokens.shape),
        latent_grad.reshape(latents.shape),
        size.reshape(()),
        *made,
    )


def solution(mesh):
    in_specs = (
        P(("dp", "head"), None, None),
        P(("dp", "head"), None, None),
        P(("dp", "head"), None, None),
        P("dp"),
        P(None, "dp", "head"),
        P(None, "dp", "head"),
        P(None, "dp", "head"),
        P("dp", "head"),
        P("dp", "head"),
        P("dp", "head"),
        P("head", "dp"),
        P("head", "dp"),
        P("head", "dp"),
        P(),
        P(),
        P(),
    )
    out_specs = (
        P(("dp", "head"), None, None),
        P(("dp", "head"), None, None),
        P(("dp", "head"), None, None),
        P(),
        P(None, "dp", "head"),
        P(None, "dp", "head"),
        P(None, "dp", "head"),
        P("dp", "head"),
        P("dp", "head"),
        P("dp", "head"),
        P("head", "dp"),
        P("head", "dp"),
        P("head", "dp"),
        P(),
        P(),
        P(),
    )
    return jax.shard_map(
        on_device, mesh=mesh, in_specs=in_specs, out_specs=out_specs, check_vma=False
    )
```

```python
import functools
from types import SimpleNamespace

import jax
import jax.numpy as jnp
from jax import lax
from jax.experimental import pallas as pl
from jax.experimental.pallas import tpu as pltpu
from jax.sharding import PartitionSpec as P

D = 1024
HEADS = 16
HEAD = D // HEADS
GROUP = 256
GROUPS = D // GROUP
STEP = 10

LN_EPS = 1e-05
BETA_ONE = 0.9
BETA_TWO = 0.999
ADAM_EPS = 1e-08
MATRIX_RATE = 0.1
NORM_RATE = 0.6
DECAY_RATE = 0.1
MAX_NORM = 0.05

MESH = pl.DeviceIdType.MESH
F32 = jnp.float32
BF16 = jnp.bfloat16
MIB = 2**20
EARLY = 2


def grid_of(dp_count, head_count):
    x = 1
    while 4 * x * x <= dp_count:
        x *= 2
    return {"z": dp_count // x, "x": x, "y": head_count // 2, "c": 2}


class Links:
    def __init__(self, sizes, send, recv, local):
        self.sizes, self.send, self.recv, self.local = sizes, send, recv, local
        self.used = self.used_local = 0
        dp, head = lax.axis_index("dp"), lax.axis_index("head")
        self.at = {
            "z": lax.div(dp, sizes["x"]),
            "x": lax.rem(dp, sizes["x"]),
            "y": lax.div(head, sizes["c"]),
            "c": lax.rem(head, sizes["c"]),
        }
        self.head = head

    def place(self, axis, k):
        return lax.rem(self.at[axis] + k, self.sizes[axis])

    def peer(self, steps):
        at = dict(self.at)
        for axis, k in steps.items():
            at[axis] = self.place(axis, k)
        return {
            "dp": at["z"] * self.sizes["x"] + at["x"],
            "head": at["y"] * self.sizes["c"] + at["c"],
        }

    def around(self, axes):
        ways = [{}]
        for axis in axes:
            ways = [{**way, axis: k} for way in ways for k in range(self.sizes[axis])]
        return ways[1:]

    def greet(self, *groups):
        barrier = pltpu.get_barrier_semaphore()
        self.met = [way for axes in groups for way in self.around(axes)]
        for way in self.met:
            pl.semaphore_signal(barrier, inc=1, device_id=self.peer(way), device_id_type=MESH)

    def meet(self):
        pl.semaphore_wait(pltpu.get_barrier_semaphore(), len(self.met))

    def copy(self, src, dst, slot, axis, k):
        return self.send_to(src, dst, slot, {axis: k})

    def send_to(self, src, dst, slot, way):
        return pltpu.make_async_remote_copy(
            src_ref=src,
            dst_ref=dst,
            send_sem=self.send.at[slot],
            recv_sem=self.recv.at[slot],
            device_id=self.peer(way),
            device_id_type=MESH,
        )

    def take(self):
        self.used += 1
        return self.used - 1

    def move(self, src, dst):
        self.used_local += 1
        made = pltpu.make_async_copy(src, dst, self.local.at[self.used_local - 1])
        made.start()
        return made


class Gather:
    def __init__(self, links, order, view):
        self.links, self.order, self.view = links, order, view
        self.sent, self.coming = [], {}

    def region(self, step, place):
        at = dict(self.links.at)
        for axis in self.order[:step]:
            at[axis] = None
        at[self.order[step]] = place
        return self.view(at)

    def start(self, step):
        axis, links = self.order[step], self.links
        mine = self.region(step, links.at[axis])
        self.coming[step] = []
        for k in range(1, links.sizes[axis]):
            slot = links.take()
            copy = links.copy(mine, mine, slot, axis, k)
            copy.start()
            self.sent.append(copy)
            lands = self.region(step, links.place(axis, links.sizes[axis] - k))
            self.coming[step].append(links.copy(lands, lands, slot, axis, k))

    def wait(self, step):
        for copy in self.coming[step]:
            copy.wait_recv()

    def go(self, step):
        self.wait(step)
        if step + 1 < len(self.order):
            self.start(step + 1)

    def close(self):
        for copy in self.sent:
            copy.wait_send()


def some(place):
    return slice(None) if place is None else place


def dot(a, b):
    return lax.dot_general(a, b, (((1,), (0,)), ((), ())), preferred_element_type=F32)


def dot_nt(a, b):
    return lax.dot_general(a, b, (((1,), (1,)), ((), ())), preferred_element_type=F32)


def dot_tn(a, b):
    return lax.dot_general(a, b, (((0,), (0,)), ((), ())), preferred_element_type=F32)


def normed(values):
    center = values - jnp.mean(values, axis=-1, keepdims=True)
    scale = lax.rsqrt(jnp.mean(center * center, axis=-1, keepdims=True) + LN_EPS)
    return center * scale, scale


def norm_back(up, hat, scale, gain):
    inner = up * gain
    return scale * (
        inner
        - jnp.mean(inner, axis=-1, keepdims=True)
        - hat * jnp.mean(inner * hat, axis=-1, keepdims=True)
    )


def fold(rows):
    return jnp.sum(rows.reshape(rows.shape[0] // 8, 8, rows.shape[1]), axis=0)


def gelu_and_slope(v):
    root = 0.7978845608028654
    square = v * v
    t = jnp.tanh(root * v * (1.0 + 0.044715 * square))
    half = 0.5 + 0.5 * t
    slope = half + (0.5 * root) * v * (1.0 - t * t) * (1.0 + (3.0 * 0.044715) * square)
    return v * half, slope


def diagonal(rows):
    n = GROUP // HEAD
    lat = rows.shape[0]
    tall = jnp.concatenate([rows] * n, axis=0)
    row = lax.broadcasted_iota(jnp.int32, tall.shape, 0) // lat
    col = lax.broadcasted_iota(jnp.int32, tall.shape, 1) // HEAD
    return jnp.where(row == col, tall, jnp.zeros_like(tall))


def undiagonal(tall):
    n = GROUP // HEAD
    lat = tall.shape[0] // n
    col = lax.broadcasted_iota(jnp.int32, (lat, GROUP), 1) // HEAD
    total = jnp.where(col == 0, tall[:lat], 0.0)
    for h in range(1, n):
        total = total + jnp.where(col == h, tall[h * lat : (h + 1) * lat], 0.0)
    return total


def weight_block(weights, m, g, sizes):
    block = weights.shape[-1]
    per = GROUP // block
    parts = []
    for s in range(per):
        h = g * per + s
        part = weights[m, lax.div(h, sizes["c"]), lax.rem(h, sizes["c"])]
        parts.append(part.reshape(D, block))
    return parts[0] if per == 1 else jnp.concatenate(parts, axis=1)


def softmax_columns(keys, spread_queries, seen):
    scores = dot_nt(keys, spread_queries)
    scores = jnp.where(seen, scores, -1e30)
    raised = jnp.exp(scores - jnp.max(scores, axis=0, keepdims=True))
    return raised * (1.0 / jnp.sum(raised, axis=0, keepdims=True))


def forward_kernel(
    sizes,
    att_ref,
    expand_ref,
    reduce_ref,
    tokens_ref,
    latents_ref,
    cotangent_ref,
    counts_ref,
    norm_ref,
    att_out,
    pairs_out,
    turned_out,
    queries_out,
    mixed_out,
    ff_grad_out,
    added_out,
    middle_out,
    middle_grad_out,
    branch_out,
    ff_norm_out,
    att,
    pairs,
    turned,
    queries,
    mixed,
    ff,
    added,
    middle,
    middle_grad,
    branch,
    ff_norm,
    rows,
    back,
    hid,
    bg,
    part,
    land_c,
    land_y,
    land_x,
    tokens,
    inputs,
    send,
    recv,
    local,
):
    links = Links(sizes, send, recv, local)
    links.greet(*"zxyc")
    images, span, _ = inputs.shape
    patches = tokens_ref.shape[1]
    lat = span - patches
    at = links.at
    outs = []

    loads = {}

    def fetch(i):
        if i < images:
            loads[i] = links.move(tokens_ref.at[i], tokens.at[i % 2])

    fetch(0)
    fetch(1)
    for m in range(4):
        att[m, at["y"], at["c"], at["z"], at["x"]] = att_ref[m].astype(BF16)
    back[at["y"], at["c"]] = cotangent_ref[...].astype(BF16)
    quarters, tile = ff.shape[0], ff.shape[-1]
    for q in range(quarters):
        ff[q, 0, at["z"], at["x"]] = expand_ref[:, q * tile : (q + 1) * tile].astype(BF16)
        ff[q, 1, at["z"], at["x"]] = reduce_ref[q * tile : (q + 1) * tile].T.astype(BF16)

    half = att.shape[5] // 2

    def att_view(m, s):
        def view(p):
            return att.at[m, some(p["y"]), some(p["c"]), some(p["z"]), some(p["x"]), pl.ds(s * half, half)]

        return view

    def ff_view(q, m):
        def view(p):
            return ff.at[q, m, some(p["z"]), some(p["x"])]

        return view

    def back_view(p):
        return back.at[some(p["y"]), some(p["c"])]

    def row_view(i):
        def view(p):
            return rows.at[some(p["y"]), some(p["c"]), pl.ds(i * lat, lat)]

        return view

    query, key, value, output = ([Gather(links, "zxyc", att_view(m, s)) for s in range(2)] for m in range(4))
    hidden = [Gather(links, "zx", ff_view(q, m)) for q in range(quarters) for m in range(2)]
    cotangent = [Gather(links, "yc", back_view)]
    ff_rows = [Gather(links, "yc", row_view(i)) for i in range(images)]
    everything = [*query, *key, *value, *output, *hidden, *cotangent, *ff_rows]

    def start(parts):
        for part in parts:
            part.start(0)

    def go(parts, step):
        for part in parts:
            part.go(step)

    links.meet()
    start(cotangent + key + value + hidden[:1] + query + hidden[1:2] + output)

    for i in range(images):
        low = normed(latents_ref[pl.ds(i * lat, lat)].astype(F32))[0] * norm_ref[2:3] + norm_ref[3:4]
        inputs[i, pl.ds(patches, lat)] = low.astype(BF16)

    def normalize(i):
        loads[i].wait()
        some_rows = 64

        def one(t, _):
            part = pl.ds(pl.multiple_of(t * some_rows, some_rows), some_rows)
            low = normed(tokens[i % 2, part].astype(F32))[0] * norm_ref[0:1] + norm_ref[1:2]
            inputs[i, part] = low.astype(BF16)
            return 0

        lax.fori_loop(0, patches // some_rows, one, 0)
        fetch(i + 2)

    turning = {}

    def turn(i):
        if i >= 2:
            turning[i - 2].wait()

        def one(t, _):
            part = pl.ds(pl.multiple_of(t * 128, 128), 128)
            turned[i % 2, :, part] = inputs[i, part].T
            return 0

        lax.fori_loop(0, span // 128, one, 0)
        turning[i] = links.move(turned.at[i % 2], turned_out.at[:, pl.ds(i * span, span)])

    k0, k1, v0, v1, q0, q1, o0, o1 = *key, *value, *query, *output
    f = [*hidden, *[None] * (8 - len(hidden))]
    steps = []

    def plan(*ticks):
        steps.extend(ticks)

    plan(
        [(k0, 0)],
        [(k1, 0)],
        [(k0, 1), (v0, 0)],
        [(k1, 1), (v1, 0)],
        [(v0, 1)],
        [(k0, 2), (v1, 1)],
        [(f[0], 0)],
        [(k1, 2), (q0, 0)],
    )

    def tick():
        for part, step in steps.pop(0) if steps else ():
            if part is not None:
                part.go(step)
            if part in hidden:
                start(hidden[hidden.index(part) + 2 :][:1])

    def rest():
        while steps:
            tick()

    for i in range(images):
        normalize(i)
        tick()
        turn(i)
        tick()
    plan([(q1, 0), (v0, 2), (q0, 1)])
    rest()
    for i in range(max(0, images - 2), images):
        turning[i].wait()
    go(key, 3)

    def project(i, m):
        def one(g, _):
            weight = weight_block(att, m, g, sizes)
            pairs[i, (m - 1) * GROUPS + g] = dot(inputs[i], weight).astype(BF16)
            return 0

        lax.fori_loop(0, GROUPS, one, 0)

    def attend(i):
        position = lax.broadcasted_iota(jnp.int32, (span, GROUP), 0)
        count = counts_ref[links.head * images + i]
        seen = (position < count) | (position >= patches)

        def one(g, _):
            spread = diagonal(queries[g, pl.ds(i * lat, lat)])
            probs = softmax_columns(pairs[i, g], spread, seen).astype(BF16)
            wide = dot_tn(probs, pairs[i, GROUPS + g])
            mixed[g, pl.ds(i * lat, lat)] = undiagonal(wide).astype(BF16)
            return 0

        lax.fori_loop(0, GROUPS, one, 0)

    def finish(i):
        part = pl.ds(i * lat, lat)
        whole = jnp.concatenate([mixed[g, part] for g in range(GROUPS)], axis=1)
        made = jnp.concatenate(
            [dot(whole, weight_block(att, 3, g, sizes)) for g in range(GROUPS)], axis=1
        )
        value = latents_ref[part].astype(F32) + made
        middle[part] = value
        low = normed(value)[0] * norm_ref[4:5] + norm_ref[5:6]
        rows[at["y"], at["c"], part] = low.astype(BF16)
        ff_rows[i].start(0)

    plan([], [(q1, 1)], [(f[1], 0)], [(v1, 2)])
    for i in range(images):
        project(i, 1)
        tick()
    plan([(o0, 0), (q0, 2), (o1, 0)])
    rest()
    go(value, 3)
    plan([(o0, 1)], [(q1, 2)], [(f[2], 0), (o1, 1)], [(f[3], 0)])
    for i in range(images):
        project(i, 2)
        outs.append(links.move(pairs.at[i], pairs_out.at[i]))
        tick()
    plan([(o0, 2)])
    rest()
    go(query, 3)
    stack = inputs[:, patches:].reshape(images * lat, D)
    for g in range(GROUPS):
        made = dot(stack, weight_block(att, 0, g, sizes)) * HEAD ** (-0.5)
        queries[g] = made.astype(BF16)
    outs.append(links.move(queries, queries_out))
    plan([(f[4], 0)], [(o1, 2)], [(f[5], 0)])
    for i in range(images):
        attend(i)
        tick()
    rest()
    go(output, 3)
    outs.append(links.move(att, att_out))
    outs.append(links.move(mixed, mixed_out))
    plan([], [(f[6], 0)], [(cotangent[0], 0)], [(f[7], 0)])
    for i in range(images):
        finish(i)
        tick()
    rest()
    outs.append(links.move(middle, middle_out))
    go(cotangent, 1)
    go(ff_rows, 0)
    n = images * lat
    cs, ys, zs = (sizes[a] for a in "cyz")
    sib = links.place("c", 1)
    xr = sizes["x"] * att.shape[5]

    def first(q):
        def one(yi, _):
            before = dot(rows[yi].reshape(cs * n, D), ff[q, 0].reshape(D, tile))
            up = dot(back[yi].reshape(cs * n, D), ff[q, 1].reshape(D, tile))
            made, slope = gelu_and_slope(before)
            hid[yi, :, :, q * tile : (q + 1) * tile] = made.astype(BF16).reshape(cs, n, tile)
            bg[yi, :, :, q * tile : (q + 1) * tile] = (up * slope).astype(BF16).reshape(cs, n, tile)
            return 0

        lax.fori_loop(0, ys, one, 0)

    go(ff_rows, 1)
    for q in range(quarters):
        go(hidden[2 * q : 2 * q + 2], 1)
        first(q)

    ff_block = quarters * tile

    def second(kind, yi):
        wide = (hid if kind else bg)[yi].reshape(cs * n, ff_block)
        made = added if kind else part

        def one(z, _):
            cols = pl.ds(pl.multiple_of(z * xr, xr), xr)
            weight = jnp.concatenate([ff[q, kind, z].reshape(xr, tile) for q in range(quarters)], axis=1)
            made[yi, :, :, cols] = dot_nt(wide, weight).astype(BF16).reshape(cs, n, xr)
            return 0

        lax.fori_loop(0, zs, one, 0)

    sent, chip, along = [], {}, {}
    for k in [*range(1, ys), 0]:
        yi = links.place("y", k)
        second(0, yi)
        slot = links.take()
        land = land_c.at[yi]
        copy = links.copy(part.at[yi, sib], land, slot, "c", 1)
        copy.start()
        sent.append(copy)
        chip[k] = links.copy(land, land, slot, "c", 1)
    for k in range(1, ys):
        yi = links.place("y", k)
        chip[k].wait_recv()
        summed = part[yi, at["c"]].astype(F32) + land_c[yi].astype(F32)
        part[yi, at["c"]] = summed.astype(BF16)
        slot = links.take()
        land = land_y.at[k - 1]
        copy = links.copy(part.at[yi, at["c"]], land, slot, "y", k)
        copy.start()
        sent.append(copy)
        along[k] = links.copy(land, land, slot, "y", k)
    for gather in hidden:
        gather.close()

    def gradient(m, z):
        left, right = (back, hid) if m else (rows, bg)
        cols = pl.ds(pl.multiple_of(z * xr, xr), xr)
        made = dot_tn(
            left[:, :, :, cols].reshape(ys * cs * n, xr), right[...].reshape(ys * cs * n, ff_block)
        ).astype(BF16)
        for q in range(quarters):
            ff[q, m, z] = made[:, q * tile : (q + 1) * tile].reshape(*ff.shape[3:5], tile)

    xs = sizes["x"]
    early = range(1, 1 + land_x.shape[0])
    x_slots = {k: [links.take() for _ in range(1, xs)] for k in early}

    def x_copies(k):
        for j, slot in enumerate(x_slots[k], 1):
            block = ff.at[:, 0, links.place("z", k), links.place("x", j)]
            yield links.copy(block, land_x.at[k - 1, j - 1], slot, "x", j)

    for k in early:
        gradient(0, links.place("z", k))
        for copy in x_copies(k):
            copy.start()
    for yi in range(ys):
        second(1, yi)
    outs.append(links.move(added, added_out))

    def other(k, _):
        gradient(0, links.place("z", k))
        return 0

    lax.fori_loop(1 + len(early), zs + 1, other, 0)

    def both(z, _):
        gradient(1, z)
        return 0

    lax.fori_loop(0, zs, both, 0)
    chip[0].wait_recv()
    for k in range(1, ys):
        along[k].wait_recv()

    def back_one(t, carry):
        gain, shift = carry
        rws = pl.ds(pl.multiple_of(t * lat, lat), lat)
        up = part[at["y"], at["c"], rws].astype(F32) + land_c[at["y"], rws].astype(F32)
        for k in range(1, ys):
            up = up + land_y[k - 1, rws].astype(F32)
        hat, scale = normed(middle[rws])
        value = cotangent_ref[rws] + norm_back(up, hat, scale, norm_ref[4:5])
        middle_grad[rws] = value
        branch[rws] = value.astype(BF16)
        return gain + fold(up * hat), shift + fold(up)

    zero = jnp.zeros((8, D), F32)
    ff_norm[0], ff_norm[1] = lax.fori_loop(0, images, back_one, (zero, zero))
    outs.append(links.move(middle_grad, middle_grad_out))
    outs.append(links.move(branch, branch_out))
    outs.append(links.move(ff_norm, ff_norm_out))
    for k in early:
        for copy in x_copies(k):
            copy.wait_recv()
        z = links.place("z", k)
        for q in range(quarters):
            total = ff[q, 0, z, at["x"]].astype(F32)
            for j in range(xs - 1):
                total = total + land_x[k - 1, j, q].astype(F32)
            ff[q, 0, z, at["x"]] = total.astype(BF16)
        for copy in x_copies(k):
            copy.wait_send()
    outs.append(links.move(ff, ff_grad_out))
    for copy in sent:
        copy.wait_send()
    for gather in everything:
        if gather not in hidden:
            gather.close()
    for out in outs:
        out.wait()


def forward(att, expand, reduce, tokens, latents, cotangent, counts, norm_params):
    sizes = grid_of(lax.axis_size("dp"), lax.axis_size("head"))
    z, x, y, c = (sizes[a] for a in "zxyc")
    images, patches, _ = tokens.shape
    lat = latents.shape[1]
    span = patches + lat
    n = images * lat
    _, row_block, col_block = att.shape
    ff_block = expand.shape[1]
    tile = min(GROUP, ff_block)
    quarters = ff_block // tile
    shapes = dict(
        att=((4, y, c, z, x, row_block, col_block), BF16),
        pairs=((images, 2 * GROUPS, span, GROUP), BF16),
        turned=((D, images * span), BF16),
        queries=((GROUPS, n, GROUP), BF16),
        mixed=((GROUPS, n, GROUP), BF16),
        ff=((quarters, 2, z, x, row_block, tile), BF16),
        added=((y, c, n, D), BF16),
        middle=((n, D), F32),
        middle_grad=((n, D), F32),
        branch=((n, D), BF16),
        ff_norm=((2, 8, D), F32),
    )
    held = dict(shapes)
    held.update(turned=((2, D, span), BF16))
    inside = [
        ((y, c, n, D), BF16),
        ((y, c, n, D), BF16),
        ((y, c, n, ff_block), BF16),
        ((y, c, n, ff_block), BF16),
        ((y, c, n, D), BF16),
        ((y, n, D), BF16),
        ((y - 1, n, D), BF16),
        ((EARLY, x - 1, quarters, row_block, tile), BF16),
        ((2, patches, D), BF16),
        ((images, span, D), BF16),
    ]
    per_att = sum(s - 1 for s in sizes.values())
    slots = 8 * per_att + 8 * (z + x - 2) + (1 + images) * (y + c - 2) + 2 * y + EARLY * x
    vmem, anywhere = pl.BlockSpec(memory_space=pltpu.VMEM), pl.BlockSpec(memory_space=pl.ANY)
    made = pl.pallas_call(
        functools.partial(forward_kernel, sizes),
        out_shape=[jax.ShapeDtypeStruct(*v) for v in shapes.values()],
        in_specs=[vmem, vmem, vmem, anywhere, vmem, vmem, pl.BlockSpec(memory_space=pltpu.SMEM), vmem],
        out_specs=[anywhere] * len(shapes),
        scratch_shapes=[pltpu.VMEM(*v) for v in [*held.values(), *inside]]
        + [
            pltpu.SemaphoreType.DMA((slots,)),
            pltpu.SemaphoreType.DMA((slots,)),
            pltpu.SemaphoreType.DMA((2 * images + 20,)),
        ],
        compiler_params=pltpu.CompilerParams(
            collective_id=0, has_side_effects=True, vmem_limit_bytes=63 * MIB + 900 * 1024
        ),
        name="gather_and_attend",
    )(att, expand, reduce, tokens, latents.reshape(n, D), cotangent.reshape(n, D), counts, norm_params)
    return SimpleNamespace(**dict(zip(shapes, made)))


class Scatter:
    def __init__(self, links, order, view, lands):
        self.links, self.order, self.view, self.lands = links, order, view, lands
        self.slots = {}

    def region(self, step, place):
        at = dict(self.links.at)
        for axis in self.order[step + 1 :]:
            at[axis] = None
        at[self.order[step]] = place
        return self.view(at)

    def copies(self, step):
        axis, links = self.order[step], self.links
        for k, slot in enumerate(self.slots[step], 1):
            yield links.copy(self.region(step, links.place(axis, k)), self.lands[step][k - 1], slot, axis, k)

    def start(self, step):
        self.slots[step] = [self.links.take() for _ in range(1, self.links.sizes[self.order[step]])]
        for copy in self.copies(step):
            copy.start()

    def wait(self, step):
        for k, slot in enumerate(self.slots[step], 1):
            land = self.lands[step][k - 1]
            self.links.copy(land, land, slot, self.order[step], k).wait_recv()

    def add(self, step, out=None):
        mine = self.region(step, self.links.at[self.order[step]])
        lands = self.lands[step]
        lead = mine.shape[0] if len(mine.shape) > 2 else None

        def total(at):
            value = mine[at].astype(F32)
            for land in lands:
                value = value + land[at].astype(F32)
            return value

        if out is not None:
            out[...] = total(Ellipsis)
        elif lead is None:
            mine[...] = total(Ellipsis).astype(BF16)
        else:

            def one(t, _):
                mine[t] = total(t).astype(BF16)
                return 0

            lax.fori_loop(0, lead, one, 0)

    def go(self, step, out=None):
        self.wait(step)
        self.add(step, out)
        if step + 1 < len(self.order):
            self.start(step + 1)

    def close(self):
        for step in self.slots:
            for copy in self.copies(step):
                copy.wait_send()


ATT_ORDERS = {0: ("yxz", "yxz"), 1: ("yxz", "xyz"), 2: ("yxz", "xyz"), 3: ("yxz", "yxz")}


def land_shapes(sizes, order, axes, tail):
    shapes, left = [], list(axes)
    for axis in order:
        left.remove(axis)
        shapes.append((sizes[axis] - 1, *(sizes[a] for a in left), *tail))
    return shapes


def backward_kernel(sizes, dims, *refs):
    names, keys, images, patches, lat, ff_block = dims
    r = SimpleNamespace(**dict(zip(names, refs)))
    total_lands = dict(zip("cyxz", refs[len(names) :]))
    r.square_lands = refs[len(names) + 4 : len(names) + 6]
    att_lands = dict(zip(keys, refs[len(names) + 6 :]))
    links = Links(sizes, r.send, r.recv, r.local)
    links.greet("zx", "yc")
    at = links.at
    sib = links.place("c", 1)
    n = images * lat
    span = patches + lat
    zs, xs, ys, cs = (sizes[a] for a in "zxyc")
    row_block, col_block = r.att_share.shape[1:]
    xr = xs * row_block
    heads = ys * cs
    half = row_block // 2
    norm_ref, latents = r.norm, r.latents
    queries, mixed = r.queries, r.mixed
    grads_ff = r.grads_ff
    middle_grad, branch, latent_low = r.middle_grad, r.branch, r.latent_low
    mixed_grad, query_back = r.mixed_grad, r.query_back
    outs = []

    units = [(m, k) for k in [*range(1, zs), 0] for m in range(2)]
    ready = [(0, k) for k in range(1, 1 + EARLY)]
    units = [unit for unit in units if unit not in ready]
    x_slots = {unit: [links.take() for _ in range(1, xs)] for unit in units}
    z_slots = {unit: links.take() for unit in units + ready if unit[1]}

    def x_copies(unit):
        m, k = unit
        z = links.place("z", k)
        for j, slot in enumerate(x_slots[unit], 1):
            yield links.copy(
                grads_ff.at[:, m, z, links.place("x", j)], r.ff_land_x.at[m, z, j - 1], slot, "x", j
            )

    def z_copy(unit):
        m, k = unit
        return links.copy(
            grads_ff.at[:, m, links.place("z", k), at["x"]], r.ff_land_z.at[m, k - 1], z_slots[unit], "z", k
        )

    quarters, tile = grads_ff.shape[0], grads_ff.shape[-1]

    def ff_along(unit):
        m, k = unit
        z = links.place("z", k)
        for copy in x_copies(unit):
            copy.wait_recv()
        for q in range(quarters):
            total = grads_ff[q, m, z, at["x"]].astype(F32)
            for j in range(xs - 1):
                total = total + r.ff_land_x[m, z, j, q].astype(F32)
            if k:
                grads_ff[q, m, z, at["x"]] = total.astype(BF16)
            else:
                r.ff_share[m, :, q * tile : (q + 1) * tile] = total
        if k:
            z_copy(unit).start()

    def ff_finish():
        for m in range(2):
            for k in range(1, zs):
                z_copy((m, k)).wait_recv()
            for q in range(quarters):
                cols = pl.ds(q * tile, tile)
                total = r.ff_share[m, :, cols]
                for k in range(1, zs):
                    total = total + r.ff_land_z[m, k - 1, q].astype(F32)
                r.ff_share[m, :, cols] = total

    pairs = r.pairs_here
    early = [links.move(r.pairs.at[i], pairs.at[i]) for i in range(images)]

    load = links.move(r.ff_grad, grads_ff)
    own = links.move(r.added.at[:, at["c"]], r.added_here)
    links.meet()
    load.wait()
    for unit in units:
        for copy in x_copies(unit):
            copy.start()
    for unit in ready:
        z_copy(unit).start()

    c_slots = [links.take() for _ in range(ys)]
    y_slots = [links.take() for _ in range(1, ys)]

    def added_chip(k):
        yi = links.place("y", k)
        return links.copy(r.added.at[yi, sib], r.added_land_c.at[yi], c_slots[k], "c", 1)

    def added_along(k):
        return links.copy(r.added_here.at[links.place("y", k)], r.added_land_y.at[k - 1], y_slots[k - 1], "y", k)

    for k in range(ys):
        added_chip(k).start()
    own.wait()

    def added_out():
        for k in range(1, ys):
            yi = links.place("y", k)
            added_chip(k).wait_recv()
            summed = r.added_here[yi].astype(F32) + r.added_land_c[yi].astype(F32)
            r.added_here[yi] = summed.astype(BF16)
            added_along(k).start()

    resampled_low = r.added_here.at[at["y"]]

    def added_finish():
        added_chip(0).wait_recv()
        for k in range(1, ys):
            added_along(k).wait_recv()

        def one(t, _):
            rws = pl.ds(pl.multiple_of(t * lat, lat), lat)
            up = r.added_here[at["y"], rws].astype(F32) + r.added_land_c[at["y"], rws].astype(F32)
            for k in range(1, ys):
                up = up + r.added_land_y[k - 1, rws].astype(F32)
            resampled_low[rws] = (r.middle[rws] + up).astype(BF16)
            return 0

        lax.fori_loop(0, images, one, 0)
        for k in range(ys):
            added_chip(k).wait_send()
        for k in range(1, ys):
            added_along(k).wait_send()
        return links.move(resampled_low, r.resampled)

    r.norm_parts[4] = r.ff_norm[0]
    r.norm_parts[5] = r.ff_norm[1]

    steps = []

    def tick():
        if steps:
            steps.pop(0)()

    def plan(*calls):
        steps.append(lambda: [f(*args) for f, *args in calls])

    waiting = []

    def attention(grads, turned_left):
        per = GROUP // col_block
        block_slots = {m: [links.take() for _ in range(ys)] for m in range(4)}

        def block_copy(m, yi):
            slot = block_slots[m][0] + yi
            return links.copy(grads.at[m, yi, sib], r.att_land_c.at[m, yi], slot, "c", 1)

        def att_scatter(m, s):
            def view(p):
                return grads.at[m, some(p["y"]), at["c"], some(p["z"]), some(p["x"]), pl.ds(s * half, half)]

            order = ATT_ORDERS[m][s]
            lands = [
                [att_lands[m, s, step].at[k] for k in range(sizes[axis] - 1)]
                for step, axis in enumerate(order)
            ]
            return Scatter(links, order, view, lands)

        scatter = {m: [att_scatter(m, s) for s in range(2)] for m in range(4)}

        def go(m, step):
            for s, part in enumerate(scatter[m]):
                part.go(step, r.att_share.at[m, pl.ds(s * half, half)] if step == 2 else None)

        def chip_sum(m):
            for yi in range(ys):
                block_copy(m, yi).wait_recv()

                def one(z, _):
                    value = grads[m, yi, at["c"], z].astype(F32) + r.att_land_c[m, yi, z].astype(F32)
                    grads[m, yi, at["c"], z] = value.astype(BF16)
                    return 0

                lax.fori_loop(0, zs, one, 0)
            for part in scatter[m]:
                part.start(0)

        def products(m, left, right, between=None):
            def of(ci, send):
                def one(yi, _):
                    made = dot(left(), right(yi * cs + ci)).astype(BF16)
                    grads[m, yi, ci] = made.reshape(zs, xs, row_block, col_block)
                    if send:
                        block_copy(m, yi).start()
                    return 0

                lax.fori_loop(0, ys, one, 0)

            of(sib, True)
            if between is not None:
                between()
            of(at["c"], False)

        def query_columns(h):
            j = lax.div(h * col_block, GROUP)
            if per == 1:
                return query_back[j]
            off = pl.multiple_of(lax.rem(h, per) * col_block, col_block)
            return query_back[j, :, pl.ds(off, col_block)]

        def columns(m):
            def right(h):
                j = lax.div(h * col_block, GROUP) + (m - 1) * GROUPS
                if per == 1:
                    return pairs[:, j].reshape(images * span, GROUP)
                off = pl.multiple_of(lax.rem(h, per) * col_block, col_block)
                return pairs[:, j, :, pl.ds(off, col_block)].reshape(images * span, col_block)

            return right

        def attend(i):
            position = lax.broadcasted_iota(jnp.int32, (span, GROUP), 0)
            count = r.counts[links.head * images + i]
            seen = (position < count) | (position >= patches)
            rws = pl.ds(i * lat, lat)

            def one(g, _):
                keys, values = pairs[i, g], pairs[i, GROUPS + g]
                spread = diagonal(queries[g, rws])
                probs = softmax_columns(keys, spread, seen)
                upstream = diagonal(mixed_grad[g, rws])
                prob_grad = dot_nt(values, upstream)
                inner = jnp.sum(probs * prob_grad, axis=0, keepdims=True)
                score_grad = (probs * (prob_grad - inner)).astype(BF16)
                back = undiagonal(dot_tn(score_grad, keys)) * HEAD ** (-0.5)
                query_back[g, rws] = back.astype(BF16)
                pairs[i, GROUPS + g] = dot(probs.astype(BF16), upstream).astype(BF16)
                pairs[i, g] = dot(score_grad, spread).astype(BF16)
                return 0

            lax.fori_loop(0, GROUPS, one, 0, unroll=True)

        def weights(turned, weight):
            load_weight = links.move(r.att.at[3], weight)
            load_turned = links.move(r.turned, turned)
            for g in range(GROUPS):
                turned_left[pl.ds(g * GROUP, GROUP)] = mixed[g].T
            products(
                3,
                lambda: turned_left[...],
                lambda h: branch[:, pl.ds(pl.multiple_of(h * col_block, col_block), col_block)],
            )
            load_weight.wait()
            for g in range(GROUPS):
                first = g * GROUP // row_block
                wide = []
                for h in range(heads):
                    blocks = [
                        weight[h // cs, h % cs, b // xs, b % xs] for b in range(first, first + GROUP // row_block)
                    ]
                    wide.append(jnp.concatenate(blocks, axis=0))
                mixed_grad[g] = dot_nt(branch[...], jnp.concatenate(wide, axis=1)).astype(BF16)
            ff_steps = [lambda u=u: ff_along(u) for u in units]
            plan((chip_sum, 3), (ff_steps[0],))
            plan((ff_steps[1],))
            plan()
            plan((ff_steps[2],))
            for i in range(images):
                attend(i)
                tick()
            while steps:
                tick()
            load_turned.wait()
            for i in range(images):
                turned_left[:, pl.ds(i * lat, lat)] = turned[:, i * span + patches : (i + 1) * span]
            products(0, lambda: turned_left[...], query_columns)
            late = ff_steps[3:]
            plan((late.pop(0),), (chip_sum, 0))
            products(2, lambda: turned[...], columns(2), tick)
            plan((late.pop(0),), (chip_sum, 2), (go, 3, 0))
            products(1, lambda: turned[...], columns(1), tick)
            waiting.extend(late)

        pl.run_scoped(
            weights,
            pltpu.VMEM((D, images * span), BF16),
            pltpu.VMEM((ys, cs, zs, xs, row_block, col_block), BF16),
        )

        def inputs(att, tokens, pair_grad):
            weight_loads = [links.move(r.att.at[m], att.at[m]) for m in (1, 2, 0)]
            loads = {}

            def fetch(i):
                loads[i] = links.move(r.tokens.at[i], tokens.at[i % 2])

            media_out = {}
            for i in range(min(2, images)):
                fetch(i)
            few = len(waiting) // 2
            plan((chip_sum, 1), (added_out,), *[(f,) for f in waiting[:few]])
            plan((go, 0, 0))
            plan(*[(f,) for f in waiting[few:]])
            plan((go, 3, 1), (go, 2, 0))
            plan((go, 0, 1))
            plan((go, 1, 0), (go, 3, 2))
            plan((go, 2, 1))
            plan((go, 0, 2))
            zero = jnp.zeros((8, D), F32)
            sums = (zero, zero, zero, zero)
            for load in weight_loads:
                load.wait()
            shares = 4
            share = patches // shares

            def product(i, t):
                for u in range(zs // shares):
                    product_block(i, t * (zs // shares) + u)

            def product_block(i, z):
                out = pair_grad.at[i % 2]
                cols = pl.ds(pl.multiple_of(z * xr, xr), xr)
                stacked = jnp.concatenate([pairs[i, j] for j in range(2 * GROUPS)], axis=1)
                asked = jnp.concatenate([query_back[g, pl.ds(i * lat, lat)] for g in range(GROUPS)], axis=1)
                wide = jnp.concatenate(
                    [att[m, h // cs, h % cs, z].reshape(xr, col_block) for m in (1, 2) for h in range(heads)], axis=1
                )
                narrow = jnp.concatenate(
                    [att[0, h // cs, h % cs, z].reshape(xr, col_block) for h in range(heads)], axis=1
                )
                out[:, cols] = dot_nt(stacked, wide)
                out[patches:, cols] += dot_nt(asked, narrow)

            def media(i, z, carry):
                gain, shift = carry
                rws = pl.ds(pl.multiple_of(z * share, 16), share)
                hat, scale = normed(tokens[i % 2, rws].astype(F32))
                up = pair_grad[i % 2, rws]
                tokens[i % 2, rws] = norm_back(up, hat, scale, norm_ref[0:1]).astype(BF16)
                return gain + fold(up * hat), shift + fold(up)

            def first_product(z, _):
                product(0, z)
                return 0

            lax.fori_loop(0, shares, first_product, 0)
            tick()
            for i in range(images):
                loads[i].wait()

                def one(z, carry):
                    if i + 1 < images:
                        product(i + 1, z)
                    return media(i, z, carry)

                gain, shift = lax.fori_loop(0, shares, one, (sums[0], sums[1]))
                media_out[i] = links.move(tokens.at[i % 2], r.media_grad.at[i])
                rws = pl.ds(i * lat, lat)
                hat, scale = normed(latents[rws].astype(F32))
                up = pair_grad[i % 2, patches:]
                made = middle_grad[rws] + norm_back(up, hat, scale, norm_ref[2:3])
                latent_low[rws] = made.astype(BF16)
                sums = (gain, shift, sums[2] + fold(up * hat), sums[3] + fold(up))
                tick()
                tick()
                if i + 2 < images:
                    media_out[i].wait()
                    fetch(i + 2)
            for k, value in enumerate(sums):
                r.norm_parts[k] = value
            for i in range(max(0, images - 2), images):
                media_out[i].wait()

        pl.run_scoped(
            inputs,
            pltpu.VMEM((3, ys, cs, zs, xs, row_block, col_block), BF16),
            pltpu.VMEM((2, patches, D), BF16),
            pltpu.VMEM((2, span, D), F32),
        )
        sums = [jnp.sum(r.norm_parts[k], axis=0, keepdims=True) for k in range(6)]
        r.totals[...] = jnp.concatenate([*sums, jnp.zeros((2, D), F32)], axis=0)
        total_slots = {axis: [links.take() for _ in range(1, sizes[axis])] for axis in "cyxz"}

        def total_copies(axis):
            mine = total_lands[axis].at[at[axis]]
            for k, slot in enumerate(total_slots[axis], 1):
                yield links.copy(mine, mine, slot, axis, k)

        def total_start(axis):
            total_lands[axis][at[axis]] = r.totals[...]
            for copy in total_copies(axis):
                copy.start()

        def total_finish(axis):
            lands = total_lands[axis]
            for k, slot in enumerate(total_slots[axis], 1):
                land = lands.at[links.place(axis, sizes[axis] - k)]
                links.copy(land, land, slot, axis, k).wait_recv()
            value = lands[0]
            for k in range(1, sizes[axis]):
                value = value + lands[k]
            r.totals[...] = value

        total_start("c")
        while steps:
            tick()
        total_finish("c")
        total_start("y")
        go(1, 1)
        total_finish("y")
        total_start("x")
        go(2, 2)
        total_finish("x")
        total_start("z")
        ff_finish()
        go(1, 2)
        resampled = added_finish()
        total_finish("z")
        for axis in "cyxz":
            for copy in total_copies(axis):
                copy.wait_send()
        resampled.wait()
        for m in range(4):
            for yi in range(ys):
                block_copy(m, yi).wait_send()
            for part in scatter[m]:
                part.close()
        for unit in units:
            for copy in x_copies(unit):
                copy.wait_send()
            if unit[1]:
                z_copy(unit).wait_send()
        for unit in ready:
            z_copy(unit).wait_send()

    for load in early:
        load.wait()
    pl.run_scoped(
        attention,
        pltpu.VMEM((4, ys, cs, zs, xs, row_block, col_block), BF16),
        pltpu.VMEM((D, n), BF16),
    )

    outs.append(links.move(latent_low, r.latent_grad))
    squares = jnp.sum(r.att_share[...] * r.att_share[...]) + jnp.sum(r.ff_share[...] * r.ff_share[...])
    value = jnp.full((8, 128), squares, F32)
    last = []
    for axes, lands in zip(("yc", "zx"), r.square_lands):
        first, second = axes

        def spot(way):
            return links.place(first, way.get(first, 0)) * sizes[second] + links.place(second, way.get(second, 0))

        mine = lands.at[spot({})]
        mine[...] = value
        coming = []
        for way in links.around(axes):
            slot = links.take()
            copy = links.send_to(mine, mine, slot, way)
            copy.start()
            last.append(copy)
            land = lands.at[spot({axis: sizes[axis] - k for axis, k in way.items()})]
            coming.append(links.send_to(land, land, slot, way))
        for copy in coming:
            copy.wait_recv()
        value = lands[0]
        for k in range(1, lands.shape[0]):
            value = value + lands[k]
    r.squares[...] = value
    for copy in last:
        copy.wait_send()
    for out in outs:
        out.wait()


def backward(got, tokens, latents, counts, norm_params, row_block, col_block, ff_block):
    sizes = grid_of(lax.axis_size("dp"), lax.axis_size("head"))
    zs, xs, ys, cs = (sizes[a] for a in "zxyc")
    images, patches, _ = tokens.shape
    lat = latents.shape[1]
    n = images * lat
    half = row_block // 2
    vmem, anywhere = pl.BlockSpec(memory_space=pltpu.VMEM), pl.BlockSpec(memory_space=pl.ANY)
    smem = pl.BlockSpec(memory_space=pltpu.SMEM)
    inputs = dict(
        att=(got.att, anywhere),
        ff_grad=(got.ff, anywhere),
        added=(got.added, anywhere),
        middle=(got.middle, vmem),
        pairs=(got.pairs, anywhere),
        turned=(got.turned, anywhere),
        tokens=(tokens, anywhere),
        queries=(got.queries, vmem),
        mixed=(got.mixed, vmem),
        middle_grad=(got.middle_grad, vmem),
        branch=(got.branch, vmem),
        ff_norm=(got.ff_norm, vmem),
        latents=(latents.reshape(n, D), vmem),
        norm=(norm_params, vmem),
        counts=(counts, smem),
    )
    outputs = dict(
        resampled=((n, D), BF16, anywhere),
        media_grad=((images, patches, D), BF16, anywhere),
        latent_grad=((n, D), BF16, anywhere),
        att_share=((4, row_block, col_block), F32, vmem),
        ff_share=((2, row_block, ff_block), F32, vmem),
        totals=((8, D), F32, vmem),
        squares=((8, 128), F32, vmem),
    )
    scratch = dict(
        grads_ff=(got.ff.shape, BF16),
        ff_land_x=((2, zs, xs - 1, got.ff.shape[0], row_block, got.ff.shape[-1]), BF16),
        ff_land_z=((2, zs - 1, got.ff.shape[0], row_block, got.ff.shape[-1]), BF16),
        added_here=((ys, n, D), BF16),
        added_land_c=((ys, n, D), BF16),
        added_land_y=((ys - 1, n, D), BF16),
        att_land_c=((4, ys, zs, xs, row_block, col_block), BF16),
        pairs_here=(got.pairs.shape, BF16),
        latent_low=((n, D), BF16),
        mixed_grad=((GROUPS, n, GROUP), BF16),
        query_back=((GROUPS, n, GROUP), BF16),
        norm_parts=((6, 8, D), F32),
    )
    totals = [((sizes[axis], 8, D), F32) for axis in "cyxz"]
    totals += [((sizes[a] * sizes[b], 8, 128), F32) for a, b in ("yc", "zx")]
    lands = {}
    for m, orders in ATT_ORDERS.items():
        for s, order in enumerate(orders):
            for step, shape in enumerate(land_shapes(sizes, order, "yzx", (half, col_block))):
                lands[m, s, step] = (shape, BF16)
    steps = sum(v - 1 for v in sizes.values())
    slots = 9 * steps + 2 * (zs * xs + zs) + 6 * ys + zs * xs + ys * cs
    semaphores = dict(send=slots, recv=slots, local=3 * images + 30)
    names = [*inputs, *outputs, *semaphores, *scratch]
    made = pl.pallas_call(
        functools.partial(backward_kernel, sizes, (names, tuple(lands), images, patches, lat, ff_block)),
        out_shape=[jax.ShapeDtypeStruct(shape, dtype) for shape, dtype, _ in outputs.values()],
        in_specs=[spec for _, spec in inputs.values()],
        out_specs=[spec for _, _, spec in outputs.values()],
        scratch_shapes=[pltpu.SemaphoreType.DMA((v,)) for v in semaphores.values()]
        + [pltpu.VMEM(*v) for v in [*scratch.values(), *totals, *lands.values()]],
        compiler_params=pltpu.CompilerParams(
            collective_id=1, has_side_effects=True, vmem_limit_bytes=63 * MIB + 900 * 1024
        ),
        name="backward_and_scatter",
    )(*(value for value, _ in inputs.values()))
    return SimpleNamespace(**dict(zip(outputs, made)))


def adam_step(master, first, second, gradient, step_rate, decay_rate):
    first_new = BETA_ONE * first + (1.0 - BETA_ONE) * gradient
    second_new = BETA_TWO * second + (1.0 - BETA_TWO) * gradient * gradient
    first_hat = first_new / (1.0 - BETA_ONE**STEP)
    second_hat = second_new / (1.0 - BETA_TWO**STEP)
    master_new = master - step_rate * (
        first_hat / (jnp.sqrt(second_hat) + ADAM_EPS) + decay_rate * master
    )
    return (master_new, first_new, second_new)


def update_kernel(cuts, *refs):
    shares, refs = refs[:5], refs[5:]
    att, expand, reduce, norm, refs = refs[:3], refs[3:6], refs[6:9], refs[9:12], refs[12:]
    carried, refs = refs[:3], refs[3:]
    att_out, expand_out, reduce_out, norm_out, refs = refs[:3], refs[3:6], refs[6:9], refs[9:12], refs[12:]
    size_out, carried_out = refs[0], refs[1:4]
    att_share, expand_share, reduce_share, totals, local_squares = shares
    step = pl.program_id(0)
    for a, b in zip(carried, carried_out):
        b[...] = a[...]
    norm_total = totals[:6]
    squares = local_squares[:1, :1] + jnp.sum(norm_total * norm_total).reshape(1, 1)
    size = jnp.sqrt(squares)
    clip = jnp.minimum(1.0, MAX_NORM / (size + 1e-06))

    def write(outs, values):
        for out, value in zip(outs, values):
            out[...] = value

    write(att_out, adam_step(*(v[...] for v in att), att_share[...] * clip[None], MATRIX_RATE, DECAY_RATE))
    write(expand_out, adam_step(*(v[...] for v in expand), expand_share[0] * clip, MATRIX_RATE, DECAY_RATE))
    write(reduce_out, adam_step(*(v[...] for v in reduce), reduce_share[0].T * clip, MATRIX_RATE, DECAY_RATE))

    @pl.when(step == cuts - 1)
    def _():
        size_out[...] = size
        write(norm_out, adam_step(*(v[...] for v in norm), norm_total * clip, NORM_RATE, 0.0))


def update(back, attention, expand, reduce, norm):
    cuts = 4
    _, row_block, col_block = attention[0].shape
    ff_block = expand[0].shape[1]
    att_spec = pl.BlockSpec((1, row_block, col_block), lambda j: (j, 0, 0))
    expand_spec = pl.BlockSpec((row_block // cuts, ff_block), lambda j: (j, 0))
    reduce_spec = pl.BlockSpec((ff_block // cuts, row_block), lambda j: (j, 0))
    norm_spec = pl.BlockSpec(norm[0].shape, lambda j: (0, 0))
    shapes = [*attention, *expand, *reduce, *norm]
    specs = [att_spec] * 3 + [expand_spec] * 3 + [reduce_spec] * 3 + [norm_spec] * 3
    carried = [back.resampled, back.media_grad.reshape(-1, D), back.latent_grad]
    carried_specs = [pl.BlockSpec((v.shape[0] // cuts, D), lambda j: (j, 0)) for v in carried]
    out_shape = [jax.ShapeDtypeStruct(v.shape, v.dtype) for v in shapes]
    out_shape += [jax.ShapeDtypeStruct((1, 1), F32)]
    out_shape += [jax.ShapeDtypeStruct(v.shape, v.dtype) for v in carried]
    made = pl.pallas_call(
        functools.partial(update_kernel, cuts),
        grid=(cuts,),
        out_shape=out_shape,
        in_specs=[
            att_spec,
            pl.BlockSpec((1, row_block // cuts, ff_block), lambda j: (0, j, 0)),
            pl.BlockSpec((1, row_block, ff_block // cuts), lambda j: (1, 0, j)),
            pl.BlockSpec((8, D), lambda j: (0, 0)),
            pl.BlockSpec((8, 128), lambda j: (0, 0)),
            *specs,
            *carried_specs,
        ],
        out_specs=[*specs, pl.BlockSpec((1, 1), lambda j: (0, 0)), *carried_specs],
        compiler_params=pltpu.CompilerParams(vmem_limit_bytes=63 * MIB),
        name="update_kernel",
    )(back.att_share, back.ff_share, back.ff_share, back.totals, back.squares, *shapes, *carried)
    return made[:12], made[12], made[13:]


def on_device(
    media_tokens,
    latents,
    cotangent,
    counts,
    attention_weights,
    attention_first,
    attention_second,
    expand_weight,
    expand_first,
    expand_second,
    reduce_weight,
    reduce_first,
    reduce_second,
    norm_params,
    norm_first,
    norm_second,
):
    _, row_block, col_block = attention_weights.shape
    got = forward(
        attention_weights,
        expand_weight,
        reduce_weight,
        media_tokens,
        latents,
        cotangent,
        counts,
        norm_params,
    )
    back = backward(
        got, media_tokens, latents, counts, norm_params, row_block, col_block, expand_weight.shape[1]
    )
    made, size, (resampled, media_grad, latent_grad) = update(
        back,
        (attention_weights, attention_first, attention_second),
        (expand_weight, expand_first, expand_second),
        (reduce_weight, reduce_first, reduce_second),
        (norm_params, norm_first, norm_second),
    )
    return (
        resampled.reshape(latents.shape),
        media_grad.reshape(media_tokens.shape),
        latent_grad.reshape(latents.shape),
        size.reshape(()),
        *made,
    )


def solution(mesh):
    in_specs = (
        P(("dp", "head"), None, None),
        P(("dp", "head"), None, None),
        P(("dp", "head"), None, None),
        P("dp"),
        P(None, "dp", "head"),
        P(None, "dp", "head"),
        P(None, "dp", "head"),
        P("dp", "head"),
        P("dp", "head"),
        P("dp", "head"),
        P("head", "dp"),
        P("head", "dp"),
        P("head", "dp"),
        P(),
        P(),
        P(),
    )
    out_specs = (
        P(("dp", "head"), None, None),
        P(("dp", "head"), None, None),
        P(("dp", "head"), None, None),
        P(),
        P(None, "dp", "head"),
        P(None, "dp", "head"),
        P(None, "dp", "head"),
        P("dp", "head"),
        P("dp", "head"),
        P("dp", "head"),
        P("head", "dp"),
        P("head", "dp"),
        P("head", "dp"),
        P(),
        P(),
        P(),
    )
    return jax.shard_map(
        on_device, mesh=mesh, in_specs=in_specs, out_specs=out_specs, check_vma=False
    )
```

```python
import functools
from types import SimpleNamespace

import jax
import jax.numpy as jnp
from jax import lax
from jax.experimental import pallas as pl
from jax.experimental.pallas import tpu as pltpu
from jax.sharding import PartitionSpec as P

D = 1024
HEADS = 16
HEAD = D // HEADS
GROUP = 256
GROUPS = D // GROUP
STEP = 10

LN_EPS = 1e-05
BETA_ONE = 0.9
BETA_TWO = 0.999
ADAM_EPS = 1e-08
MATRIX_RATE = 0.1
NORM_RATE = 0.6
DECAY_RATE = 0.1
MAX_NORM = 0.05

MESH = pl.DeviceIdType.MESH
F32 = jnp.float32
BF16 = jnp.bfloat16
MIB = 2**20
EARLY = 2


def grid_of(dp_count, head_count):
    x = 1
    while 4 * x * x <= dp_count:
        x *= 2
    return {"z": dp_count // x, "x": x, "y": head_count // 2, "c": 2}


class Links:
    def __init__(self, sizes, send, recv, local):
        self.sizes, self.send, self.recv, self.local = sizes, send, recv, local
        self.used = self.used_local = 0
        dp, head = lax.axis_index("dp"), lax.axis_index("head")
        self.at = {
            "z": lax.div(dp, sizes["x"]),
            "x": lax.rem(dp, sizes["x"]),
            "y": lax.div(head, sizes["c"]),
            "c": lax.rem(head, sizes["c"]),
        }
        self.head = head

    def place(self, axis, k):
        return lax.rem(self.at[axis] + k, self.sizes[axis])

    def peer(self, steps):
        at = dict(self.at)
        for axis, k in steps.items():
            at[axis] = self.place(axis, k)
        return {
            "dp": at["z"] * self.sizes["x"] + at["x"],
            "head": at["y"] * self.sizes["c"] + at["c"],
        }

    def around(self, axes):
        ways = [{}]
        for axis in axes:
            ways = [{**way, axis: k} for way in ways for k in range(self.sizes[axis])]
        return ways[1:]

    def greet(self, *groups):
        barrier = pltpu.get_barrier_semaphore()
        self.met = [way for axes in groups for way in self.around(axes)]
        for way in self.met:
            pl.semaphore_signal(barrier, inc=1, device_id=self.peer(way), device_id_type=MESH)

    def meet(self):
        pl.semaphore_wait(pltpu.get_barrier_semaphore(), len(self.met))

    def copy(self, src, dst, slot, axis, k):
        return self.send_to(src, dst, slot, {axis: k})

    def send_to(self, src, dst, slot, way):
        return pltpu.make_async_remote_copy(
            src_ref=src,
            dst_ref=dst,
            send_sem=self.send.at[slot],
            recv_sem=self.recv.at[slot],
            device_id=self.peer(way),
            device_id_type=MESH,
        )

    def take(self):
        self.used += 1
        return self.used - 1

    def move(self, src, dst):
        self.used_local += 1
        made = pltpu.make_async_copy(src, dst, self.local.at[self.used_local - 1])
        made.start()
        return made


class Gather:
    def __init__(self, links, order, view):
        self.links, self.order, self.view = links, order, view
        self.sent, self.coming = [], {}

    def region(self, step, place):
        at = dict(self.links.at)
        for axis in self.order[:step]:
            at[axis] = None
        at[self.order[step]] = place
        return self.view(at)

    def start(self, step):
        axis, links = self.order[step], self.links
        mine = self.region(step, links.at[axis])
        self.coming[step] = []
        for k in range(1, links.sizes[axis]):
            slot = links.take()
            copy = links.copy(mine, mine, slot, axis, k)
            copy.start()
            self.sent.append(copy)
            lands = self.region(step, links.place(axis, links.sizes[axis] - k))
            self.coming[step].append(links.copy(lands, lands, slot, axis, k))

    def wait(self, step):
        for copy in self.coming[step]:
            copy.wait_recv()

    def go(self, step):
        self.wait(step)
        if step + 1 < len(self.order):
            self.start(step + 1)

    def close(self):
        for copy in self.sent:
            copy.wait_send()


def some(place):
    return slice(None) if place is None else place


def dot(a, b):
    return lax.dot_general(a, b, (((1,), (0,)), ((), ())), preferred_element_type=F32)


def dot_nt(a, b):
    return lax.dot_general(a, b, (((1,), (1,)), ((), ())), preferred_element_type=F32)


def dot_tn(a, b):
    return lax.dot_general(a, b, (((0,), (0,)), ((), ())), preferred_element_type=F32)


def normed(values):
    center = values - jnp.mean(values, axis=-1, keepdims=True)
    scale = lax.rsqrt(jnp.mean(center * center, axis=-1, keepdims=True) + LN_EPS)
    return center * scale, scale


def norm_back(up, hat, scale, gain):
    inner = up * gain
    return scale * (
        inner
        - jnp.mean(inner, axis=-1, keepdims=True)
        - hat * jnp.mean(inner * hat, axis=-1, keepdims=True)
    )


def fold(rows):
    return jnp.sum(rows.reshape(rows.shape[0] // 8, 8, rows.shape[1]), axis=0)


def gelu_and_slope(v):
    root = 0.7978845608028654
    square = v * v
    t = jnp.tanh(root * v * (1.0 + 0.044715 * square))
    half = 0.5 + 0.5 * t
    slope = half + (0.5 * root) * v * (1.0 - t * t) * (1.0 + (3.0 * 0.044715) * square)
    return v * half, slope


def diagonal(rows):
    n = GROUP // HEAD
    lat = rows.shape[0]
    tall = jnp.concatenate([rows] * n, axis=0)
    row = lax.broadcasted_iota(jnp.int32, tall.shape, 0) // lat
    col = lax.broadcasted_iota(jnp.int32, tall.shape, 1) // HEAD
    return jnp.where(row == col, tall, jnp.zeros_like(tall))


def undiagonal(tall):
    n = GROUP // HEAD
    lat = tall.shape[0] // n
    col = lax.broadcasted_iota(jnp.int32, (lat, GROUP), 1) // HEAD
    total = jnp.where(col == 0, tall[:lat], 0.0)
    for h in range(1, n):
        total = total + jnp.where(col == h, tall[h * lat : (h + 1) * lat], 0.0)
    return total


def weight_block(weights, m, g, sizes):
    block = weights.shape[-1]
    per = GROUP // block
    parts = []
    for s in range(per):
        h = g * per + s
        part = weights[m, lax.div(h, sizes["c"]), lax.rem(h, sizes["c"])]
        parts.append(part.reshape(D, block))
    return parts[0] if per == 1 else jnp.concatenate(parts, axis=1)


def softmax_columns(keys, spread_queries, seen):
    scores = dot_nt(keys, spread_queries)
    scores = jnp.where(seen, scores, -1e30)
    raised = jnp.exp(scores - jnp.max(scores, axis=0, keepdims=True))
    return raised * (1.0 / jnp.sum(raised, axis=0, keepdims=True))


def forward_kernel(
    sizes,
    att_ref,
    expand_ref,
    reduce_ref,
    tokens_ref,
    latents_ref,
    cotangent_ref,
    counts_ref,
    norm_ref,
    att_out,
    pairs_out,
    turned_out,
    queries_out,
    mixed_out,
    ff_grad_out,
    added_out,
    middle_out,
    middle_grad_out,
    branch_out,
    ff_norm_out,
    att,
    pairs,
    turned,
    queries,
    mixed,
    ff,
    added,
    middle,
    middle_grad,
    branch,
    ff_norm,
    rows,
    back,
    hid,
    bg,
    part,
    land_c,
    land_y,
    land_x,
    tokens,
    inputs,
    send,
    recv,
    local,
):
    links = Links(sizes, send, recv, local)
    links.greet(*"zxyc")
    images, span, _ = inputs.shape
    patches = tokens_ref.shape[1]
    lat = span - patches
    at = links.at
    outs = []

    loads = {}

    def fetch(i):
        if i < images:
            loads[i] = links.move(tokens_ref.at[i], tokens.at[i % 2])

    fetch(0)
    fetch(1)
    for m in range(4):
        att[m, at["y"], at["c"], at["z"], at["x"]] = att_ref[m].astype(BF16)
    back[at["y"], at["c"]] = cotangent_ref[...].astype(BF16)
    quarters, tile = ff.shape[0], ff.shape[-1]
    for q in range(quarters):
        ff[q, 0, at["z"], at["x"]] = expand_ref[:, q * tile : (q + 1) * tile].astype(BF16)
        ff[q, 1, at["z"], at["x"]] = reduce_ref[q * tile : (q + 1) * tile].T.astype(BF16)

    half = att.shape[5] // 2

    def att_view(m, s):
        def view(p):
            return att.at[m, some(p["y"]), some(p["c"]), some(p["z"]), some(p["x"]), pl.ds(s * half, half)]

        return view

    def ff_view(q, m):
        def view(p):
            return ff.at[q, m, some(p["z"]), some(p["x"])]

        return view

    def back_view(p):
        return back.at[some(p["y"]), some(p["c"])]

    def row_view(i):
        def view(p):
            return rows.at[some(p["y"]), some(p["c"]), pl.ds(i * lat, lat)]

        return view

    query, key, value, output = ([Gather(links, "zxyc", att_view(m, s)) for s in range(2)] for m in range(4))
    hidden = [Gather(links, "zx", ff_view(q, m)) for q in range(quarters) for m in range(2)]
    cotangent = [Gather(links, "yc", back_view)]
    ff_rows = [Gather(links, "yc", row_view(i)) for i in range(images)]
    everything = [*query, *key, *value, *output, *hidden, *cotangent, *ff_rows]

    def start(parts):
        for part in parts:
            part.start(0)

    def go(parts, step):
        for part in parts:
            part.go(step)

    links.meet()
    start(cotangent + key + value + hidden[:1] + query + hidden[1:2] + output)

    for i in range(images):
        low = normed(latents_ref[pl.ds(i * lat, lat)].astype(F32))[0] * norm_ref[2:3] + norm_ref[3:4]
        inputs[i, pl.ds(patches, lat)] = low.astype(BF16)

    def normalize(i):
        loads[i].wait()
        some_rows = 64

        def one(t, _):
            part = pl.ds(pl.multiple_of(t * some_rows, some_rows), some_rows)
            low = normed(tokens[i % 2, part].astype(F32))[0] * norm_ref[0:1] + norm_ref[1:2]
            inputs[i, part] = low.astype(BF16)
            return 0

        lax.fori_loop(0, patches // some_rows, one, 0)
        fetch(i + 2)

    turning = {}

    def turn(i):
        if i >= 2:
            turning[i - 2].wait()

        def one(t, _):
            part = pl.ds(pl.multiple_of(t * 128, 128), 128)
            turned[i % 2, :, part] = inputs[i, part].T
            return 0

        lax.fori_loop(0, span // 128, one, 0)
        turning[i] = links.move(turned.at[i % 2], turned_out.at[:, pl.ds(i * span, span)])

    k0, k1, v0, v1, q0, q1, o0, o1 = *key, *value, *query, *output
    f = [*hidden, *[None] * (8 - len(hidden))]
    steps = []

    def plan(*ticks):
        steps.extend(ticks)

    plan(
        [(k0, 0)],
        [(k1, 0)],
        [(k0, 1), (v0, 0)],
        [(k1, 1), (v1, 0)],
        [(v0, 1)],
        [(k0, 2), (v1, 1)],
        [(f[0], 0)],
        [(k1, 2), (q0, 0)],
    )

    def tick():
        for part, step in steps.pop(0) if steps else ():
            if part is not None:
                part.go(step)
            if part in hidden:
                start(hidden[hidden.index(part) + 2 :][:1])

    def rest():
        while steps:
            tick()

    for i in range(images):
        normalize(i)
        tick()
        turn(i)
        tick()
    plan([(q1, 0), (v0, 2), (q0, 1)])
    rest()
    for i in range(max(0, images - 2), images):
        turning[i].wait()
    go(key, 3)

    def project(i, m):
        def one(g, _):
            weight = weight_block(att, m, g, sizes)
            pairs[i, (m - 1) * GROUPS + g] = dot(inputs[i], weight).astype(BF16)
            return 0

        lax.fori_loop(0, GROUPS, one, 0)

    def attend(i):
        position = lax.broadcasted_iota(jnp.int32, (span, GROUP), 0)
        count = counts_ref[links.head * images + i]
        seen = (position < count) | (position >= patches)

        def one(g, _):
            spread = diagonal(queries[g, pl.ds(i * lat, lat)])
            probs = softmax_columns(pairs[i, g], spread, seen).astype(BF16)
            wide = dot_tn(probs, pairs[i, GROUPS + g])
            mixed[g, pl.ds(i * lat, lat)] = undiagonal(wide).astype(BF16)
            return 0

        lax.fori_loop(0, GROUPS, one, 0)

    def finish(i):
        part = pl.ds(i * lat, lat)
        whole = jnp.concatenate([mixed[g, part] for g in range(GROUPS)], axis=1)
        made = jnp.concatenate(
            [dot(whole, weight_block(att, 3, g, sizes)) for g in range(GROUPS)], axis=1
        )
        value = latents_ref[part].astype(F32) + made
        middle[part] = value
        low = normed(value)[0] * norm_ref[4:5] + norm_ref[5:6]
        rows[at["y"], at["c"], part] = low.astype(BF16)
        ff_rows[i].start(0)

    plan([], [(q1, 1)], [(f[1], 0)], [(v1, 2)])
    for i in range(images):
        project(i, 1)
        tick()
    plan([(o0, 0), (q0, 2), (o1, 0)])
    rest()
    go(value, 3)
    plan([(o0, 1)], [(q1, 2)], [(f[2], 0), (o1, 1)], [(f[3], 0)])
    for i in range(images):
        project(i, 2)
        outs.append(links.move(pairs.at[i], pairs_out.at[i]))
        tick()
    plan([(o0, 2)])
    rest()
    go(query, 3)
    stack = inputs[:, patches:].reshape(images * lat, D)
    for g in range(GROUPS):
        made = dot(stack, weight_block(att, 0, g, sizes)) * HEAD ** (-0.5)
        queries[g] = made.astype(BF16)
    outs.append(links.move(queries, queries_out))
    plan([(f[4], 0)], [(o1, 2)], [(f[5], 0)])
    for i in range(images):
        attend(i)
        tick()
    rest()
    go(output, 3)
    outs.append(links.move(att, att_out))
    outs.append(links.move(mixed, mixed_out))
    plan([], [(f[6], 0)], [(cotangent[0], 0)], [(f[7], 0)])
    for i in range(images):
        finish(i)
        tick()
    rest()
    outs.append(links.move(middle, middle_out))
    go(cotangent, 1)
    go(ff_rows, 0)
    n = images * lat
    cs, ys, zs = (sizes[a] for a in "cyz")
    sib = links.place("c", 1)
    xr = sizes["x"] * att.shape[5]

    def first(q):
        def one(yi, _):
            before = dot(rows[yi].reshape(cs * n, D), ff[q, 0].reshape(D, tile))
            up = dot(back[yi].reshape(cs * n, D), ff[q, 1].reshape(D, tile))
            made, slope = gelu_and_slope(before)
            hid[yi, :, :, q * tile : (q + 1) * tile] = made.astype(BF16).reshape(cs, n, tile)
            bg[yi, :, :, q * tile : (q + 1) * tile] = (up * slope).astype(BF16).reshape(cs, n, tile)
            return 0

        lax.fori_loop(0, ys, one, 0)

    go(ff_rows, 1)
    for q in range(quarters):
        go(hidden[2 * q : 2 * q + 2], 1)
        first(q)

    ff_block = quarters * tile

    def second(kind, yi):
        wide = (hid if kind else bg)[yi].reshape(cs * n, ff_block)
        made = added if kind else part

        def one(z, _):
            cols = pl.ds(pl.multiple_of(z * xr, xr), xr)
            weight = jnp.concatenate([ff[q, kind, z].reshape(xr, tile) for q in range(quarters)], axis=1)
            made[yi, :, :, cols] = dot_nt(wide, weight).astype(BF16).reshape(cs, n, xr)
            return 0

        lax.fori_loop(0, zs, one, 0)

    sent, chip, along = [], {}, {}
    for k in [*range(1, ys), 0]:
        yi = links.place("y", k)
        second(0, yi)
        slot = links.take()
        land = land_c.at[yi]
        copy = links.copy(part.at[yi, sib], land, slot, "c", 1)
        copy.start()
        sent.append(copy)
        chip[k] = links.copy(land, land, slot, "c", 1)
    for k in range(1, ys):
        yi = links.place("y", k)
        chip[k].wait_recv()
        summed = part[yi, at["c"]].astype(F32) + land_c[yi].astype(F32)
        part[yi, at["c"]] = summed.astype(BF16)
        slot = links.take()
        land = land_y.at[k - 1]
        copy = links.copy(part.at[yi, at["c"]], land, slot, "y", k)
        copy.start()
        sent.append(copy)
        along[k] = links.copy(land, land, slot, "y", k)
    for gather in hidden:
        gather.close()

    def gradient(m, z):
        left, right = (back, hid) if m else (rows, bg)
        cols = pl.ds(pl.multiple_of(z * xr, xr), xr)
        made = dot_tn(
            left[:, :, :, cols].reshape(ys * cs * n, xr), right[...].reshape(ys * cs * n, ff_block)
        ).astype(BF16)
        for q in range(quarters):
            ff[q, m, z] = made[:, q * tile : (q + 1) * tile].reshape(*ff.shape[3:5], tile)

    xs = sizes["x"]
    early = range(1, 1 + land_x.shape[0])
    x_slots = {k: [links.take() for _ in range(1, xs)] for k in early}

    def x_copies(k):
        for j, slot in enumerate(x_slots[k], 1):
            block = ff.at[:, 0, links.place("z", k), links.place("x", j)]
            yield links.copy(block, land_x.at[k - 1, j - 1], slot, "x", j)

    for k in early:
        gradient(0, links.place("z", k))
        for copy in x_copies(k):
            copy.start()
    for yi in range(ys):
        second(1, yi)
    outs.append(links.move(added, added_out))

    def other(k, _):
        gradient(0, links.place("z", k))
        return 0

    lax.fori_loop(1 + len(early), zs + 1, other, 0)

    def both(z, _):
        gradient(1, z)
        return 0

    lax.fori_loop(0, zs, both, 0)
    chip[0].wait_recv()
    for k in range(1, ys):
        along[k].wait_recv()

    def back_one(t, carry):
        gain, shift = carry
        rws = pl.ds(pl.multiple_of(t * lat, lat), lat)
        up = part[at["y"], at["c"], rws].astype(F32) + land_c[at["y"], rws].astype(F32)
        for k in range(1, ys):
            up = up + land_y[k - 1, rws].astype(F32)
        hat, scale = normed(middle[rws])
        value = cotangent_ref[rws] + norm_back(up, hat, scale, norm_ref[4:5])
        middle_grad[rws] = value
        branch[rws] = value.astype(BF16)
        return gain + fold(up * hat), shift + fold(up)

    zero = jnp.zeros((8, D), F32)
    ff_norm[0], ff_norm[1] = lax.fori_loop(0, images, back_one, (zero, zero))
    outs.append(links.move(middle_grad, middle_grad_out))
    outs.append(links.move(branch, branch_out))
    outs.append(links.move(ff_norm, ff_norm_out))
    for k in early:
        for copy in x_copies(k):
            copy.wait_recv()
        z = links.place("z", k)
        for q in range(quarters):
            total = ff[q, 0, z, at["x"]].astype(F32)
            for j in range(xs - 1):
                total = total + land_x[k - 1, j, q].astype(F32)
            ff[q, 0, z, at["x"]] = total.astype(BF16)
        for copy in x_copies(k):
            copy.wait_send()
    outs.append(links.move(ff, ff_grad_out))
    for copy in sent:
        copy.wait_send()
    for gather in everything:
        if gather not in hidden:
            gather.close()
    for out in outs:
        out.wait()


def forward(att, expand, reduce, tokens, latents, cotangent, counts, norm_params):
    sizes = grid_of(lax.axis_size("dp"), lax.axis_size("head"))
    z, x, y, c = (sizes[a] for a in "zxyc")
    images, patches, _ = tokens.shape
    lat = latents.shape[1]
    span = patches + lat
    n = images * lat
    _, row_block, col_block = att.shape
    ff_block = expand.shape[1]
    tile = min(GROUP, ff_block)
    quarters = ff_block // tile
    shapes = dict(
        att=((4, y, c, z, x, row_block, col_block), BF16),
        pairs=((images, 2 * GROUPS, span, GROUP), BF16),
        turned=((D, images * span), BF16),
        queries=((GROUPS, n, GROUP), BF16),
        mixed=((GROUPS, n, GROUP), BF16),
        ff=((quarters, 2, z, x, row_block, tile), BF16),
        added=((y, c, n, D), BF16),
        middle=((n, D), F32),
        middle_grad=((n, D), F32),
        branch=((n, D), BF16),
        ff_norm=((2, 8, D), F32),
    )
    held = dict(shapes)
    held.update(turned=((2, D, span), BF16))
    inside = [
        ((y, c, n, D), BF16),
        ((y, c, n, D), BF16),
        ((y, c, n, ff_block), BF16),
        ((y, c, n, ff_block), BF16),
        ((y, c, n, D), BF16),
        ((y, n, D), BF16),
        ((y - 1, n, D), BF16),
        ((EARLY, x - 1, quarters, row_block, tile), BF16),
        ((2, patches, D), BF16),
        ((images, span, D), BF16),
    ]
    per_att = sum(s - 1 for s in sizes.values())
    slots = 8 * per_att + 8 * (z + x - 2) + (1 + images) * (y + c - 2) + 2 * y + EARLY * x
    vmem, anywhere = pl.BlockSpec(memory_space=pltpu.VMEM), pl.BlockSpec(memory_space=pl.ANY)
    made = pl.pallas_call(
        functools.partial(forward_kernel, sizes),
        out_shape=[jax.ShapeDtypeStruct(*v) for v in shapes.values()],
        in_specs=[vmem, vmem, vmem, anywhere, vmem, vmem, pl.BlockSpec(memory_space=pltpu.SMEM), vmem],
        out_specs=[anywhere] * len(shapes),
        scratch_shapes=[pltpu.VMEM(*v) for v in [*held.values(), *inside]]
        + [
            pltpu.SemaphoreType.DMA((slots,)),
            pltpu.SemaphoreType.DMA((slots,)),
            pltpu.SemaphoreType.DMA((2 * images + 20,)),
        ],
        compiler_params=pltpu.CompilerParams(
            collective_id=0, has_side_effects=True, vmem_limit_bytes=63 * MIB + 900 * 1024
        ),
        name="gather_and_attend",
    )(att, expand, reduce, tokens, latents.reshape(n, D), cotangent.reshape(n, D), counts, norm_params)
    return SimpleNamespace(**dict(zip(shapes, made)))


class Scatter:
    def __init__(self, links, order, view, lands):
        self.links, self.order, self.view, self.lands = links, order, view, lands
        self.slots = {}

    def region(self, step, place):
        at = dict(self.links.at)
        for axis in self.order[step + 1 :]:
            at[axis] = None
        at[self.order[step]] = place
        return self.view(at)

    def copies(self, step):
        axis, links = self.order[step], self.links
        for k, slot in enumerate(self.slots[step], 1):
            yield links.copy(self.region(step, links.place(axis, k)), self.lands[step][k - 1], slot, axis, k)

    def start(self, step):
        self.slots[step] = [self.links.take() for _ in range(1, self.links.sizes[self.order[step]])]
        for copy in self.copies(step):
            copy.start()

    def wait(self, step):
        for k, slot in enumerate(self.slots[step], 1):
            land = self.lands[step][k - 1]
            self.links.copy(land, land, slot, self.order[step], k).wait_recv()

    def add(self, step, out=None):
        mine = self.region(step, self.links.at[self.order[step]])
        lands = self.lands[step]
        lead = mine.shape[0] if len(mine.shape) > 2 else None

        def total(at):
            value = mine[at].astype(F32)
            for land in lands:
                value = value + land[at].astype(F32)
            return value

        if out is not None:
            out[...] = total(Ellipsis)
        elif lead is None:
            mine[...] = total(Ellipsis).astype(BF16)
        else:

            def one(t, _):
                mine[t] = total(t).astype(BF16)
                return 0

            lax.fori_loop(0, lead, one, 0)

    def go(self, step, out=None):
        self.wait(step)
        self.add(step, out)
        if step + 1 < len(self.order):
            self.start(step + 1)

    def close(self):
        for step in self.slots:
            for copy in self.copies(step):
                copy.wait_send()


ATT_ORDERS = {0: ("yxz", "yxz"), 1: ("yxz", "xyz"), 2: ("yxz", "xyz"), 3: ("yxz", "yxz")}


def land_shapes(sizes, order, axes, tail):
    shapes, left = [], list(axes)
    for axis in order:
        left.remove(axis)
        shapes.append((sizes[axis] - 1, *(sizes[a] for a in left), *tail))
    return shapes


def backward_kernel(sizes, dims, *refs):
    names, keys, images, patches, lat, ff_block = dims
    r = SimpleNamespace(**dict(zip(names, refs)))
    total_lands = dict(zip("cyxz", refs[len(names) :]))
    r.square_lands = refs[len(names) + 4 : len(names) + 6]
    att_lands = dict(zip(keys, refs[len(names) + 6 :]))
    links = Links(sizes, r.send, r.recv, r.local)
    links.greet("zx", "yc")
    at = links.at
    sib = links.place("c", 1)
    n = images * lat
    span = patches + lat
    zs, xs, ys, cs = (sizes[a] for a in "zxyc")
    row_block, col_block = r.att_share.shape[1:]
    xr = xs * row_block
    heads = ys * cs
    half = row_block // 2
    norm_ref, latents = r.norm, r.latents
    queries, mixed = r.queries, r.mixed
    grads_ff = r.grads_ff
    middle_grad, branch, latent_low = r.middle_grad, r.branch, r.latent_low
    mixed_grad, query_back = r.mixed_grad, r.query_back
    outs = []

    units = [(m, k) for k in [*range(1, zs), 0] for m in range(2)]
    ready = [(0, k) for k in range(1, 1 + EARLY)]
    units = [unit for unit in units if unit not in ready]
    x_slots = {unit: [links.take() for _ in range(1, xs)] for unit in units}
    z_slots = {unit: links.take() for unit in units + ready if unit[1]}

    def x_copies(unit):
        m, k = unit
        z = links.place("z", k)
        for j, slot in enumerate(x_slots[unit], 1):
            yield links.copy(
                grads_ff.at[:, m, z, links.place("x", j)], r.ff_land_x.at[m, z, j - 1], slot, "x", j
            )

    def z_copy(unit):
        m, k = unit
        return links.copy(
            grads_ff.at[:, m, links.place("z", k), at["x"]], r.ff_land_z.at[m, k - 1], z_slots[unit], "z", k
        )

    quarters, tile = grads_ff.shape[0], grads_ff.shape[-1]

    def ff_along(unit):
        m, k = unit
        z = links.place("z", k)
        for copy in x_copies(unit):
            copy.wait_recv()
        for q in range(quarters):
            total = grads_ff[q, m, z, at["x"]].astype(F32)
            for j in range(xs - 1):
                total = total + r.ff_land_x[m, z, j, q].astype(F32)
            if k:
                grads_ff[q, m, z, at["x"]] = total.astype(BF16)
            else:
                r.ff_share[m, :, q * tile : (q + 1) * tile] = total
        if k:
            z_copy(unit).start()

    def ff_finish():
        for m in range(2):
            for k in range(1, zs):
                z_copy((m, k)).wait_recv()
            for q in range(quarters):
                cols = pl.ds(q * tile, tile)
                total = r.ff_share[m, :, cols]
                for k in range(1, zs):
                    total = total + r.ff_land_z[m, k - 1, q].astype(F32)
                r.ff_share[m, :, cols] = total

    pairs = r.pairs_here
    early = [links.move(r.pairs.at[i], pairs.at[i]) for i in range(images)]

    load = links.move(r.ff_grad, grads_ff)
    own = links.move(r.added.at[:, at["c"]], r.added_here)
    links.meet()
    load.wait()
    for unit in units:
        for copy in x_copies(unit):
            copy.start()
    for unit in ready:
        z_copy(unit).start()

    c_slots = [links.take() for _ in range(ys)]
    y_slots = [links.take() for _ in range(1, ys)]

    def added_chip(k):
        yi = links.place("y", k)
        return links.copy(r.added.at[yi, sib], r.added_land_c.at[yi], c_slots[k], "c", 1)

    def added_along(k):
        return links.copy(r.added_here.at[links.place("y", k)], r.added_land_y.at[k - 1], y_slots[k - 1], "y", k)

    for k in range(ys):
        added_chip(k).start()
    own.wait()

    def added_out():
        for k in range(1, ys):
            yi = links.place("y", k)
            added_chip(k).wait_recv()
            summed = r.added_here[yi].astype(F32) + r.added_land_c[yi].astype(F32)
            r.added_here[yi] = summed.astype(BF16)
            added_along(k).start()

    resampled_low = r.added_here.at[at["y"]]

    def added_finish():
        added_chip(0).wait_recv()
        for k in range(1, ys):
            added_along(k).wait_recv()

        def one(t, _):
            rws = pl.ds(pl.multiple_of(t * lat, lat), lat)
            up = r.added_here[at["y"], rws].astype(F32) + r.added_land_c[at["y"], rws].astype(F32)
            for k in range(1, ys):
                up = up + r.added_land_y[k - 1, rws].astype(F32)
            resampled_low[rws] = (r.middle[rws] + up).astype(BF16)
            return 0

        lax.fori_loop(0, images, one, 0)
        for k in range(ys):
            added_chip(k).wait_send()
        for k in range(1, ys):
            added_along(k).wait_send()
        return links.move(resampled_low, r.resampled)

    r.norm_parts[4] = r.ff_norm[0]
    r.norm_parts[5] = r.ff_norm[1]

    steps = []

    def tick():
        if steps:
            steps.pop(0)()

    def plan(*calls):
        steps.append(lambda: [f(*args) for f, *args in calls])

    waiting = []

    def attention(grads, turned_left):
        per = GROUP // col_block
        block_slots = {m: [links.take() for _ in range(ys)] for m in range(4)}

        def block_copy(m, yi):
            slot = block_slots[m][0] + yi
            return links.copy(grads.at[m, yi, sib], r.att_land_c.at[m, yi], slot, "c", 1)

        def att_scatter(m, s):
            def view(p):
                return grads.at[m, some(p["y"]), at["c"], some(p["z"]), some(p["x"]), pl.ds(s * half, half)]

            order = ATT_ORDERS[m][s]
            lands = [
                [att_lands[m, s, step].at[k] for k in range(sizes[axis] - 1)]
                for step, axis in enumerate(order)
            ]
            return Scatter(links, order, view, lands)

        scatter = {m: [att_scatter(m, s) for s in range(2)] for m in range(4)}

        def go(m, step):
            for s, part in enumerate(scatter[m]):
                part.go(step, r.att_share.at[m, pl.ds(s * half, half)] if step == 2 else None)

        def chip_sum(m):
            for yi in range(ys):
                block_copy(m, yi).wait_recv()

                def one(z, _):
                    value = grads[m, yi, at["c"], z].astype(F32) + r.att_land_c[m, yi, z].astype(F32)
                    grads[m, yi, at["c"], z] = value.astype(BF16)
                    return 0

                lax.fori_loop(0, zs, one, 0)
            for part in scatter[m]:
                part.start(0)

        def products(m, left, right, between=None):
            def of(ci, send):
                def one(yi, _):
                    made = dot(left(), right(yi * cs + ci)).astype(BF16)
                    grads[m, yi, ci] = made.reshape(zs, xs, row_block, col_block)
                    if send:
                        block_copy(m, yi).start()
                    return 0

                lax.fori_loop(0, ys, one, 0)

            of(sib, True)
            if between is not None:
                between()
            of(at["c"], False)

        def query_columns(h):
            j = lax.div(h * col_block, GROUP)
            if per == 1:
                return query_back[j]
            off = pl.multiple_of(lax.rem(h, per) * col_block, col_block)
            return query_back[j, :, pl.ds(off, col_block)]

        def columns(m):
            def right(h):
                j = lax.div(h * col_block, GROUP) + (m - 1) * GROUPS
                if per == 1:
                    return pairs[:, j].reshape(images * span, GROUP)
                off = pl.multiple_of(lax.rem(h, per) * col_block, col_block)
                return pairs[:, j, :, pl.ds(off, col_block)].reshape(images * span, col_block)

            return right

        def attend(i):
            position = lax.broadcasted_iota(jnp.int32, (span, GROUP), 0)
            count = r.counts[links.head * images + i]
            seen = (position < count) | (position >= patches)
            rws = pl.ds(i * lat, lat)

            def one(g, _):
                keys, values = pairs[i, g], pairs[i, GROUPS + g]
                spread = diagonal(queries[g, rws])
                probs = softmax_columns(keys, spread, seen)
                upstream = diagonal(mixed_grad[g, rws])
                prob_grad = dot_nt(values, upstream)
                inner = jnp.sum(probs * prob_grad, axis=0, keepdims=True)
                score_grad = (probs * (prob_grad - inner)).astype(BF16)
                back = undiagonal(dot_tn(score_grad, keys)) * HEAD ** (-0.5)
                query_back[g, rws] = back.astype(BF16)
                pairs[i, GROUPS + g] = dot(probs.astype(BF16), upstream).astype(BF16)
                pairs[i, g] = dot(score_grad, spread).astype(BF16)
                return 0

            lax.fori_loop(0, GROUPS, one, 0)

        def weights(turned, weight):
            load_weight = links.move(r.att.at[3], weight)
            load_turned = links.move(r.turned, turned)
            for g in range(GROUPS):
                turned_left[pl.ds(g * GROUP, GROUP)] = mixed[g].T
            products(
                3,
                lambda: turned_left[...],
                lambda h: branch[:, pl.ds(pl.multiple_of(h * col_block, col_block), col_block)],
            )
            load_weight.wait()
            for g in range(GROUPS):
                first = g * GROUP // row_block
                wide = []
                for h in range(heads):
                    blocks = [
                        weight[h // cs, h % cs, b // xs, b % xs] for b in range(first, first + GROUP // row_block)
                    ]
                    wide.append(jnp.concatenate(blocks, axis=0))
                mixed_grad[g] = dot_nt(branch[...], jnp.concatenate(wide, axis=1)).astype(BF16)
            ff_steps = [lambda u=u: ff_along(u) for u in units]
            plan((chip_sum, 3), (ff_steps[0],))
            plan((ff_steps[1],))
            plan()
            plan((ff_steps[2],))
            for i in range(images):
                attend(i)
                tick()
            while steps:
                tick()
            load_turned.wait()
            for i in range(images):
                turned_left[:, pl.ds(i * lat, lat)] = turned[:, i * span + patches : (i + 1) * span]
            products(0, lambda: turned_left[...], query_columns)
            late = ff_steps[3:]
            plan((late.pop(0),), (chip_sum, 0))
            products(2, lambda: turned[...], columns(2), tick)
            plan((late.pop(0),), (chip_sum, 2), (go, 3, 0))
            products(1, lambda: turned[...], columns(1), tick)
            waiting.extend(late)

        pl.run_scoped(
            weights,
            pltpu.VMEM((D, images * span), BF16),
            pltpu.VMEM((ys, cs, zs, xs, row_block, col_block), BF16),
        )

        def inputs(att, tokens, pair_grad):
            weight_loads = [links.move(r.att.at[m], att.at[m]) for m in (1, 2, 0)]
            loads = {}

            def fetch(i):
                loads[i] = links.move(r.tokens.at[i], tokens.at[i % 2])

            media_out = {}
            for i in range(min(2, images)):
                fetch(i)
            few = len(waiting) // 2
            plan((chip_sum, 1), (added_out,), *[(f,) for f in waiting[:few]])
            plan((go, 0, 0))
            plan(*[(f,) for f in waiting[few:]])
            plan((go, 3, 1), (go, 2, 0))
            plan((go, 0, 1))
            plan((go, 1, 0), (go, 3, 2))
            plan((go, 2, 1))
            plan((go, 0, 2))
            zero = jnp.zeros((8, D), F32)
            sums = (zero, zero, zero, zero)
            for load in weight_loads:
                load.wait()
            shares = 4
            share = patches // shares

            def product(i, t):
                for u in range(zs // shares):
                    product_block(i, t * (zs // shares) + u)

            def product_block(i, z):
                out = pair_grad.at[i % 2]
                cols = pl.ds(pl.multiple_of(z * xr, xr), xr)
                stacked = jnp.concatenate([pairs[i, j] for j in range(2 * GROUPS)], axis=1)
                asked = jnp.concatenate([query_back[g, pl.ds(i * lat, lat)] for g in range(GROUPS)], axis=1)
                wide = jnp.concatenate(
                    [att[m, h // cs, h % cs, z].reshape(xr, col_block) for m in (1, 2) for h in range(heads)], axis=1
                )
                narrow = jnp.concatenate(
                    [att[0, h // cs, h % cs, z].reshape(xr, col_block) for h in range(heads)], axis=1
                )
                out[:, cols] = dot_nt(stacked, wide)
                out[patches:, cols] += dot_nt(asked, narrow)

            def media(i, z, carry):
                gain, shift = carry
                rws = pl.ds(pl.multiple_of(z * share, 16), share)
                hat, scale = normed(tokens[i % 2, rws].astype(F32))
                up = pair_grad[i % 2, rws]
                tokens[i % 2, rws] = norm_back(up, hat, scale, norm_ref[0:1]).astype(BF16)
                return gain + fold(up * hat), shift + fold(up)

            def first_product(z, _):
                product(0, z)
                return 0

            lax.fori_loop(0, shares, first_product, 0)
            tick()
            for i in range(images):
                loads[i].wait()

                def one(z, carry):
                    if i + 1 < images:
                        product(i + 1, z)
                    return media(i, z, carry)

                gain, shift = lax.fori_loop(0, shares, one, (sums[0], sums[1]))
                media_out[i] = links.move(tokens.at[i % 2], r.media_grad.at[i])
                rws = pl.ds(i * lat, lat)
                hat, scale = normed(latents[rws].astype(F32))
                up = pair_grad[i % 2, patches:]
                made = middle_grad[rws] + norm_back(up, hat, scale, norm_ref[2:3])
                latent_low[rws] = made.astype(BF16)
                sums = (gain, shift, sums[2] + fold(up * hat), sums[3] + fold(up))
                tick()
                tick()
                if i + 2 < images:
                    media_out[i].wait()
                    fetch(i + 2)
            for k, value in enumerate(sums):
                r.norm_parts[k] = value
            for i in range(max(0, images - 2), images):
                media_out[i].wait()

        pl.run_scoped(
            inputs,
            pltpu.VMEM((3, ys, cs, zs, xs, row_block, col_block), BF16),
            pltpu.VMEM((2, patches, D), BF16),
            pltpu.VMEM((2, span, D), F32),
        )
        sums = [jnp.sum(r.norm_parts[k], axis=0, keepdims=True) for k in range(6)]
        r.totals[...] = jnp.concatenate([*sums, jnp.zeros((2, D), F32)], axis=0)
        total_slots = {axis: [links.take() for _ in range(1, sizes[axis])] for axis in "cyxz"}

        def total_copies(axis):
            mine = total_lands[axis].at[at[axis]]
            for k, slot in enumerate(total_slots[axis], 1):
                yield links.copy(mine, mine, slot, axis, k)

        def total_start(axis):
            total_lands[axis][at[axis]] = r.totals[...]
            for copy in total_copies(axis):
                copy.start()

        def total_finish(axis):
            lands = total_lands[axis]
            for k, slot in enumerate(total_slots[axis], 1):
                land = lands.at[links.place(axis, sizes[axis] - k)]
                links.copy(land, land, slot, axis, k).wait_recv()
            value = lands[0]
            for k in range(1, sizes[axis]):
                value = value + lands[k]
            r.totals[...] = value

        total_start("c")
        while steps:
            tick()
        total_finish("c")
        total_start("y")
        go(1, 1)
        total_finish("y")
        total_start("x")
        go(2, 2)
        total_finish("x")
        total_start("z")
        ff_finish()
        go(1, 2)
        resampled = added_finish()
        total_finish("z")
        for axis in "cyxz":
            for copy in total_copies(axis):
                copy.wait_send()
        resampled.wait()
        for m in range(4):
            for yi in range(ys):
                block_copy(m, yi).wait_send()
            for part in scatter[m]:
                part.close()
        for unit in units:
            for copy in x_copies(unit):
                copy.wait_send()
            if unit[1]:
                z_copy(unit).wait_send()
        for unit in ready:
            z_copy(unit).wait_send()

    for load in early:
        load.wait()
    pl.run_scoped(
        attention,
        pltpu.VMEM((4, ys, cs, zs, xs, row_block, col_block), BF16),
        pltpu.VMEM((D, n), BF16),
    )

    outs.append(links.move(latent_low, r.latent_grad))
    squares = jnp.sum(r.att_share[...] * r.att_share[...]) + jnp.sum(r.ff_share[...] * r.ff_share[...])
    value = jnp.full((8, 128), squares, F32)
    last = []
    for axes, lands in zip(("yc", "zx"), r.square_lands):
        first, second = axes

        def spot(way):
            return links.place(first, way.get(first, 0)) * sizes[second] + links.place(second, way.get(second, 0))

        mine = lands.at[spot({})]
        mine[...] = value
        coming = []
        for way in links.around(axes):
            slot = links.take()
            copy = links.send_to(mine, mine, slot, way)
            copy.start()
            last.append(copy)
            land = lands.at[spot({axis: sizes[axis] - k for axis, k in way.items()})]
            coming.append(links.send_to(land, land, slot, way))
        for copy in coming:
            copy.wait_recv()
        value = lands[0]
        for k in range(1, lands.shape[0]):
            value = value + lands[k]
    r.squares[...] = value
    for copy in last:
        copy.wait_send()
    for out in outs:
        out.wait()


def backward(got, tokens, latents, counts, norm_params, row_block, col_block, ff_block):
    sizes = grid_of(lax.axis_size("dp"), lax.axis_size("head"))
    zs, xs, ys, cs = (sizes[a] for a in "zxyc")
    images, patches, _ = tokens.shape
    lat = latents.shape[1]
    n = images * lat
    half = row_block // 2
    vmem, anywhere = pl.BlockSpec(memory_space=pltpu.VMEM), pl.BlockSpec(memory_space=pl.ANY)
    smem = pl.BlockSpec(memory_space=pltpu.SMEM)
    inputs = dict(
        att=(got.att, anywhere),
        ff_grad=(got.ff, anywhere),
        added=(got.added, anywhere),
        middle=(got.middle, vmem),
        pairs=(got.pairs, anywhere),
        turned=(got.turned, anywhere),
        tokens=(tokens, anywhere),
        queries=(got.queries, vmem),
        mixed=(got.mixed, vmem),
        middle_grad=(got.middle_grad, vmem),
        branch=(got.branch, vmem),
        ff_norm=(got.ff_norm, vmem),
        latents=(latents.reshape(n, D), vmem),
        norm=(norm_params, vmem),
        counts=(counts, smem),
    )
    outputs = dict(
        resampled=((n, D), BF16, anywhere),
        media_grad=((images, patches, D), BF16, anywhere),
        latent_grad=((n, D), BF16, anywhere),
        att_share=((4, row_block, col_block), F32, vmem),
        ff_share=((2, row_block, ff_block), F32, vmem),
        totals=((8, D), F32, vmem),
        squares=((8, 128), F32, vmem),
    )
    scratch = dict(
        grads_ff=(got.ff.shape, BF16),
        ff_land_x=((2, zs, xs - 1, got.ff.shape[0], row_block, got.ff.shape[-1]), BF16),
        ff_land_z=((2, zs - 1, got.ff.shape[0], row_block, got.ff.shape[-1]), BF16),
        added_here=((ys, n, D), BF16),
        added_land_c=((ys, n, D), BF16),
        added_land_y=((ys - 1, n, D), BF16),
        att_land_c=((4, ys, zs, xs, row_block, col_block), BF16),
        pairs_here=(got.pairs.shape, BF16),
        latent_low=((n, D), BF16),
        mixed_grad=((GROUPS, n, GROUP), BF16),
        query_back=((GROUPS, n, GROUP), BF16),
        norm_parts=((6, 8, D), F32),
    )
    totals = [((sizes[axis], 8, D), F32) for axis in "cyxz"]
    totals += [((sizes[a] * sizes[b], 8, 128), F32) for a, b in ("yc", "zx")]
    lands = {}
    for m, orders in ATT_ORDERS.items():
        for s, order in enumerate(orders):
            for step, shape in enumerate(land_shapes(sizes, order, "yzx", (half, col_block))):
                lands[m, s, step] = (shape, BF16)
    steps = sum(v - 1 for v in sizes.values())
    slots = 9 * steps + 2 * (zs * xs + zs) + 6 * ys + zs * xs + ys * cs
    semaphores = dict(send=slots, recv=slots, local=3 * images + 30)
    names = [*inputs, *outputs, *semaphores, *scratch]
    made = pl.pallas_call(
        functools.partial(backward_kernel, sizes, (names, tuple(lands), images, patches, lat, ff_block)),
        out_shape=[jax.ShapeDtypeStruct(shape, dtype) for shape, dtype, _ in outputs.values()],
        in_specs=[spec for _, spec in inputs.values()],
        out_specs=[spec for _, _, spec in outputs.values()],
        scratch_shapes=[pltpu.SemaphoreType.DMA((v,)) for v in semaphores.values()]
        + [pltpu.VMEM(*v) for v in [*scratch.values(), *totals, *lands.values()]],
        compiler_params=pltpu.CompilerParams(
            collective_id=1, has_side_effects=True, vmem_limit_bytes=63 * MIB + 900 * 1024
        ),
        name="backward_and_scatter",
    )(*(value for value, _ in inputs.values()))
    return SimpleNamespace(**dict(zip(outputs, made)))


def adam_step(master, first, second, gradient, step_rate, decay_rate):
    first_new = BETA_ONE * first + (1.0 - BETA_ONE) * gradient
    second_new = BETA_TWO * second + (1.0 - BETA_TWO) * gradient * gradient
    first_hat = first_new / (1.0 - BETA_ONE**STEP)
    second_hat = second_new / (1.0 - BETA_TWO**STEP)
    master_new = master - step_rate * (
        first_hat / (jnp.sqrt(second_hat) + ADAM_EPS) + decay_rate * master
    )
    return (master_new, first_new, second_new)


def update_kernel(cuts, *refs):
    shares, refs = refs[:5], refs[5:]
    att, expand, reduce, norm, refs = refs[:3], refs[3:6], refs[6:9], refs[9:12], refs[12:]
    carried, refs = refs[:3], refs[3:]
    att_out, expand_out, reduce_out, norm_out, refs = refs[:3], refs[3:6], refs[6:9], refs[9:12], refs[12:]
    size_out, carried_out = refs[0], refs[1:4]
    att_share, expand_share, reduce_share, totals, local_squares = shares
    step = pl.program_id(0)
    for a, b in zip(carried, carried_out):
        b[...] = a[...]
    norm_total = totals[:6]
    squares = local_squares[:1, :1] + jnp.sum(norm_total * norm_total).reshape(1, 1)
    size = jnp.sqrt(squares)
    clip = jnp.minimum(1.0, MAX_NORM / (size + 1e-06))

    def write(outs, values):
        for out, value in zip(outs, values):
            out[...] = value

    write(att_out, adam_step(*(v[...] for v in att), att_share[...] * clip[None], MATRIX_RATE, DECAY_RATE))
    write(expand_out, adam_step(*(v[...] for v in expand), expand_share[0] * clip, MATRIX_RATE, DECAY_RATE))
    write(reduce_out, adam_step(*(v[...] for v in reduce), reduce_share[0].T * clip, MATRIX_RATE, DECAY_RATE))

    @pl.when(step == cuts - 1)
    def _():
        size_out[...] = size
        write(norm_out, adam_step(*(v[...] for v in norm), norm_total * clip, NORM_RATE, 0.0))


def update(back, attention, expand, reduce, norm):
    cuts = 4
    _, row_block, col_block = attention[0].shape
    ff_block = expand[0].shape[1]
    att_spec = pl.BlockSpec((1, row_block, col_block), lambda j: (j, 0, 0))
    expand_spec = pl.BlockSpec((row_block // cuts, ff_block), lambda j: (j, 0))
    reduce_spec = pl.BlockSpec((ff_block // cuts, row_block), lambda j: (j, 0))
    norm_spec = pl.BlockSpec(norm[0].shape, lambda j: (0, 0))
    shapes = [*attention, *expand, *reduce, *norm]
    specs = [att_spec] * 3 + [expand_spec] * 3 + [reduce_spec] * 3 + [norm_spec] * 3
    carried = [back.resampled, back.media_grad.reshape(-1, D), back.latent_grad]
    carried_specs = [pl.BlockSpec((v.shape[0] // cuts, D), lambda j: (j, 0)) for v in carried]
    out_shape = [jax.ShapeDtypeStruct(v.shape, v.dtype) for v in shapes]
    out_shape += [jax.ShapeDtypeStruct((1, 1), F32)]
    out_shape += [jax.ShapeDtypeStruct(v.shape, v.dtype) for v in carried]
    made = pl.pallas_call(
        functools.partial(update_kernel, cuts),
        grid=(cuts,),
        out_shape=out_shape,
        in_specs=[
            att_spec,
            pl.BlockSpec((1, row_block // cuts, ff_block), lambda j: (0, j, 0)),
            pl.BlockSpec((1, row_block, ff_block // cuts), lambda j: (1, 0, j)),
            pl.BlockSpec((8, D), lambda j: (0, 0)),
            pl.BlockSpec((8, 128), lambda j: (0, 0)),
            *specs,
            *carried_specs,
        ],
        out_specs=[*specs, pl.BlockSpec((1, 1), lambda j: (0, 0)), *carried_specs],
        compiler_params=pltpu.CompilerParams(vmem_limit_bytes=63 * MIB),
        name="update_kernel",
    )(back.att_share, back.ff_share, back.ff_share, back.totals, back.squares, *shapes, *carried)
    return made[:12], made[12], made[13:]


def on_device(
    media_tokens,
    latents,
    cotangent,
    counts,
    attention_weights,
    attention_first,
    attention_second,
    expand_weight,
    expand_first,
    expand_second,
    reduce_weight,
    reduce_first,
    reduce_second,
    norm_params,
    norm_first,
    norm_second,
):
    _, row_block, col_block = attention_weights.shape
    got = forward(
        attention_weights,
        expand_weight,
        reduce_weight,
        media_tokens,
        latents,
        cotangent,
        counts,
        norm_params,
    )
    back = backward(
        got, media_tokens, latents, counts, norm_params, row_block, col_block, expand_weight.shape[1]
    )
    made, size, (resampled, media_grad, latent_grad) = update(
        back,
        (attention_weights, attention_first, attention_second),
        (expand_weight, expand_first, expand_second),
        (reduce_weight, reduce_first, reduce_second),
        (norm_params, norm_first, norm_second),
    )
    return (
        resampled.reshape(latents.shape),
        media_grad.reshape(media_tokens.shape),
        latent_grad.reshape(latents.shape),
        size.reshape(()),
        *made,
    )


def solution(mesh):
    in_specs = (
        P(("dp", "head"), None, None),
        P(("dp", "head"), None, None),
        P(("dp", "head"), None, None),
        P("dp"),
        P(None, "dp", "head"),
        P(None, "dp", "head"),
        P(None, "dp", "head"),
        P("dp", "head"),
        P("dp", "head"),
        P("dp", "head"),
        P("head", "dp"),
        P("head", "dp"),
        P("head", "dp"),
        P(),
        P(),
        P(),
    )
    out_specs = (
        P(("dp", "head"), None, None),
        P(("dp", "head"), None, None),
        P(("dp", "head"), None, None),
        P(),
        P(None, "dp", "head"),
        P(None, "dp", "head"),
        P(None, "dp", "head"),
        P("dp", "head"),
        P("dp", "head"),
        P("dp", "head"),
        P("head", "dp"),
        P("head", "dp"),
        P("head", "dp"),
        P(),
        P(),
        P(),
    )
    return jax.shard_map(
        on_device, mesh=mesh, in_specs=in_specs, out_specs=out_specs, check_vma=False
    )
```
